32 devices in a mesh: ctx: 4 (over z), exp: 8 (over y, x, core).
Axes of the slice: x: 2, y: 2, z: 4, core: 2. Of those that a mesh axis runs over, the one named last changes fastest.
Arguments:
- tokens: bfloat16 [2, 8, 1024, 2048], P(None, 'exp', 'ctx'), may hold values from -6 to 6
- routes: int32 [2, 8, 1024, 8], P(None, 'exp', 'ctx'), may hold values from 0 to 31, all different within a row; in each aligned block of 256 rows (0 to 255, 256 to 511, ..., all dimensions but the last counted through in order) at most 80 rows name the same one
- route_weights: float32 [2, 8, 1024, 8], P(None, 'exp', 'ctx'), may hold values from 0.05 to 0.25
- bounds: int32 [2, 8], P(None, 'exp'), may hold values from 1 to 1023, as said below
- norm_attn: float32 [2048], replicated, may hold values from 0.5 to 1.5
- norm_ffn: float32 [2048], replicated, may hold values from 0.5 to 1.5
- q_gain: float32 [128], replicated, may hold values from 0.25 to 1.75
- k_gain: float32 [128], replicated, may hold values from 0.25 to 1.75
- w_q: bfloat16 [2048, 4096], P('exp'), may hold values from -0.125 to 0.125
- w_k: bfloat16 [2048, 512], P('exp'), may hold values from -0.125 to 0.125
- w_v: bfloat16 [2048, 512], P('exp'), may hold values from -0.125 to 0.125
- w_o: bfloat16 [4096, 2048], P('exp'), may hold values from -0.75 to 0.75
- w_gate: bfloat16 [32, 2048, 768], P(('ctx', 'exp')), may hold values from -0.125 to 0.125
- w_up: bfloat16 [32, 2048, 768], P(('ctx', 'exp')), may hold values from -0.125 to 0.125
- w_down: bfloat16 [32, 768, 2048], P(('ctx', 'exp')), may hold values from -0.875 to 0.875
- cotangent: bfloat16 [2, 8, 1024, 2048], P(None, 'exp', 'ctx'), may hold values from -6 to 6
Outputs:
- output: bfloat16 [2, 8, 1024, 2048], P(None, 'exp', 'ctx')
- tokens_grad: float32 [2, 8, 1024, 2048], P(None, 'exp', 'ctx')
- route_weights_grad: float32 [2, 8, 1024, 8], P(None, 'exp', 'ctx')
- w_q_grad: float32 [2048, 4096], P(('ctx', 'exp'))
- w_k_grad: float32 [2048, 512], P(('ctx', 'exp'))
- w_v_grad: float32 [2048, 512], P(('ctx', 'exp'))
- w_o_grad: float32 [4096, 2048], P(('ctx', 'exp'))
- gains_grad: float32 [4352], P(('ctx', 'exp'))
- w_gate_grad: float32 [32, 2048, 768], P(('ctx', 'exp'))
- w_up_grad: float32 [32, 2048, 768], P(('ctx', 'exp'))
- w_down_grad: float32 [32, 768, 2048], P(('ctx', 'exp'))
The draws below stay inside these ranges and needn't reach their ends.
Inputs may be any that keep to these rules, and one draw needn't show every extreme that they name: `routes`: each position names 8 different experts; within one micro-batch the 256 positions of one device name no expert more than 80 times, a bound that some block reaches in some of these blocks. `bounds`: each packed row holds two documents, the second beginning at the bound; one of the two is longer than 768 positions.
All inputs are finite; a program needn't handle non-finite values.
Results may differ from the reference program's by a relative error of at most 0.018.
Values may be sent and summed in bfloat16 or wider, within the bound.
A program may use at most 640 MiB of HBM per device.

```python
import math
import jax
import jax.numpy as jnp
import numpy as np
from jax import lax

D = 2048
HEADS = 32
KV_HEADS = 4
HEAD_DIM = 128
FF_E = 768
TOP = 8
MICRO = 2
EXPERTS = 32
SEQ_LEN = 1024
CTX_TOK = 256
BATCH = 8
CAP = 80
N_CTX = 4


def draw_bounds(key, part):
    key = jax.random.fold_in(key, 7)
    side_key, offset_key = jax.random.split(key)
    side = jax.random.randint(side_key, (MICRO, BATCH), 0, 2)
    offset = jax.random.randint(offset_key, (MICRO, BATCH), 1, CTX_TOK)
    return jnp.where(side == 0, offset, SEQ_LEN - offset).astype(jnp.int32)


def block_scale(key, extent, shards, least, high):
    def one(position, parts):
        heights = jax.random.uniform(jax.random.fold_in(jax.random.fold_in(key, 6), position), (parts,), jnp.float32, least / len(shards), high / len(shards))
        return jnp.repeat(jnp.exp(heights), extent[position] // parts).reshape((-1,) + (1,) * (len(extent) - position - 1))

    factor_of = one(*shards[0])
    for cut in shards[1:]:
        factor_of = factor_of * one(*cut)
    return factor_of


def routed_block(key, own, number, rows, number_of, top, limit, slope):
    sequence = jax.random.permutation(key, number_of)
    heavy_load, usual = load_shares(number_of, rows * top, limit, slope, True), load_shares(number_of, rows * top, limit, slope, False)
    places = jnp.arange(number_of)

    def named(sizes, turn):
        used = int((sizes > 0).sum())
        fixed = max(1, used // 4)
        shifted = fixed + (places - fixed + turn * (used - fixed)) % max(1, number_of - fixed)
        return jnp.zeros((number_of,), jnp.int32).at[sequence[jnp.where(places < fixed, places, shifted)]].set(jnp.asarray(sizes, jnp.int32))

    sizes = jnp.where(number % 4 == 0, named(heavy_load, number // 4), named(usual, number - number // 4 - 1))
    mixed = jax.random.permutation(jax.random.fold_in(own, 3), number_of)
    source_of, sink = mixed[0:number_of // 2 * 2:2], mixed[1:number_of // 2 * 2:2]
    room = jnp.minimum(sizes[source_of] - 1, limit - sizes[sink]) // 2
    room = jnp.where((source_of == sequence[0]) | (sink == sequence[0]) | (sizes[sink] == 0), 0, jnp.maximum(room, 0))
    shifted = jax.random.randint(jax.random.fold_in(own, 4), (number_of // 2,), 0, 1 << 20) % (room + 1)
    sizes = sizes.at[source_of].add(-shifted).at[sink].add(shifted)
    members = jnp.searchsorted(jnp.cumsum(sizes), jnp.arange(rows * top), side="right").astype(jnp.int32)
    listing = members.reshape(top, rows).T
    listing = listing[jax.random.permutation(jax.random.fold_in(own, 1), rows)]
    turn = jax.random.randint(jax.random.fold_in(own, 2), (rows, 1), 0, top)
    return jnp.take_along_axis(listing, (jnp.arange(top)[None, :] + turn) % top, axis=1)


def load_shares(number_of, total, most, skew, full):
    loads = [(1 << 20) // math.isqrt(grade ** skew) + 1 for grade in range(1, number_of + 1)]
    largest = most if full else min(most, max(-(-total // number_of), total * loads[0] // sum(loads)))
    least = 1 if total - largest >= number_of - 1 else 0
    holding, surplus = [largest] + [least] * (number_of - 1), total - largest - least * (number_of - 1)
    while surplus > 0:
        candidates = [i for i in range(1, number_of) if holding[i] < largest] or [i for i in range(1, number_of) if holding[i] < most]
        mass, remaining = sum([loads[i] for i in candidates]), surplus
        for i in candidates:
            addition = min(most - holding[i], max(1, remaining * loads[i] // mass), surplus)
            holding[i] = holding[i] + addition
            surplus = surplus - addition
    return np.array(holding)


def normal_values(stream_key, shape, scale, reach, pieces=(), held_as=jnp.bfloat16):
    factor_of = block_scale(stream_key, shape, pieces, -0.22, 0.18) if pieces else 1.0
    entries = jax.random.normal(stream_key, shape, jnp.float32) * scale * factor_of
    return jnp.minimum(jnp.maximum(entries, -reach), reach).astype(held_as)


def setup_inputs(seed: int = 0) -> dict:
    splits = jax.random.split(jax.random.key(seed), 17)
    tokens = normal_values(splits[0], (MICRO, BATCH, SEQ_LEN, D), 1.0, 6.0, ((1, 8), (2, 4)))
    routes_keys = jax.random.split(jax.random.fold_in(splits[1], 1), MICRO * BATCH * SEQ_LEN // CTX_TOK)
    routes_turns = jax.random.permutation(jax.random.fold_in(splits[1], 3), MICRO * BATCH * SEQ_LEN // CTX_TOK)
    routes = jax.vmap(lambda own, number: routed_block(jax.random.fold_in(splits[1], 2), own, number, CTX_TOK, EXPERTS, TOP, CAP, 1))(routes_keys, routes_turns).reshape((MICRO, BATCH, SEQ_LEN, TOP))
    route_weights = jnp.clip(jnp.exp(math.log(0.25) - 1.609438 * jax.random.uniform(splits[2], (MICRO, BATCH, SEQ_LEN, TOP), jnp.float32) ** block_scale(splits[2], (MICRO, BATCH, SEQ_LEN, TOP), ((1, 8), (2, 4)), -0.2, 0.2)), 0.05, 0.25)
    bounds = draw_bounds(jax.random.fold_in(splits[16], 71), 0)
    norm_attn = jnp.clip(1.0 + 0.1 * jax.random.normal(splits[4], (D,), jnp.float32), 0.5, 1.5)
    norm_ffn = jnp.clip(1.0 + 0.1 * jax.random.normal(splits[5], (D,), jnp.float32), 0.5, 1.5)
    q_gain = jnp.clip(1.0 + 0.15 * jax.random.normal(splits[6], (HEAD_DIM,), jnp.float32), 0.25, 1.75)
    k_gain = jnp.clip(1.0 + 0.15 * jax.random.normal(splits[7], (HEAD_DIM,), jnp.float32), 0.25, 1.75)
    w_q = normal_values(splits[8], (D, HEADS * HEAD_DIM), D ** -0.5, 0.125, ((0, 8),))
    w_k = normal_values(splits[9], (D, KV_HEADS * HEAD_DIM), D ** -0.5, 0.125, ((0, 8),))
    w_v = normal_values(splits[10], (D, KV_HEADS * HEAD_DIM), D ** -0.5, 0.125, ((0, 8),))
    w_o = normal_values(splits[11], (HEADS * HEAD_DIM, D), (HEADS * HEAD_DIM // 64) ** -0.5, 0.75, ((0, 8),))
    w_gate = normal_values(splits[12], (EXPERTS, D, FF_E), D ** -0.5, 0.125, ((0, 32),))
    w_up = normal_values(splits[13], (EXPERTS, D, FF_E), D ** -0.5, 0.125, ((0, 32),))
    w_down = normal_values(splits[14], (EXPERTS, FF_E, D), (FF_E // 16) ** -0.5, 0.875, ((0, 32),))
    cotangent = normal_values(splits[15], (MICRO, BATCH, SEQ_LEN, D), 1.0, 6.0, ((1, 8), (2, 4)))
    return dict(tokens=tokens, routes=routes, route_weights=route_weights, bounds=bounds, norm_attn=norm_attn, norm_ffn=norm_ffn, q_gain=q_gain, k_gain=k_gain, w_q=w_q, w_k=w_k, w_v=w_v, w_o=w_o, w_gate=w_gate, w_up=w_up, w_down=w_down, cotangent=cotangent)


EPSILON = 1e-06
ROPE_BASE = 1000000.0
MASKED = -1e+30
HIGHEST = lax.Precision.HIGHEST

@jax.custom_vjp
def low(v):
    return lax.optimization_barrier(v.astype(jnp.bfloat16)).astype(jnp.float32)

@jax.custom_vjp
def low_back(v):
    return v

def low_keep(v):
    return (low(v), None)

def low_pass(kept, grad):
    return (grad,)

def back_keep(v):
    return (v, None)

def back_low(kept, grad):
    return (low(grad),)
low.defvjp(low_keep, low_pass)
low_back.defvjp(back_keep, back_low)

def norm_rows(value, gain):
    return value * lax.rsqrt(lax.optimization_barrier(jnp.mean(value * value, -1, keepdims=True)) + EPSILON) * gain

def rope_tables(length):
    half = HEAD_DIM // 2
    inverse = ROPE_BASE ** (-jnp.arange(half, dtype=jnp.float32) * 2.0 / HEAD_DIM)
    angle = jnp.arange(length, dtype=jnp.float32)[:, None] * inverse[None, :]
    return (jnp.cos(angle), jnp.sin(angle))

def rotate(value, cosine, sine):
    half = value.shape[-1] // 2
    first = value[..., :half]
    second = value[..., half:]
    cos_b = cosine[:, None, :]
    sin_b = sine[:, None, :]
    return jnp.concatenate([first * cos_b - second * sin_b, second * cos_b + first * sin_b], -1)

def slot_layout(route_block):
    flat = route_block.reshape(-1).astype(jnp.int32)
    one_hot = (flat[:, None] == jnp.arange(EXPERTS, dtype=jnp.int32)[None, :]).astype(jnp.int32)
    before = jnp.cumsum(one_hot, 0) - one_hot
    place = lax.optimization_barrier(jnp.sum(before * one_hot, 1))
    slot = (flat * CAP + place).astype(jnp.int32)
    owner_token = (jnp.arange(flat.shape[0], dtype=jnp.int32) // TOP).astype(jnp.int32)
    table = jnp.zeros((EXPERTS * CAP,), jnp.int32).at[slot].set(owner_token)
    filled = jnp.zeros((EXPERTS * CAP,), jnp.float32).at[slot].set(1.0)
    return (slot, table, filled)

def expert_block(feed_in, route_block, route_row, w_gate, w_up, w_down):
    slot, table, filled = slot_layout(route_block)
    sent = low_back(jnp.take(feed_in, table, axis=0) * filled[:, None]).reshape(EXPERTS, CAP, D)
    gate = low_back(jnp.einsum('ecd,edf->ecf', sent, w_gate, precision=HIGHEST))
    upper = low_back(jnp.einsum('ecd,edf->ecf', sent, w_up, precision=HIGHEST))
    active = low(gate * jax.nn.sigmoid(gate) * upper)
    produced = low(low_back(jnp.einsum('ecf,efd->ecd', active, w_down, precision=HIGHEST)))
    picked = jnp.take(produced.reshape(EXPERTS * CAP, D), slot, axis=0).reshape(CTX_TOK, TOP, D)
    return lax.optimization_barrier(jnp.sum(picked * route_row[:, :, None], 1))

def layer_row(row, route_block, route_row, bound, params):
    norm_attn, norm_ffn, q_gain, k_gain, w_q, w_k, w_v, w_o, w_gate, w_up, w_down = params
    length = row.shape[0]
    group = HEADS // KV_HEADS
    cosine, sine = rope_tables(length)
    hidden = low(norm_rows(row, norm_attn))
    queries = low_back(jnp.dot(hidden, w_q, precision=HIGHEST)).reshape(length, HEADS, HEAD_DIM)
    keys = low_back(jnp.dot(hidden, w_k, precision=HIGHEST)).reshape(length, KV_HEADS, HEAD_DIM)
    values = low(low_back(jnp.dot(hidden, w_v, precision=HIGHEST))).reshape(length, KV_HEADS, HEAD_DIM)
    queries = low(low_back(rotate(norm_rows(queries, q_gain), cosine, sine))).reshape(length, KV_HEADS, group, HEAD_DIM)
    keys = low(low_back(rotate(norm_rows(keys, k_gain), cosine, sine)))
    place = jnp.arange(length)
    document = place >= bound
    allowed = (place[None, :] <= place[:, None]) & (document[None, :] == document[:, None])
    scores = low_back(jnp.einsum('qgjd,kgd->gjqk', queries, keys, precision=HIGHEST) * HEAD_DIM ** (-0.5))
    scores = jnp.where(allowed[None, None], scores, MASKED)
    top_score = lax.optimization_barrier(jnp.max(scores, -1, keepdims=True))
    raised = jnp.exp(scores - top_score)
    chances = low(raised / lax.optimization_barrier(jnp.sum(raised, -1, keepdims=True)))
    attended = jnp.einsum('gjqk,kgd->qgjd', chances, values, precision=HIGHEST).reshape(length, HEADS * HEAD_DIM)
    attended = low(low_back(attended))
    middle = row + low_back(jnp.dot(attended, w_o, precision=HIGHEST))
    feed_in = low(norm_rows(middle, norm_ffn))
    mixed = lax.map(lambda item: expert_block(item[0], item[1], item[2], w_gate, w_up, w_down), (feed_in.reshape(N_CTX, CTX_TOK, D), route_block.reshape(N_CTX, CTX_TOK, TOP), route_row.reshape(N_CTX, CTX_TOK, TOP)))
    return middle + mixed.reshape(length, D)

def reference(tokens, routes, route_weights, bounds, norm_attn, norm_ffn, q_gain, k_gain, w_q, w_k, w_v, w_o, w_gate, w_up, w_down, cotangent):
    params = tuple((weight.astype(jnp.float32) for weight in (norm_attn, norm_ffn, q_gain, k_gain, w_q, w_k, w_v, w_o, w_gate, w_up, w_down)))
    rows = MICRO * BATCH

    def forward(inputs, weights_in, params):

        def step(carry, item):
            return (carry, jax.checkpoint(layer_row)(item[0], item[1], item[2], item[3], params))
        _, result = lax.scan(step, jnp.zeros((), jnp.float32), (inputs.reshape(rows, SEQ_LEN, D), routes.reshape(rows, SEQ_LEN, TOP), weights_in.reshape(rows, SEQ_LEN, TOP), bounds.reshape(rows)))
        return result.reshape(MICRO, BATCH, SEQ_LEN, D)
    result, pullback = jax.vjp(forward, tokens.astype(jnp.float32), route_weights.astype(jnp.float32), params)
    token_grad, weight_grad, param_grads = pullback(cotangent.astype(jnp.float32))
    gains = jnp.concatenate([param_grads[0], param_grads[1], param_grads[2], param_grads[3]])
    return (result.astype(jnp.bfloat16), token_grad, weight_grad, param_grads[4], param_grads[5], param_grads[6], param_grads[7], gains, param_grads[8], param_grads[9], param_grads[10])
```

```python
import jax
import jax.numpy as jnp
from jax import lax
from jax.sharding import PartitionSpec as P

EPSILON = 1e-06
ROPE_BASE = 1000000.0
MASKED = -1e30


def norm_rows(value, gain):
    scale = lax.rsqrt(jnp.mean(value * value, -1, keepdims=True) + EPSILON)
    return (value * scale * gain, scale)


def norm_back(value, scale, gain, grad):
    inner = grad * gain
    first = scale * inner - value * (scale * scale * scale) * jnp.mean(
        inner * value, -1, keepdims=True
    )
    return (first, grad * value * scale)


def rope_tables(positions, width):
    half = width // 2
    inverse = ROPE_BASE ** (-jnp.arange(half, dtype=jnp.float32) * 2.0 / width)
    angle = positions.astype(jnp.float32)[:, None] * inverse[None, :]
    return (jnp.cos(angle), jnp.sin(angle))


def rotate(value, cosine, sine):
    half = value.shape[-1] // 2
    first = value[..., :half]
    second = value[..., half:]
    cos_b = cosine[:, None, :]
    sin_b = sine[:, None, :]
    return jnp.concatenate([first * cos_b - second * sin_b, second * cos_b + first * sin_b], -1)


def rotate_back(value, cosine, sine):
    half = value.shape[-1] // 2
    first = value[..., :half]
    second = value[..., half:]
    cos_b = cosine[:, None, :]
    sin_b = sine[:, None, :]
    return jnp.concatenate([first * cos_b + second * sin_b, second * cos_b - first * sin_b], -1)

def plane_tables(routes_all, weights_all, first, planned, capacity):
    hit = routes_all[..., None] == first + jnp.arange(planned, dtype=jnp.int32)
    named = jnp.any(hit, -2)
    weight = jnp.sum(jnp.where(hit, weights_all[..., None], 0.0), -2)
    rows = routes_all.shape[-2]
    earlier = (
        jnp.arange(rows, dtype=jnp.int32)[:, None] > jnp.arange(rows, dtype=jnp.int32)[None, :]
    ).astype(jnp.bfloat16)
    rank = jnp.einsum(
        "tu,cuj->ctj", earlier, named.astype(jnp.bfloat16), preferred_element_type=jnp.float32
    ).astype(jnp.int32)
    place = jnp.where(named, rank, -1)
    chosen = place.transpose(2, 0, 1)[:, :, None, :] == jnp.arange(capacity, dtype=jnp.int32)[
        None, None, :, None
    ]
    return chosen, weight.transpose(2, 0, 1)


def per_device(
    tokens,
    routes,
    route_weights,
    bounds,
    norm_attn,
    norm_ffn,
    q_gain,
    k_gain,
    w_q,
    w_k,
    w_v,
    w_o,
    w_gate,
    w_up,
    w_down,
    cotangent,
):
    micro = tokens.shape[0]
    local = tokens.shape[2]
    width = tokens.shape[3]
    head_dim = q_gain.shape[0]
    heads = w_q.shape[1] // head_dim
    kv_heads = w_k.shape[1] // head_dim
    group = heads // kv_heads
    top = routes.shape[3]
    ring = lax.axis_size("ctx")
    plane = lax.axis_size("exp")
    assert w_gate.shape[0] == 1
    experts = ring * plane
    capacity = max(2, local * top * 5 // (4 * experts))
    seq_len = local * ring
    scale = head_dim ** (-0.5)
    query_width = heads * head_dim
    pair_width = kv_heads * head_dim
    here = lax.axis_index("ctx")
    positions = here * local + jnp.arange(local, dtype=jnp.int32)
    every_place = jnp.arange(seq_len, dtype=jnp.int32)
    cosine, sine = rope_tables(positions, head_dim)
    in_weight = lax.all_gather(jnp.concatenate([w_q, w_k, w_v], 1), "exp", axis=0, tiled=True)
    out_weight = lax.all_gather(w_o, "exp", axis=0, tiled=True)
    query_weight = in_weight[:, :query_width]
    key_weight = in_weight[:, query_width : query_width + pair_width]
    value_weight = in_weight[:, query_width + pair_width :]
    gate_weight, up_weight, down_weight = w_gate[0], w_up[0], w_down[0]

    def dot(a, b):
        return jnp.dot(a, b, preferred_element_type=jnp.float32)

    def dot_t(a, b):
        return jnp.einsum("te,de->td", a, b, preferred_element_type=jnp.float32)

    def t_dot(a, b):
        return jnp.einsum("td,te->de", a, b, preferred_element_type=jnp.float32)

    meta = jnp.concatenate([routes[:, 0].astype(jnp.float32), route_weights[:, 0]], -1)
    meta = lax.all_gather(meta, "ctx", axis=0)
    chosen, slot_weights = [], []
    for step in range(micro):
        taken, weight = plane_tables(
            meta[:, step, :, :top].astype(jnp.int32),
            meta[:, step, :, top:],
            here * plane,
            plane,
            capacity,
        )
        chosen.append(taken)
        slot_weights.append(weight)

    def to_experts(rows, step, weighted):
        blocks = lax.all_gather(rows, "ctx", axis=0)
        picked = jnp.einsum(
            "jcst,ctd->jcsd",
            chosen[step].astype(jnp.bfloat16),
            blocks,
            preferred_element_type=jnp.float32,
        )
        if weighted:
            factor = jnp.sum(jnp.where(chosen[step], slot_weights[step][:, :, None, :], 0.0), -1)
            picked = picked * factor[..., None]
        picked = picked.astype(jnp.bfloat16).reshape(plane, ring * capacity, width)
        return lax.all_to_all(picked, "exp", split_axis=0, concat_axis=0, tiled=True).reshape(
            plane * ring * capacity, width
        )

    def from_experts(rows, step, weighted):
        back = lax.all_to_all(
            rows.reshape(plane, ring * capacity, width),
            "exp",
            split_axis=0,
            concat_axis=0,
            tiled=True,
        ).reshape(plane, ring, capacity, width)
        if weighted:
            factor = jnp.where(chosen[step], slot_weights[step][:, :, None, :], 0.0)
        else:
            factor = chosen[step]
        part = jnp.einsum(
            "jcst,jcsd->ctd",
            factor.astype(jnp.bfloat16),
            back,
            preferred_element_type=jnp.float32,
        )
        return lax.psum_scatter(
            part.astype(jnp.bfloat16).reshape(seq_len, width),
            "ctx",
            scatter_dimension=0,
            tiled=True,
        ).astype(jnp.float32)

    kept = []
    for step in range(micro):
        row = tokens[step, 0].astype(jnp.float32)
        hidden, first_scale = norm_rows(row, norm_attn)
        hidden = hidden.astype(jnp.bfloat16)
        query_raw = dot(hidden, query_weight).reshape(local, heads, head_dim)
        key_raw = dot(hidden, key_weight).reshape(local, kv_heads, head_dim)
        value_low = dot(hidden, value_weight).astype(jnp.bfloat16)
        query_normed, query_scale = norm_rows(query_raw, q_gain)
        key_normed, key_scale = norm_rows(key_raw, k_gain)
        queries = (
            rotate(query_normed, cosine, sine)
            .astype(jnp.bfloat16)
            .reshape(local, kv_heads, group, head_dim)
        )
        keys = rotate(key_normed, cosine, sine).astype(jnp.bfloat16).reshape(local, pair_width)
        both = lax.all_gather(jnp.concatenate([keys, value_low], 1), "ctx", axis=0, tiled=True)
        all_keys = both[:, :pair_width].reshape(seq_len, kv_heads, head_dim)
        all_values = both[:, pair_width:].reshape(seq_len, kv_heads, head_dim)
        bound = bounds[step, 0]
        allowed = (every_place[None, :] <= positions[:, None]) & (
            (every_place[None, :] >= bound) == (positions[:, None] >= bound)
        )
        raw = (
            jnp.einsum("qgjd,kgd->gjqk", queries, all_keys, preferred_element_type=jnp.float32)
            * scale
        )
        scores = jnp.where(allowed[None, None], raw, MASKED)
        top_score = jnp.max(scores, -1, keepdims=True)
        total = jnp.sum(jnp.exp(scores - top_score), -1, keepdims=True)
        log_total = top_score + jnp.log(total)
        chances = jnp.exp(scores - log_total).astype(jnp.bfloat16)
        attended = jnp.einsum(
            "gjqk,kgd->qgjd", chances, all_values, preferred_element_type=jnp.float32
        )
        attended = attended.reshape(local, query_width).astype(jnp.bfloat16)
        middle = row + dot(attended, out_weight)
        feed_in, second_scale = norm_rows(middle, norm_ffn)
        feed_in = feed_in.astype(jnp.bfloat16)
        kept.append(
            (
                row,
                hidden,
                first_scale,
                query_raw,
                query_scale,
                key_raw,
                key_scale,
                queries,
                all_keys,
                all_values,
                allowed,
                log_total,
                attended,
                middle,
                feed_in,
                second_scale,
            )
        )

    outputs, token_grads, value_rows = [], [], []
    received_list, active_list, incoming_list, gate_grad_list, up_grad_list = [], [], [], [], []
    hidden_list, raw_grad_list, attended_list, branch_list, gain_list = [], [], [], [], []
    for step in range(micro):
        (
            row,
            hidden,
            first_scale,
            query_raw,
            query_scale,
            key_raw,
            key_scale,
            queries,
            all_keys,
            all_values,
            allowed,
            log_total,
            attended,
            middle,
            feed_in,
            second_scale,
        ) = kept[step]
        grad = cotangent[step, 0].astype(jnp.float32)
        incoming = to_experts(cotangent[step, 0], step, True)
        received = to_experts(feed_in, step, False)
        gate = dot(received, gate_weight)
        upper = dot(received, up_weight)
        sigma = jax.nn.sigmoid(gate)
        swish = gate * sigma
        active = (swish * upper).astype(jnp.bfloat16)
        produced = dot(active, down_weight).astype(jnp.bfloat16)
        active_grad = dot_t(incoming, down_weight)
        gate_grad = (active_grad * upper * sigma * (1.0 + gate * (1.0 - sigma))).astype(
            jnp.bfloat16
        )
        upper_grad = (active_grad * swish).astype(jnp.bfloat16)
        pair_value = jnp.sum(active_grad * active.astype(jnp.float32), -1)
        back = (dot_t(gate_grad, gate_weight) + dot_t(upper_grad, up_weight)).astype(jnp.bfloat16)
        received_list.append(received)
        active_list.append(active)
        incoming_list.append(incoming)
        gate_grad_list.append(gate_grad)
        up_grad_list.append(upper_grad)
        feed_grad = from_experts(back, step, False)
        outputs.append((middle + from_experts(produced, step, True)).astype(jnp.bfloat16))
        pair_value = lax.all_to_all(
            pair_value.reshape(plane, ring * capacity),
            "exp",
            split_axis=0,
            concat_axis=0,
            tiled=True,
        ).reshape(plane, ring, capacity)
        value_rows.append(
            jnp.sum(jnp.where(chosen[step], pair_value[..., None], 0.0), 2).transpose(1, 2, 0)
        )

        middle_norm_grad, second_gain = norm_back(middle, second_scale, norm_ffn, feed_grad)
        middle_grad = grad + middle_norm_grad
        branch_grad = middle_grad.astype(jnp.bfloat16)
        attended_grad = dot_t(branch_grad, out_weight)
        attended_grad = attended_grad.astype(jnp.bfloat16).reshape(local, kv_heads, group, head_dim)
        raw = (
            jnp.einsum("qgjd,kgd->gjqk", queries, all_keys, preferred_element_type=jnp.float32)
            * scale
        )
        chances_again = jnp.exp(jnp.where(allowed[None, None], raw, MASKED) - log_total)
        chance_grad = jnp.einsum(
            "qgjd,kgd->gjqk", attended_grad, all_values, preferred_element_type=jnp.float32
        )
        score_grad = chances_again * (
            chance_grad - jnp.sum(chances_again * chance_grad, -1, keepdims=True)
        )
        score_grad = score_grad.astype(jnp.bfloat16)
        query_grad = (
            jnp.einsum("gjqk,kgd->qgjd", score_grad, all_keys, preferred_element_type=jnp.float32)
            * scale
        ).astype(jnp.bfloat16)
        key_part = (
            jnp.einsum("gjqk,qgjd->kgd", score_grad, queries, preferred_element_type=jnp.float32)
            * scale
        )
        value_part = jnp.einsum(
            "gjqk,qgjd->kgd",
            chances_again.astype(jnp.bfloat16),
            attended_grad,
            preferred_element_type=jnp.float32,
        )
        key_value_grad = lax.psum_scatter(
            jnp.concatenate(
                [key_part.reshape(seq_len, pair_width), value_part.reshape(seq_len, pair_width)], -1
            ).astype(jnp.bfloat16),
            "ctx",
            scatter_dimension=0,
            tiled=True,
        )
        key_grad = key_value_grad[:, :pair_width].astype(jnp.float32)
        value_grad = key_value_grad[:, pair_width:]
        query_grad = query_grad.astype(jnp.float32).reshape(local, heads, head_dim)
        query_turned = rotate_back(query_grad, cosine, sine)
        key_turned = rotate_back(key_grad.reshape(local, kv_heads, head_dim), cosine, sine)
        query_raw_grad, query_gain_part = norm_back(query_raw, query_scale, q_gain, query_turned)
        key_raw_grad, key_gain_part = norm_back(key_raw, key_scale, k_gain, key_turned)
        raw_grad = jnp.concatenate(
            [
                query_raw_grad.astype(jnp.bfloat16).reshape(local, query_width),
                key_raw_grad.astype(jnp.bfloat16).reshape(local, pair_width),
                value_grad,
            ],
            1,
        )
        hidden_grad = dot_t(raw_grad, in_weight)
        first_grad, first_gain = norm_back(row, first_scale, norm_attn, hidden_grad)
        token_grads.append(middle_grad + first_grad)
        gain_list.append(
            jnp.concatenate(
                [
                    jnp.sum(first_gain, 0),
                    jnp.sum(second_gain, 0),
                    jnp.sum(query_gain_part, (0, 1)),
                    jnp.sum(key_gain_part, (0, 1)),
                ]
            )
        )
        hidden_list.append(hidden)
        raw_grad_list.append(raw_grad)
        attended_list.append(attended)
        branch_list.append(branch_grad)

    def sum_over_devices(left, right):
        left = jnp.concatenate(left, 0)
        share = left.shape[1] // experts
        left = left.reshape(-1, ring, plane, share).transpose(0, 2, 1, 3)
        term = t_dot(left.reshape(-1, experts * share), jnp.concatenate(right, 0))
        term = lax.psum_scatter(
            term.astype(jnp.bfloat16), "exp", scatter_dimension=0, tiled=True
        )
        return lax.psum_scatter(term, "ctx", scatter_dimension=0, tiled=True).astype(jnp.float32)

    out_total = sum_over_devices(attended_list, branch_list)
    in_total = sum_over_devices(hidden_list, raw_grad_list)
    gain_total = lax.psum_scatter(
        sum(gain_list), ("ctx", "exp"), scatter_dimension=0, tiled=True
    )
    received_all = jnp.concatenate(received_list, 0)
    gate_term = t_dot(received_all, jnp.concatenate(gate_grad_list, 0))[None]
    up_term = t_dot(received_all, jnp.concatenate(up_grad_list, 0))[None]
    down_term = t_dot(jnp.concatenate(active_list, 0), jnp.concatenate(incoming_list, 0))[None]

    values = lax.all_to_all(
        jnp.stack(value_rows, 1), "ctx", split_axis=0, concat_axis=0, tiled=True
    )
    values = values.transpose(1, 2, 0, 3).reshape(micro, local, experts)
    match = routes[:, 0, :, :, None] == jnp.arange(experts, dtype=jnp.int32)
    route_grads = jnp.sum(jnp.where(match, values[:, :, None, :], 0.0), -1) / route_weights[:, 0]
    return (
        jnp.stack(outputs)[:, None],
        jnp.stack(token_grads)[:, None],
        route_grads[:, None],
        in_total[:, :query_width],
        in_total[:, query_width : query_width + pair_width],
        in_total[:, query_width + pair_width :],
        out_total,
        gain_total,
        gate_term,
        up_term,
        down_term,
    )


def solution(mesh):
    in_specs = (
        P(None, "exp", "ctx", None),
        P(None, "exp", "ctx", None),
        P(None, "exp", "ctx", None),
        P(None, "exp"),
        P(),
        P(),
        P(),
        P(),
        P("exp", None),
        P("exp", None),
        P("exp", None),
        P("exp", None),
        P(("ctx", "exp"), None, None),
        P(("ctx", "exp"), None, None),
        P(("ctx", "exp"), None, None),
        P(None, "exp", "ctx", None),
    )
    out_specs = (
        P(None, "exp", "ctx", None),
        P(None, "exp", "ctx", None),
        P(None, "exp", "ctx", None),
        P(("ctx", "exp"), None),
        P(("ctx", "exp"), None),
        P(("ctx", "exp"), None),
        P(("ctx", "exp"), None),
        P(("ctx", "exp")),
        P(("ctx", "exp"), None, None),
        P(("ctx", "exp"), None, None),
        P(("ctx", "exp"), None, None),
    )
    return jax.shard_map(
        per_device, mesh=mesh, in_specs=in_specs, out_specs=out_specs, check_vma=False
    )
```

```python
import functools
import math

import jax
import jax.numpy as jnp
from jax import lax
from jax.experimental import pallas as pl
from jax.experimental.pallas import tpu as pltpu
from jax.sharding import PartitionSpec as P

EPSILON = 1e-06
ROPE_BASE = 1000000.0
MASKED = -1e30
VMEM_BYTES = 56 * 2**20


def norm_rows(value, gain):
    scale = lax.rsqrt(jnp.mean(value * value, -1, keepdims=True) + EPSILON)
    return (value * scale * gain, scale)


def norm_back(value, scale, gain, grad):
    inner = grad * gain
    first = scale * inner - value * (scale * scale * scale) * jnp.mean(
        inner * value, -1, keepdims=True
    )
    return (first, grad * value * scale)


def rope_tables(positions, width):
    half = width // 2
    inverse = ROPE_BASE ** (-jnp.arange(half, dtype=jnp.float32) * 2.0 / width)
    angle = positions.astype(jnp.float32)[:, None] * inverse[None, :]
    cosine, sine = jnp.cos(angle), jnp.sin(angle)
    return (jnp.concatenate([cosine, cosine], -1), jnp.concatenate([-sine, sine], -1))


def swap_halves(value):
    half = value.shape[-1] // 2
    return jnp.concatenate([value[..., half:], value[..., :half]], -1)


def nothing_kernel(*refs):
    pass


def after(value, *others):
    return pl.pallas_call(
        nothing_kernel,
        in_specs=[pl.BlockSpec(memory_space=pl.ANY)] * (1 + len(others)),
        out_specs=pl.BlockSpec(memory_space=pl.ANY),
        out_shape=jax.ShapeDtypeStruct(value.shape, value.dtype),
        input_output_aliases={0: 0},
    )(value, *others)


def gather_kernel(count, arrays, *refs):
    own, full = refs[:arrays], refs[arrays : 2 * arrays]
    send_sem, recv_sem, own_sem = refs[2 * arrays :]
    me = lax.axis_index("ctx")
    barrier = pltpu.get_barrier_semaphore()
    for other in (lax.rem(me + 1, count), lax.rem(me + count - 1, count)):
        pl.semaphore_signal(
            barrier, inc=1, device_id={"ctx": other}, device_id_type=pl.DeviceIdType.MESH
        )
    pl.semaphore_wait(barrier, 2)

    def block(i, at):
        rows = own[i].shape[0]
        return full[i].at[pl.ds(at * rows, rows)]

    def passing(way, step, i, at):
        return pltpu.make_async_remote_copy(
            src_ref=own[i] if step == 0 else block(i, at),
            dst_ref=block(i, at),
            send_sem=send_sem.at[way, step, i],
            recv_sem=recv_sem.at[way, step, i],
            device_id={"ctx": me + (1 if way == 0 else -1)},
            device_id_type=pl.DeviceIdType.MESH,
        )

    def sends(way, step):
        if way == 0:
            return (me >= step) & (me < count - 1)
        return (me + step < count) & (me > 0)

    def receives(way, step):
        return me >= step + 1 if way == 0 else me + step + 1 < count

    kept = [pltpu.make_async_copy(own[i], block(i, me), own_sem.at[i]) for i in range(arrays)]
    for step in range(count - 1):
        for i in range(arrays):
            for way in (0, 1):
                sign = 1 if way == 0 else -1

                @pl.when(sends(way, step))
                def _():
                    passing(way, step, i, me - sign * step).start()

        if step == 0:
            for copy in kept:
                copy.start()
        for i in range(arrays):
            for way in (0, 1):
                sign = 1 if way == 0 else -1

                @pl.when(receives(way, step))
                def _():
                    passing(way, step, i, me - sign * (step + 1)).wait_recv()

    for copy in kept:
        copy.wait()
    for step in range(count - 1):
        for i in range(arrays):
            for way in (0, 1):
                sign = 1 if way == 0 else -1

                @pl.when(sends(way, step))
                def _():
                    passing(way, step, i, me - sign * step).wait_send()


def line_gather(*blocks):
    count = lax.axis_size("ctx")
    arrays = len(blocks)
    return pl.pallas_call(
        functools.partial(gather_kernel, count, arrays),
        in_specs=[pl.BlockSpec(memory_space=pl.ANY)] * arrays,
        out_specs=[pl.BlockSpec(memory_space=pl.ANY)] * arrays,
        out_shape=[
            jax.ShapeDtypeStruct((count * block.shape[0],) + block.shape[1:], block.dtype)
            for block in blocks
        ],
        scratch_shapes=[
            pltpu.SemaphoreType.DMA((2, count - 1, arrays)),
            pltpu.SemaphoreType.DMA((2, count - 1, arrays)),
            pltpu.SemaphoreType.DMA((arrays,)),
        ],
        compiler_params=pltpu.CompilerParams(collective_id=0, has_side_effects=True),
        cost_estimate=pl.CostEstimate(flops=0, bytes_accessed=200 * 2**20, transcendentals=0),
    )(*blocks)


def expert_kernel(
    rows_ref,
    grad_ref,
    gate_ref,
    up_ref,
    down_ref,
    active_ref,
    gate_grad_ref,
    up_grad_ref,
    out_ref,
    back_ref,
    value_ref,
):
    gate = along(rows_ref[...], gate_ref[...])
    upper = along(rows_ref[...], up_ref[...])
    active_grad = across(grad_ref[...], down_ref[...])
    sigma = jax.nn.sigmoid(gate)
    swish = gate * sigma
    active = (swish * upper).astype(jnp.bfloat16)
    active_ref[...] = active
    out_ref[...] = along(active, down_ref[...]).astype(jnp.bfloat16)
    gate_grad = (active_grad * upper * sigma * (1.0 + gate * (1.0 - sigma))).astype(jnp.bfloat16)
    up_grad = (active_grad * swish).astype(jnp.bfloat16)
    gate_grad_ref[...] = gate_grad
    up_grad_ref[...] = up_grad
    value_ref[...] = jnp.sum(active_grad * active.astype(jnp.float32), -1, keepdims=True)
    back_ref[...] = (across(gate_grad, gate_ref[...]) + across(up_grad, up_ref[...])).astype(
        jnp.bfloat16
    )


def run_expert(rows, grad, gate, up, down):
    total, width = rows.shape
    units = gate.shape[1]
    block = 256 if total % 256 == 0 else total
    wide = pl.BlockSpec((block, width), lambda i: (i, 0))
    narrow = pl.BlockSpec((block, units), lambda i: (i, 0))

    def whole(shape):
        return pl.BlockSpec(shape, lambda i: (0, 0), pipeline_mode=pl.Buffered(1))

    low = jax.ShapeDtypeStruct((total, units), jnp.bfloat16)
    full = jax.ShapeDtypeStruct((total, width), jnp.bfloat16)
    return pl.pallas_call(
        expert_kernel,
        grid=(total // block,),
        in_specs=[wide, wide, whole(gate.shape), whole(up.shape), whole(down.shape)],
        out_specs=(narrow, narrow, narrow, wide, wide, pl.BlockSpec((block, 1), lambda i: (i, 0))),
        out_shape=(low, low, low, full, full, jax.ShapeDtypeStruct((total, 1), jnp.float32)),
        compiler_params=pltpu.CompilerParams(vmem_limit_bytes=VMEM_BYTES),
        cost_estimate=pl.CostEstimate(
            flops=14 * total * width * units,
            bytes_accessed=8 * total * width,
            transcendentals=total * units,
        ),
    )(rows, grad, gate, up, down)


def plane_tables(routes_all, weights_all, first, planned):
    hit = routes_all[..., None] == first + jnp.arange(planned, dtype=jnp.int32)
    named = jnp.any(hit, -2)
    weight = jnp.sum(jnp.where(hit, weights_all[..., None], 0.0), -2)
    rows = routes_all.shape[-2]
    earlier = (
        jnp.arange(rows, dtype=jnp.int32)[:, None] > jnp.arange(rows, dtype=jnp.int32)[None, :]
    ).astype(jnp.bfloat16)
    rank = jnp.einsum(
        "tu,cuj->ctj", earlier, named.astype(jnp.bfloat16), preferred_element_type=jnp.float32
    ).astype(jnp.int32)
    place = jnp.where(named, rank, -1)
    return place.transpose(0, 2, 1), weight.transpose(0, 2, 1)


def pick_kernel(planes, place_ref, weight_ref, rows_ref, out_ref, weighted):
    capacity = out_ref.shape[2]
    local = rows_ref.shape[0]
    slots = lax.broadcasted_iota(jnp.int32, (capacity, local), 0)
    for j in range(planes):
        chosen = place_ref[0, 0, j : j + 1, :] == slots
        picked = jnp.dot(
            jnp.where(chosen, 1.0, 0.0).astype(jnp.bfloat16),
            rows_ref[...],
            preferred_element_type=jnp.float32,
        )
        if weighted:
            picked = picked * jnp.sum(
                jnp.where(chosen, weight_ref[0, 0, j : j + 1, :], 0.0), -1, keepdims=True
            )
        out_ref[j, 0] = picked.astype(jnp.bfloat16)


def pick_rows(place, weight, blocks, capacity, weighted):
    count, planned, local = place.shape
    width = blocks.shape[1]
    part = 4 if planned % 4 == 0 else planned
    shape = (count, planned // part, part, local)
    return pl.pallas_call(
        functools.partial(pick_kernel, part, weighted=weighted),
        grid=(count, planned // part),
        in_specs=[
            pl.BlockSpec((1, 1, part, local), lambda c, g: (c, g, 0, 0)),
            pl.BlockSpec((1, 1, part, local), lambda c, g: (c, g, 0, 0)),
            pl.BlockSpec((local, width), lambda c, g: (c, 0)),
        ],
        out_specs=pl.BlockSpec((part, 1, capacity, width), lambda c, g: (g, c, 0, 0)),
        out_shape=jax.ShapeDtypeStruct((planned, count, capacity, width), jnp.bfloat16),
        compiler_params=pltpu.CompilerParams(vmem_limit_bytes=VMEM_BYTES),
        cost_estimate=pl.CostEstimate(
            flops=2 * count * planned * capacity * local * width,
            bytes_accessed=2 * count * planned * capacity * width,
            transcendentals=0,
        ),
    )(place.reshape(shape), weight.reshape(shape), blocks)


def fill_mask(place_ref, mask_ref):
    base, bound = place_ref[0], place_ref[1]
    keys, rows = mask_ref.shape
    key_at = lax.broadcasted_iota(jnp.int32, (keys, rows), 0)
    row_at = lax.broadcasted_iota(jnp.int32, (keys, rows), 1) + base
    least = jnp.where(row_at >= bound, bound, 0)
    mask_ref[...] = jnp.where((key_at <= row_at) & (key_at >= least), 0.0, MASKED)


def head_queries(raw, gain, cosine, sine):
    scale = lax.rsqrt(jnp.mean(raw * raw, -1, keepdims=True) + EPSILON)
    value = raw * scale * gain
    turned = value * cosine + pltpu.roll(value, value.shape[-1] // 2, 1) * sine
    return turned.astype(jnp.bfloat16), scale


def across(a, b):
    return lax.dot_general(a, b, (((1,), (1,)), ((), ())), preferred_element_type=jnp.float32)


def along(a, b):
    return jnp.dot(a, b, preferred_element_type=jnp.float32)


def keyed(both_ref, width, which):
    count, rows = both_ref.shape[:2]
    return both_ref[:, :, which * width : (which + 1) * width].reshape(count * rows, width)


def attend_kernel(
    per, factor, place_ref, raw_ref, both_ref, gain_ref, cos_ref, sin_ref, out_ref, mask_ref, turned_ref
):
    width = gain_ref.shape[1]
    group_step, step = pl.program_id(0), pl.program_id(1)

    @pl.when((group_step == 0) & (step == 0))
    def _():
        fill_mask(place_ref, mask_ref)

    @pl.when(step == 0)
    def _():
        turned_ref[...] = keyed(both_ref, width, 1).T

    for head in range(per):
        columns = slice(head * width, (head + 1) * width)
        queries, _ = head_queries(raw_ref[:, columns], gain_ref[...], cos_ref[...], sin_ref[...])
        chances = jnp.exp2(across(keyed(both_ref, width, 0), queries) * factor + mask_ref[...])
        total = jnp.sum(chances, 0, keepdims=True)
        result = along(turned_ref[...], chances.astype(jnp.bfloat16)) * (1.0 / total)
        out_ref[:, columns] = result.T.astype(jnp.bfloat16)


def attend_back_kernel(
    per,
    steps,
    factor,
    scale,
    place_ref,
    raw_ref,
    grad_ref,
    both_ref,
    gain_ref,
    cos_ref,
    sin_ref,
    raw_grad_ref,
    both_grad_ref,
    gain_grad_ref,
    mask_ref,
    turned_ref,
    sums_ref,
):
    width = gain_ref.shape[1]
    group_step, step = pl.program_id(0), pl.program_id(1)

    @pl.when((group_step == 0) & (step == 0))
    def _():
        fill_mask(place_ref, mask_ref)
        gain_grad_ref[...] = jnp.zeros_like(gain_grad_ref)

    @pl.when(step == 0)
    def _():
        turned_ref[...] = keyed(both_ref, width, 0).T
        sums_ref[...] = jnp.zeros_like(sums_ref)

    for head in range(per):
        columns = slice(head * width, (head + 1) * width)
        raw = raw_ref[:, columns]
        queries, norm = head_queries(raw, gain_ref[...], cos_ref[...], sin_ref[...])
        grad = grad_ref[:, columns]
        chances = jnp.exp2(across(keyed(both_ref, width, 0), queries) * factor + mask_ref[...])
        chances = chances * (1.0 / jnp.sum(chances, 0, keepdims=True))
        chance_grad = across(keyed(both_ref, width, 1), grad)
        mean = jnp.sum(chances * chance_grad, 0, keepdims=True)
        score_grad = (chances * (chance_grad - mean)).astype(jnp.bfloat16)
        sums_ref[:, :width] += along(score_grad, queries)
        sums_ref[:, width:] += along(chances.astype(jnp.bfloat16), grad)
        query_grad = (along(turned_ref[...], score_grad) * scale).astype(jnp.bfloat16)
        query_grad = query_grad.astype(jnp.float32).T
        back = query_grad * cos_ref[...] - pltpu.roll(query_grad, width // 2, 1) * sin_ref[...]
        inner = back * gain_ref[...]
        first = norm * inner - raw * (norm * norm * norm) * jnp.mean(inner * raw, -1, keepdims=True)
        raw_grad_ref[:, columns] = first.astype(jnp.bfloat16)
        gain_grad_ref[0:1, :] += jnp.sum(back * raw * norm, 0, keepdims=True)

    @pl.when(step == steps - 1)
    def _():
        both_grad_ref[:, :width] = (sums_ref[:, :width] * scale).astype(jnp.bfloat16)
        both_grad_ref[:, width:] = sums_ref[:, width:].astype(jnp.bfloat16)


def attention_specs(raw, both, width, rows, step, per):
    kv_heads = both.shape[2] // (2 * width)
    heads = raw.shape[1] // width - 2 * kv_heads
    steps = heads // kv_heads // per
    count = both.shape[0]
    keys = count * rows
    wide = pl.BlockSpec((rows, per * width), lambda g, j: (0, g * steps + j))
    specs = dict(
        place=pl.BlockSpec(memory_space=pltpu.SMEM),
        raw=pl.BlockSpec((rows, per * width), lambda g, j: (step, g * steps + j)),
        heads=wide,
        both=pl.BlockSpec((count, rows, 2 * width), lambda g, j: (0, step, g)),
        both_grad=pl.BlockSpec((keys, 2 * width), lambda g, j: (0, g)),
        gain=pl.BlockSpec((1, width), lambda g, j: (0, 0)),
        table=pl.BlockSpec((rows, width), lambda g, j: (0, 0)),
    )
    params = pltpu.CompilerParams(vmem_limit_bytes=VMEM_BYTES)
    work = 2 * heads * rows * keys * width
    return kv_heads, heads, steps, keys, specs, params, work


def attend(raw, both, gain, cosine, sine, place, step, per=2):
    rows, width = cosine.shape
    kv_heads, heads, steps, keys, specs, params, work = attention_specs(
        raw, both, width, rows, step, per
    )
    return pl.pallas_call(
        functools.partial(attend_kernel, per, width ** (-0.5) * math.log2(math.e)),
        grid=(kv_heads, steps),
        in_specs=[specs[k] for k in ("place", "raw", "both", "gain", "table", "table")],
        out_specs=specs["heads"],
        out_shape=jax.ShapeDtypeStruct((rows, heads * width), jnp.bfloat16),
        scratch_shapes=[
            pltpu.VMEM((keys, rows), jnp.float32),
            pltpu.VMEM((width, keys), jnp.bfloat16),
        ],
        compiler_params=params,
        cost_estimate=pl.CostEstimate(
            flops=4 * work, bytes_accessed=4 * rows * heads * width, transcendentals=work // width
        ),
    )(place, raw, both, gain, cosine, sine)


def attend_back(raw, grad, both, gain, cosine, sine, place, step, per=2):
    rows, width = cosine.shape
    kv_heads, heads, steps, keys, specs, params, work = attention_specs(
        raw, both, width, rows, step, per
    )
    return pl.pallas_call(
        functools.partial(
            attend_back_kernel, per, steps, width ** (-0.5) * math.log2(math.e), width ** (-0.5)
        ),
        grid=(kv_heads, steps),
        in_specs=[specs[k] for k in ("place", "raw", "heads", "both", "gain", "table", "table")],
        out_specs=(
            specs["heads"],
            specs["both_grad"],
            pl.BlockSpec((8, width), lambda g, j: (0, 0)),
        ),
        out_shape=(
            jax.ShapeDtypeStruct((rows, heads * width), jnp.bfloat16),
            jax.ShapeDtypeStruct((keys, both.shape[2]), jnp.bfloat16),
            jax.ShapeDtypeStruct((8, width), jnp.float32),
        ),
        scratch_shapes=[
            pltpu.VMEM((keys, rows), jnp.float32),
            pltpu.VMEM((width, keys), jnp.bfloat16),
            pltpu.VMEM((keys, 2 * width), jnp.float32),
        ],
        compiler_params=params,
        cost_estimate=pl.CostEstimate(
            flops=10 * work, bytes_accessed=8 * rows * heads * width, transcendentals=work // width
        ),
    )(place, raw, grad, both, gain, cosine, sine)


def per_device(
    tokens,
    routes,
    route_weights,
    bounds,
    norm_attn,
    norm_ffn,
    q_gain,
    k_gain,
    w_q,
    w_k,
    w_v,
    w_o,
    w_gate,
    w_up,
    w_down,
    cotangent,
):
    micro = tokens.shape[0]
    local = tokens.shape[2]
    width = tokens.shape[3]
    head_dim = q_gain.shape[0]
    kv_heads = w_k.shape[1] // head_dim
    top = routes.shape[3]
    ring = lax.axis_size("ctx")
    plane = lax.axis_size("exp")
    assert w_gate.shape[0] == 1
    experts = ring * plane
    capacity = max(2, local * top * 5 // (4 * experts))
    seq_len = local * ring
    query_width = w_q.shape[1]
    pair_width = kv_heads * head_dim
    here = lax.axis_index("ctx")
    base = here * local
    cosine, sine = rope_tables(base + jnp.arange(local, dtype=jnp.int32), head_dim)
    gate_weight, up_weight, down_weight = w_gate[0], w_up[0], w_down[0]

    def dot(a, b):
        return jnp.dot(a, b, preferred_element_type=jnp.float32)

    def dot_t(a, b):
        return jnp.einsum("te,de->td", a, b, preferred_element_type=jnp.float32)

    def t_dot(a, b):
        return jnp.einsum("td,te->de", a, b, preferred_element_type=jnp.float32)

    def paired(keys, values):
        rows = keys.shape[0]
        return jnp.stack(
            [keys.reshape(rows, kv_heads, head_dim), values.reshape(rows, kv_heads, head_dim)], 2
        ).reshape(rows, 2 * pair_width)

    in_weight = lax.all_gather(
        jnp.concatenate([w_q, paired(w_k, w_v)], 1), "exp", axis=0, tiled=True
    )
    out_weight = lax.all_gather(w_o, "exp", axis=0, tiled=True)

    meta = jnp.concatenate([routes[:, 0].astype(jnp.float32), route_weights[:, 0]], -1)
    grads_low = [cotangent[step, 0] for step in range(micro)]
    *grad_blocks, meta = line_gather(*grads_low, meta.reshape(-1, 128))
    meta = meta.reshape(ring, micro, local, 2 * top)
    tables = [
        plane_tables(
            meta[:, step, :, :top].astype(jnp.int32), meta[:, step, :, top:], here * plane, plane
        )
        for step in range(micro)
    ]
    slots = jnp.arange(capacity, dtype=jnp.int32)
    chosen = [
        place.transpose(1, 0, 2)[:, :, None, :] == slots[None, None, :, None] for place, _ in tables
    ]

    def exchange(rows, *waits):
        if waits:
            rows = after(rows, *waits)
        rows = rows.reshape(plane, ring * capacity, width)
        return lax.all_to_all(rows, "exp", split_axis=0, concat_axis=0, tiled=True).reshape(
            plane * ring * capacity, width
        )

    def pick(blocks, step, weighted):
        return pick_rows(*tables[step], blocks, capacity, weighted)

    def from_experts(back, step, weighted):
        back = back.reshape(plane, ring, capacity, width)
        factor = chosen[step]
        if weighted:
            weight = tables[step][1].transpose(1, 0, 2)
            factor = jnp.where(factor, weight[:, :, None, :], 0.0)
        part = jnp.einsum(
            "jcst,jcsd->ctd",
            factor.astype(jnp.bfloat16),
            back,
            preferred_element_type=jnp.float32,
        )
        return lax.psum_scatter(
            part.astype(jnp.bfloat16).reshape(seq_len, width),
            "ctx",
            scatter_dimension=0,
            tiled=True,
        ).astype(jnp.float32)

    incoming = [exchange(pick(grad_blocks[0], 0, True))]
    for step in range(1, micro):
        incoming.append(exchange(pick(grad_blocks[step], step, True), incoming[-1]))

    rows = tokens[:, 0].astype(jnp.float32).reshape(micro * local, width)
    hidden, first_scale = norm_rows(rows, norm_attn)
    hidden = after(hidden.astype(jnp.bfloat16), grad_blocks[0])
    raw = dot(hidden, in_weight)
    pair_raw = raw[:, query_width:].reshape(micro * local, kv_heads, 2, head_dim)
    key_raw = pair_raw[:, :, 0]
    key_normed, key_scale = norm_rows(key_raw, k_gain)
    key_cos = jnp.tile(cosine, (micro, 1))[:, None, :]
    key_sin = jnp.tile(sine, (micro, 1))[:, None, :]
    keys = (key_normed * key_cos + swap_halves(key_normed) * key_sin).astype(jnp.bfloat16)
    pairs = jnp.stack([keys, pair_raw[:, :, 1].astype(jnp.bfloat16)], 2).reshape(
        micro * local, 2 * pair_width
    )
    both = lax.all_gather(pairs, "ctx", axis=0)
    gain_row = q_gain[None, :]
    places, attended, middles, feeds, scales = [], [], [], [], []
    for step in range(micro):
        part = slice(step * local, (step + 1) * local)
        places.append(jnp.stack([base, bounds[step, 0]]).astype(jnp.int32))
        attended.append(attend(raw, both, gain_row, cosine, sine, places[step], step))
        middles.append(rows[part] + dot(attended[step], out_weight))
        feed_in, second_scale = norm_rows(middles[step], norm_ffn)
        feeds.append(feed_in.astype(jnp.bfloat16))
        scales.append(second_scale)
    feed_blocks = [lax.all_gather(feed, "ctx", axis=0, tiled=True) for feed in feeds]

    received = []
    last = incoming[-1]
    for step in range(micro):
        received.append(exchange(pick(feed_blocks[step], step, False), last))
        last = received[-1]

    active, gate_grad, up_grad, produced, backs, pair_values = [], [], [], [], [], []
    for step in range(micro):
        parts = run_expert(received[step], incoming[step], gate_weight, up_weight, down_weight)
        for held, item in zip((active, gate_grad, up_grad, produced, backs, pair_values), parts):
            held.append(item)

    returned = []
    for step in range(micro):
        returned.append(exchange(backs[step], last))
        last = returned[-1]

    branches, raw_grads, middle_grads, gain_list, results = [], [], [], [], []
    for step in range(micro):
        results.append(exchange(produced[step], last, *raw_grads))
        last = results[-1]
        part = slice(step * local, (step + 1) * local)
        feed_grad = from_experts(returned[step], step, False)
        middle_norm_grad, second_gain = norm_back(middles[step], scales[step], norm_ffn, feed_grad)
        middle_grads.append(grads_low[step].astype(jnp.float32) + middle_norm_grad)
        branches.append(middle_grads[step].astype(jnp.bfloat16))
        attended_grad = dot_t(branches[step], out_weight).astype(jnp.bfloat16)
        raw_grad, pair_part, query_gain_part = attend_back(
            raw, attended_grad, both, gain_row, cosine, sine, places[step], step
        )
        raw_grads.append(raw_grad)
        gain_list.append([jnp.sum(second_gain, 0), query_gain_part[0], pair_part])
    pair_grads = []
    for step in range(micro):
        part = slice(step * local, (step + 1) * local)
        pair_grad = lax.psum_scatter(
            gain_list[step][2], "ctx", scatter_dimension=0, tiled=True
        ).reshape(local, kv_heads, 2, head_dim)
        key_grad = pair_grad[:, :, 0].astype(jnp.float32)
        key_turned = key_grad * cosine[:, None, :] - swap_halves(key_grad) * sine[:, None, :]
        key_raw_grad, key_gain_part = norm_back(key_raw[part], key_scale[part], k_gain, key_turned)
        pair_grad = jnp.stack([key_raw_grad.astype(jnp.bfloat16), pair_grad[:, :, 1]], 2)
        pair_grads.append(pair_grad.reshape(local, 2 * pair_width))
        gain_list[step][2] = jnp.sum(key_gain_part, (0, 1))
    results[-1] = after(results[-1], raw_grads[-1])

    def sum_over_devices(left, right):
        share = left.shape[1] // experts
        left = left.reshape(-1, ring, plane, share).transpose(0, 2, 1, 3)
        term = t_dot(left.reshape(-1, experts * share), right)
        term = lax.psum_scatter(term.astype(jnp.bfloat16), "exp", scatter_dimension=0, tiled=True)
        return lax.psum_scatter(term, "ctx", scatter_dimension=0, tiled=True).astype(jnp.float32)

    out_total = sum_over_devices(jnp.concatenate(attended, 0), jnp.concatenate(branches, 0))
    query_grad, pair_grad = jnp.concatenate(raw_grads, 0), jnp.concatenate(pair_grads, 0)
    query_total = sum_over_devices(hidden, query_grad)
    pair_total = sum_over_devices(hidden, pair_grad).reshape(-1, kv_heads, 2, head_dim)
    hidden_grad = dot_t(query_grad, in_weight[:, :query_width]) + dot_t(
        pair_grad, in_weight[:, query_width:]
    )
    first_grad, first_gain = norm_back(rows, first_scale, norm_attn, hidden_grad)
    tokens_grad = jnp.concatenate(middle_grads, 0) + first_grad
    gain_total = lax.psum_scatter(
        jnp.concatenate([jnp.sum(first_gain, 0)] + [sum(parts) for parts in zip(*gain_list)]),
        ("ctx", "exp"),
        scatter_dimension=0,
        tiled=True,
    )
    received_all = jnp.concatenate(received, 0)
    gate_term = t_dot(received_all, jnp.concatenate(gate_grad, 0))[None]
    up_term = t_dot(received_all, jnp.concatenate(up_grad, 0))[None]
    down_term = t_dot(jnp.concatenate(active, 0), jnp.concatenate(incoming, 0))[None]

    outputs = [
        (middles[step] + from_experts(results[step], step, True)).astype(jnp.bfloat16)
        for step in range(micro)
    ]

    pair_values = lax.all_to_all(
        jnp.stack([v.reshape(plane, ring, capacity) for v in pair_values], 1),
        "exp",
        split_axis=0,
        concat_axis=0,
        tiled=True,
    )
    values = jnp.stack(
        [
            jnp.sum(jnp.where(chosen[step], pair_values[:, step, :, :, None], 0.0), 2)
            for step in range(micro)
        ],
        1,
    )
    values = lax.all_to_all(
        values.transpose(2, 1, 3, 0), "ctx", split_axis=0, concat_axis=0, tiled=True
    )
    values = values.transpose(1, 2, 0, 3).reshape(micro, local, experts)
    match = routes[:, 0, :, :, None] == jnp.arange(experts, dtype=jnp.int32)
    route_grads = jnp.sum(jnp.where(match, values[:, :, None, :], 0.0), -1) / route_weights[:, 0]

    return (
        jnp.stack(outputs)[:, None],
        tokens_grad.reshape(micro, 1, local, width),
        route_grads[:, None],
        query_total,
        pair_total[:, :, 0].reshape(-1, pair_width),
        pair_total[:, :, 1].reshape(-1, pair_width),
        out_total,
        gain_total,
        gate_term,
        up_term,
        down_term,
    )


def solution(mesh):
    in_specs = (
        P(None, "exp", "ctx", None),
        P(None, "exp", "ctx", None),
        P(None, "exp", "ctx", None),
        P(None, "exp"),
        P(),
        P(),
        P(),
        P(),
        P("exp", None),
        P("exp", None),
        P("exp", None),
        P("exp", None),
        P(("ctx", "exp"), None, None),
        P(("ctx", "exp"), None, None),
        P(("ctx", "exp"), None, None),
        P(None, "exp", "ctx", None),
    )
    out_specs = (
        P(None, "exp", "ctx", None),
        P(None, "exp", "ctx", None),
        P(None, "exp", "ctx", None),
        P(("ctx", "exp"), None),
        P(("ctx", "exp"), None),
        P(("ctx", "exp"), None),
        P(("ctx", "exp"), None),
        P(("ctx", "exp")),
        P(("ctx", "exp"), None, None),
        P(("ctx", "exp"), None, None),
        P(("ctx", "exp"), None, None),
    )
    return jax.shard_map(
        per_device, mesh=mesh, in_specs=in_specs, out_specs=out_specs, check_vma=False
    )
```

```python
import functools
import math

import jax
import jax.numpy as jnp
from jax import lax
from jax.experimental import pallas as pl
from jax.experimental.pallas import tpu as pltpu
from jax.sharding import PartitionSpec as P

EPSILON = 1e-06
ROPE_BASE = 1000000.0
MASKED = -1e30
VMEM_BYTES = 56 * 2**20
SMALL = pl.CostEstimate(flops=2**20, bytes_accessed=2**20, transcendentals=0)


def norm_rows(value, gain):
    scale = lax.rsqrt(jnp.mean(value * value, -1, keepdims=True) + EPSILON)
    return (value * scale * gain, scale)


def norm_back(value, scale, gain, grad):
    inner = grad * gain
    first = scale * inner - value * (scale * scale * scale) * jnp.mean(
        inner * value, -1, keepdims=True
    )
    return (first, grad * value * scale)


def rope_tables(positions, width):
    half = width // 2
    inverse = ROPE_BASE ** (-jnp.arange(half, dtype=jnp.float32) * 2.0 / width)
    angle = positions.astype(jnp.float32)[:, None] * inverse[None, :]
    cosine, sine = jnp.cos(angle), jnp.sin(angle)
    return (jnp.concatenate([cosine, cosine], -1), jnp.concatenate([-sine, sine], -1))


def swap_halves(value):
    half = value.shape[-1] // 2
    return jnp.concatenate([value[..., half:], value[..., :half]], -1)


def nothing_kernel(*refs):
    pass


def after(value, *others):
    return pl.pallas_call(
        nothing_kernel,
        in_specs=[pl.BlockSpec(memory_space=pl.ANY)] * (1 + len(others)),
        out_specs=pl.BlockSpec(memory_space=pl.ANY),
        out_shape=jax.ShapeDtypeStruct(value.shape, value.dtype),
        input_output_aliases={0: 0},
    )(value, *others)


def gather_kernel(count, arrays, *refs):
    own, full = refs[:arrays], refs[arrays : 2 * arrays]
    send_sem, recv_sem, own_sem = refs[2 * arrays :]
    me = lax.axis_index("ctx")
    barrier = pltpu.get_barrier_semaphore()
    for other in (lax.rem(me + 1, count), lax.rem(me + count - 1, count)):
        pl.semaphore_signal(
            barrier, inc=1, device_id={"ctx": other}, device_id_type=pl.DeviceIdType.MESH
        )
    pl.semaphore_wait(barrier, 2)

    def block(i, at):
        rows = own[i].shape[0]
        return full[i].at[pl.ds(at * rows, rows)]

    def passing(way, step, i, at):
        return pltpu.make_async_remote_copy(
            src_ref=own[i] if step == 0 else block(i, at),
            dst_ref=block(i, at),
            send_sem=send_sem.at[way, step, i],
            recv_sem=recv_sem.at[way, step, i],
            device_id={"ctx": me + (1 if way == 0 else -1)},
            device_id_type=pl.DeviceIdType.MESH,
        )

    def sends(way, step):
        if way == 0:
            return (me >= step) & (me < count - 1)
        return (me + step < count) & (me > 0)

    def receives(way, step):
        return me >= step + 1 if way == 0 else me + step + 1 < count

    kept = [pltpu.make_async_copy(own[i], block(i, me), own_sem.at[i]) for i in range(arrays)]
    for step in range(count - 1):
        for i in range(arrays):
            for way in (0, 1):
                sign = 1 if way == 0 else -1

                @pl.when(sends(way, step))
                def _():
                    passing(way, step, i, me - sign * step).start()

        if step == 0:
            for copy in kept:
                copy.start()
        for i in range(arrays):
            for way in (0, 1):
                sign = 1 if way == 0 else -1

                @pl.when(receives(way, step))
                def _():
                    passing(way, step, i, me - sign * (step + 1)).wait_recv()

    for copy in kept:
        copy.wait()
    for step in range(count - 1):
        for i in range(arrays):
            for way in (0, 1):
                sign = 1 if way == 0 else -1

                @pl.when(sends(way, step))
                def _():
                    passing(way, step, i, me - sign * step).wait_send()


def line_gather(*blocks, number):
    count = lax.axis_size("ctx")
    arrays = len(blocks)
    return pl.pallas_call(
        functools.partial(gather_kernel, count, arrays),
        in_specs=[pl.BlockSpec(memory_space=pl.ANY)] * arrays,
        out_specs=[pl.BlockSpec(memory_space=pl.ANY)] * arrays,
        out_shape=[
            jax.ShapeDtypeStruct((count * block.shape[0],) + block.shape[1:], block.dtype)
            for block in blocks
        ],
        scratch_shapes=[
            pltpu.SemaphoreType.DMA((2, count - 1, arrays)),
            pltpu.SemaphoreType.DMA((2, count - 1, arrays)),
            pltpu.SemaphoreType.DMA((arrays,)),
        ],
        compiler_params=pltpu.CompilerParams(collective_id=number, has_side_effects=True),
        cost_estimate=pl.CostEstimate(flops=0, bytes_accessed=200 * 2**20, transcendentals=0),
    )(*blocks)


def expert_kernel(
    rows_ref,
    grad_ref,
    gate_ref,
    up_ref,
    down_ref,
    active_ref,
    gate_grad_ref,
    up_grad_ref,
    out_ref,
    back_ref,
    value_ref,
):
    gate = along(rows_ref[...], gate_ref[...])
    upper = along(rows_ref[...], up_ref[...])
    active_grad = across(grad_ref[...], down_ref[...])
    sigma = jax.nn.sigmoid(gate)
    swish = gate * sigma
    active = (swish * upper).astype(jnp.bfloat16)
    active_ref[...] = active
    out_ref[...] = along(active, down_ref[...]).astype(jnp.bfloat16)
    gate_grad = (active_grad * upper * sigma * (1.0 + gate * (1.0 - sigma))).astype(jnp.bfloat16)
    up_grad = (active_grad * swish).astype(jnp.bfloat16)
    gate_grad_ref[...] = gate_grad
    up_grad_ref[...] = up_grad
    value_ref[...] = jnp.sum(active_grad * active.astype(jnp.float32), -1, keepdims=True)
    back_ref[...] = (across(gate_grad, gate_ref[...]) + across(up_grad, up_ref[...])).astype(
        jnp.bfloat16
    )


def run_expert(rows, grad, gate, up, down, step):
    sources, block, width = rows.shape
    units = gate.shape[1]
    total = sources * block
    wide = pl.BlockSpec((block, width), lambda i: (i, 0))
    narrow = pl.BlockSpec((block, units), lambda i: (i, 0))

    def whole(shape):
        return pl.BlockSpec(shape, lambda i: (0, 0), pipeline_mode=pl.Buffered(1))

    low = jax.ShapeDtypeStruct((total, units), jnp.bfloat16)
    full = jax.ShapeDtypeStruct((total, width), jnp.bfloat16)
    return pl.pallas_call(
        expert_kernel,
        grid=(sources,),
        in_specs=[
            pl.BlockSpec((None, block, width), lambda i: (i, 0, 0)),
            pl.BlockSpec((None, None, block, width), lambda i: (i, step, 0, 0)),
            whole(gate.shape),
            whole(up.shape),
            whole(down.shape),
        ],
        out_specs=(narrow, narrow, narrow, wide, wide, pl.BlockSpec((block, 1), lambda i: (i, 0))),
        out_shape=(low, low, low, full, full, jax.ShapeDtypeStruct((total, 1), jnp.float32)),
        compiler_params=pltpu.CompilerParams(vmem_limit_bytes=VMEM_BYTES),
        cost_estimate=SMALL,
    )(rows, grad, gate, up, down)


def plane_tables(routes_all, weights_all, first, planned):
    hit = routes_all[..., None] == first + jnp.arange(planned, dtype=jnp.int32)
    named = jnp.any(hit, -2)
    weight = jnp.sum(jnp.where(hit, weights_all[..., None], 0.0), -2)
    rows = routes_all.shape[-2]
    earlier = (
        jnp.arange(rows, dtype=jnp.int32)[:, None] > jnp.arange(rows, dtype=jnp.int32)[None, :]
    ).astype(jnp.bfloat16)
    rank = jnp.einsum(
        "tu,cuj->ctj", earlier, named.astype(jnp.bfloat16), preferred_element_type=jnp.float32
    ).astype(jnp.int32)
    place = jnp.where(named, rank, -1)
    return place.transpose(0, 2, 1), weight.transpose(0, 2, 1)


def pick_kernel(planes, place_ref, weight_ref, rows_ref, out_ref, weighted):
    capacity = out_ref.shape[2]
    local = rows_ref.shape[0]
    slots = lax.broadcasted_iota(jnp.int32, (capacity, local), 0)
    for j in range(planes):
        chosen = place_ref[0, 0, j : j + 1, :] == slots
        picked = jnp.dot(
            jnp.where(chosen, 1.0, 0.0).astype(jnp.bfloat16),
            rows_ref[...],
            preferred_element_type=jnp.float32,
        )
        if weighted:
            picked = picked * jnp.sum(
                jnp.where(chosen, weight_ref[0, 0, j : j + 1, :], 0.0), -1, keepdims=True
            )
        out_ref[j, 0] = picked.astype(jnp.bfloat16)


def pick_rows(place, weight, blocks, capacity, weighted):
    count, planned, local = place.shape
    width = blocks.shape[1]
    part = 4 if planned % 4 == 0 else planned
    shape = (count, planned // part, part, local)
    return pl.pallas_call(
        functools.partial(pick_kernel, part, weighted=weighted),
        grid=(count, planned // part),
        in_specs=[
            pl.BlockSpec((1, 1, part, local), lambda c, g: (c, g, 0, 0)),
            pl.BlockSpec((1, 1, part, local), lambda c, g: (c, g, 0, 0)),
            pl.BlockSpec((local, width), lambda c, g: (c, 0)),
        ],
        out_specs=pl.BlockSpec((part, 1, capacity, width), lambda c, g: (g, c, 0, 0)),
        out_shape=jax.ShapeDtypeStruct((planned, count, capacity, width), jnp.bfloat16),
        compiler_params=pltpu.CompilerParams(vmem_limit_bytes=VMEM_BYTES),
        cost_estimate=SMALL,
    )(place.reshape(shape), weight.reshape(shape), blocks)


def weight_kernel(steps, micro, *refs):
    rows, (grads_ref,) = refs[:micro], refs[micro : micro + 1]
    actives, gates, ups = (refs[micro * i + 1 : micro * i + 1 + micro] for i in (1, 2, 3))
    gate_ref, up_ref, down_ref = refs[4 * micro + 1 :]
    step = pl.program_id(0)

    def add(which, fresh):
        x = rows[which][...]
        for out_ref, left, right in (
            (gate_ref, x, gates[which][...]),
            (up_ref, x, ups[which][...]),
            (down_ref, actives[which][...], grads_ref[...]),
        ):
            term = lax.dot_general(
                left, right, (((0,), (0,)), ((), ())), preferred_element_type=jnp.float32
            )
            if fresh:
                out_ref[0] = term
            else:
                out_ref[0] += term

    pl.when(step == 0)(lambda: add(0, True))
    pl.when((step > 0) & (step < steps))(lambda: add(0, False))
    for which in range(1, micro):
        pl.when((step >= which * steps) & (step < (which + 1) * steps))(
            functools.partial(add, which, False)
        )


def expert_weight_grads(rows, grads, actives, gates, ups):
    sources, micro, block, width = grads.shape
    units = gates[0].shape[1]

    def turn(i, which):
        return jnp.clip(i - which * sources, 0, sources - 1)

    def specs(size):
        return [
            pl.BlockSpec((block, size), functools.partial(lambda w, i: (turn(i, w), 0), which))
            for which in range(micro)
        ]

    def row_specs():
        return [
            pl.BlockSpec(
                (None, block, width), functools.partial(lambda w, i: (turn(i, w), 0, 0), which)
            )
            for which in range(micro)
        ]

    shapes = [(1, width, units), (1, width, units), (1, units, width)]
    return pl.pallas_call(
        functools.partial(weight_kernel, sources, micro),
        grid=(micro * sources,),
        in_specs=row_specs()
        + [
            pl.BlockSpec(
                (None, None, block, width),
                lambda i: (lax.rem(i, sources), lax.div(i, sources), 0, 0),
            )
        ]
        + specs(units) * 3,
        out_specs=[pl.BlockSpec(shape, lambda i: (0, 0, 0)) for shape in shapes],
        out_shape=[jax.ShapeDtypeStruct(shape, jnp.float32) for shape in shapes],
        compiler_params=pltpu.CompilerParams(vmem_limit_bytes=VMEM_BYTES),
        cost_estimate=SMALL,
    )(*rows, grads, *actives, *gates, *ups)


def fill_mask(place_ref, mask_ref):
    base, bound = place_ref[0], place_ref[1]
    keys, rows = mask_ref.shape
    key_at = lax.broadcasted_iota(jnp.int32, (keys, rows), 0)
    row_at = lax.broadcasted_iota(jnp.int32, (keys, rows), 1) + base
    least = jnp.where(row_at >= bound, bound, 0)
    mask_ref[...] = jnp.where((key_at <= row_at) & (key_at >= least), 0.0, MASKED)


def head_queries(raw, gain, cosine, sine):
    scale = lax.rsqrt(jnp.mean(raw * raw, -1, keepdims=True) + EPSILON)
    value = raw * scale * gain
    turned = value * cosine + pltpu.roll(value, value.shape[-1] // 2, 1) * sine
    return turned.astype(jnp.bfloat16), scale


def across(a, b):
    return lax.dot_general(a, b, (((1,), (1,)), ((), ())), preferred_element_type=jnp.float32)


def along(a, b):
    return jnp.dot(a, b, preferred_element_type=jnp.float32)


def keyed(both_ref, width, which):
    count, rows = both_ref.shape[:2]
    return both_ref[:, :, which * width : (which + 1) * width].reshape(count * rows, width)


def attend_kernel(
    per, factor, place_ref, raw_ref, both_ref, gain_ref, cos_ref, sin_ref, out_ref, mask_ref, turned_ref
):
    width = gain_ref.shape[1]
    group_step, step = pl.program_id(0), pl.program_id(1)

    @pl.when((group_step == 0) & (step == 0))
    def _():
        fill_mask(place_ref, mask_ref)

    @pl.when(step == 0)
    def _():
        turned_ref[...] = keyed(both_ref, width, 1).T

    for head in range(per):
        columns = slice(head * width, (head + 1) * width)
        queries, _ = head_queries(raw_ref[:, columns], gain_ref[...], cos_ref[...], sin_ref[...])
        chances = jnp.exp2(across(keyed(both_ref, width, 0), queries) * factor + mask_ref[...])
        total = jnp.sum(chances, 0, keepdims=True)
        result = along(turned_ref[...], chances.astype(jnp.bfloat16)) * (1.0 / total)
        out_ref[:, columns] = result.T.astype(jnp.bfloat16)


class PlaneExchange:
    def __init__(self, count, rows_ref, out_ref, send_sem, recv_sem, own_sem):
        self.count, self.rows_ref, self.out_ref = count, rows_ref, out_ref
        self.send_sem, self.recv_sem, self.own_sem = send_sem, recv_sem, own_sem
        self.me = lax.axis_index("exp")

    @staticmethod
    def scratch(count):
        return [
            pltpu.SemaphoreType.DMA((count,)),
            pltpu.SemaphoreType.DMA((count,)),
            pltpu.SemaphoreType.DMA,
        ]

    def passing(self, k, part):
        return pltpu.make_async_remote_copy(
            src_ref=self.rows_ref.at[lax.rem(self.me + k, self.count)],
            dst_ref=self.out_ref.at[part],
            send_sem=self.send_sem.at[k],
            recv_sem=self.recv_sem.at[k],
            device_id={"exp": lax.rem(self.me + k, self.count)},
            device_id_type=pl.DeviceIdType.MESH,
        )

    def kept(self):
        return pltpu.make_async_copy(
            self.rows_ref.at[self.me], self.out_ref.at[self.me], self.own_sem
        )

    def begin(self):
        for k in range(1, self.count):
            self.passing(k, self.me).start()
        self.kept().start()

    def finish(self):
        self.kept().wait()
        for k in range(1, self.count):
            self.passing(k, lax.rem(self.me + self.count - k, self.count)).wait_recv()
        for k in range(1, self.count):
            self.passing(k, self.me).wait_send()


def greet(**counts):
    barrier = pltpu.get_barrier_semaphore()
    for axis, count in counts.items():
        me = lax.axis_index(axis)
        for k in range(1, count):
            pl.semaphore_signal(
                barrier,
                inc=1,
                device_id={axis: lax.rem(me + k, count)},
                device_id_type=pl.DeviceIdType.MESH,
            )
    pl.semaphore_wait(barrier, sum(counts.values()) - len(counts))


class RowExchange:
    def __init__(self, ring, held_ref, out_ref, send_sem, recv_sem, own_sem):
        self.ring, self.held_ref, self.out_ref = ring, held_ref, out_ref
        self.send_sem, self.recv_sem, self.own_sem = send_sem, recv_sem, own_sem
        self.me = lax.axis_index("ctx")
        self.rows = out_ref.shape[2]

    @staticmethod
    def scratch(ring, groups):
        return [
            pltpu.SemaphoreType.DMA((groups, ring)),
            pltpu.SemaphoreType.DMA((groups, ring)),
            pltpu.SemaphoreType.DMA((groups,)),
        ]

    def held(self, group, at):
        return self.held_ref.at[group, pl.ds(at * self.rows, self.rows)]

    def passing(self, group, k, part):
        to = lax.rem(self.me + k, self.ring)
        return pltpu.make_async_remote_copy(
            src_ref=self.held(group, to),
            dst_ref=self.out_ref.at[part, group],
            send_sem=self.send_sem.at[group, k],
            recv_sem=self.recv_sem.at[group, k],
            device_id={"ctx": to},
            device_id_type=pl.DeviceIdType.MESH,
        )

    def kept(self, group):
        return pltpu.make_async_copy(
            self.held(group, self.me), self.out_ref.at[self.me, group], self.own_sem.at[group]
        )

    def begin(self, group):
        for k in range(1, self.ring):
            self.passing(group, k, self.me).start()
        self.kept(group).start()

    def finish(self):
        for group in range(self.out_ref.shape[1]):
            self.kept(group).wait()
            for k in range(1, self.ring):
                self.passing(group, k, lax.rem(self.me + self.ring - k, self.ring)).wait_recv()
            for k in range(1, self.ring):
                self.passing(group, k, self.me).wait_send()


def attend_back_kernel(
    per,
    steps,
    factor,
    scale,
    count,
    ring,
    place_ref,
    raw_ref,
    grad_ref,
    both_ref,
    gain_ref,
    cos_ref,
    sin_ref,
    rows_ref,
    raw_grad_ref,
    landed_ref,
    gain_grad_ref,
    moved_ref,
    mask_ref,
    turned_ref,
    sums_ref,
    held_ref,
    *sems,
):
    width = gain_ref.shape[1]
    group_step, step = pl.program_id(0), pl.program_id(1)
    moving = PlaneExchange(count, rows_ref, moved_ref, *sems[:3])
    landing = RowExchange(ring, held_ref, landed_ref, *sems[3:])

    @pl.when((group_step == 0) & (step == 0))
    def _():
        greet(exp=count, ctx=ring)
        moving.begin()

    @pl.when((group_step == 0) & (step == 0))
    def _():
        fill_mask(place_ref, mask_ref)
        gain_grad_ref[...] = jnp.zeros_like(gain_grad_ref)

    @pl.when(step == 0)
    def _():
        turned_ref[...] = keyed(both_ref, width, 0).T
        sums_ref[...] = jnp.zeros_like(sums_ref)

    for head in range(per):
        columns = slice(head * width, (head + 1) * width)
        raw = raw_ref[:, columns]
        queries, norm = head_queries(raw, gain_ref[...], cos_ref[...], sin_ref[...])
        grad = grad_ref[:, columns]
        chances = jnp.exp2(across(keyed(both_ref, width, 0), queries) * factor + mask_ref[...])
        chances = chances * (1.0 / jnp.sum(chances, 0, keepdims=True))
        chance_grad = across(keyed(both_ref, width, 1), grad)
        mean = jnp.sum(chances * chance_grad, 0, keepdims=True)
        score_grad = (chances * (chance_grad - mean)).astype(jnp.bfloat16)
        sums_ref[:, :width] += along(score_grad, queries)
        sums_ref[:, width:] += along(chances.astype(jnp.bfloat16), grad)
        query_grad = (along(turned_ref[...], score_grad) * scale).astype(jnp.bfloat16)
        query_grad = query_grad.astype(jnp.float32).T
        back = query_grad * cos_ref[...] - pltpu.roll(query_grad, width // 2, 1) * sin_ref[...]
        inner = back * gain_ref[...]
        first = norm * inner - raw * (norm * norm * norm) * jnp.mean(inner * raw, -1, keepdims=True)
        raw_grad_ref[:, columns] = first.astype(jnp.bfloat16)
        gain_grad_ref[0:1, :] += jnp.sum(back * raw * norm, 0, keepdims=True)

    @pl.when(step == steps - 1)
    def _():
        held_ref[group_step, :, :width] = (sums_ref[:, :width] * scale).astype(jnp.bfloat16)
        held_ref[group_step, :, width:] = sums_ref[:, width:].astype(jnp.bfloat16)
        landing.begin(group_step)

    @pl.when((group_step == pl.num_programs(0) - 1) & (step == steps - 1))
    def _():
        landing.finish()
        moving.finish()


def attention_specs(raw, both, width, rows, step, per):
    kv_heads = both.shape[2] // (2 * width)
    heads = raw.shape[1] // width - 2 * kv_heads
    steps = heads // kv_heads // per
    count = both.shape[0]
    keys = count * rows
    wide = pl.BlockSpec((rows, per * width), lambda g, j: (0, g * steps + j))
    specs = dict(
        place=pl.BlockSpec(memory_space=pltpu.SMEM),
        raw=pl.BlockSpec((rows, per * width), lambda g, j: (step, g * steps + j)),
        heads=wide,
        both=pl.BlockSpec((count, rows, 2 * width), lambda g, j: (0, 0, g)),
        gain=pl.BlockSpec((1, width), lambda g, j: (0, 0)),
        table=pl.BlockSpec((rows, width), lambda g, j: (0, 0)),
    )
    params = pltpu.CompilerParams(vmem_limit_bytes=VMEM_BYTES)
    work = 2 * heads * rows * keys * width
    return kv_heads, heads, steps, keys, specs, params, work


def attend(raw, both, gain, cosine, sine, place, step, per=2):
    rows, width = cosine.shape
    kv_heads, heads, steps, keys, specs, params, work = attention_specs(
        raw, both, width, rows, step, per
    )
    return pl.pallas_call(
        functools.partial(attend_kernel, per, width ** (-0.5) * math.log2(math.e)),
        grid=(kv_heads, steps),
        in_specs=[specs[k] for k in ("place", "raw", "both", "gain", "table", "table")],
        out_specs=specs["heads"],
        out_shape=jax.ShapeDtypeStruct((rows, heads * width), jnp.bfloat16),
        scratch_shapes=[
            pltpu.VMEM((keys, rows), jnp.float32),
            pltpu.VMEM((width, keys), jnp.bfloat16),
        ],
        compiler_params=params,
        cost_estimate=SMALL,
    )(place, raw, both, gain, cosine, sine)


def attend_back(raw, grad, both, gain, cosine, sine, place, step, rows_out, per=2):
    rows, width = cosine.shape
    kv_heads, heads, steps, keys, specs, params, work = attention_specs(
        raw, both, width, rows, step, per
    )
    count = rows_out.shape[0]
    anywhere = pl.BlockSpec(memory_space=pl.ANY)
    return pl.pallas_call(
        functools.partial(
            attend_back_kernel,
            per,
            steps,
            width ** (-0.5) * math.log2(math.e),
            width ** (-0.5),
            count,
            both.shape[0],
        ),
        grid=(kv_heads, steps),
        in_specs=[specs[k] for k in ("place", "raw", "heads", "both", "gain", "table", "table")]
        + [anywhere],
        out_specs=(
            specs["heads"],
            anywhere,
            pl.BlockSpec((8, width), lambda g, j: (0, 0)),
            anywhere,
        ),
        out_shape=(
            jax.ShapeDtypeStruct((rows, heads * width), jnp.bfloat16),
            jax.ShapeDtypeStruct((both.shape[0], kv_heads, rows, 2 * width), jnp.bfloat16),
            jax.ShapeDtypeStruct((8, width), jnp.float32),
            jax.ShapeDtypeStruct(rows_out.shape, rows_out.dtype),
        ),
        scratch_shapes=[
            pltpu.VMEM((keys, rows), jnp.float32),
            pltpu.VMEM((width, keys), jnp.bfloat16),
            pltpu.VMEM((keys, 2 * width), jnp.float32),
            pltpu.VMEM((kv_heads, keys, 2 * width), jnp.bfloat16),
        ]
        + PlaneExchange.scratch(count)
        + RowExchange.scratch(both.shape[0], kv_heads),
        compiler_params=pltpu.CompilerParams(
            vmem_limit_bytes=VMEM_BYTES, collective_id=1 + step, has_side_effects=True
        ),
        cost_estimate=SMALL,
    )(place, raw, grad, both, gain, cosine, sine, rows_out)


class GradSums:
    def __init__(self, ring, sizes, refs):
        self.ring = ring
        self.sizes = sizes
        kinds = len(sizes)
        self.left, self.right = refs[:kinds], refs[kinds : 2 * kinds]
        self.out = refs[2 * kinds : 3 * kinds]
        scratch = refs[3 * kinds :]
        self.left_v, self.right_v = scratch[:kinds], scratch[kinds : 2 * kinds]
        self.part, self.first, self.second, self.last = (
            scratch[(2 + i) * kinds : (3 + i) * kinds] for i in range(4)
        )
        self.load_sem, self.first_sem, self.second_sem, self.last_sem = scratch[6 * kinds :]
        e = lax.axis_index("exp")
        self.y, self.x = lax.div(e, 4), lax.rem(lax.div(e, 2), 2)
        self.across_x, self.across_y = e + 2 - 4 * self.x, e + 4 - 8 * self.y
        self.z = lax.axis_index("ctx")
        self.order = [
            (kind, chunk) for kind, size in enumerate(sizes) for chunk in range(size[2] // size[3])
        ]

    @staticmethod
    def scratch(ring, sizes):
        chunks = [size[2] // size[3] for size in sizes]
        total = sum(chunks)
        shapes = [pltpu.VMEM((4, size[0], size[1]), jnp.bfloat16) for size in sizes]
        shapes += [pltpu.VMEM((2, size[0], size[3]), jnp.bfloat16) for size in sizes]
        for lead, share in (((4,), 1), ((2,), 1), ((), 1), ((ring,), ring)):
            for size, count in zip(sizes, chunks):
                shapes.append(
                    pltpu.VMEM((count,) + lead + (size[1] // share, size[3]), jnp.bfloat16)
                )
        shapes += [
            pltpu.SemaphoreType.DMA((len(sizes) + total,)),
            pltpu.SemaphoreType.DMA((2, total, 2)),
            pltpu.SemaphoreType.DMA((2, total)),
            pltpu.SemaphoreType.DMA((2, total, ring)),
        ]
        return shapes

    def x_first(self, i):
        return i % 2 == 0

    def load(self, i):
        kind, chunk = self.order[i]
        wide = self.sizes[kind][3]
        return pltpu.make_async_copy(
            self.right[kind].at[:, pl.ds(chunk * wide, wide)],
            self.right_v[kind].at[chunk % 2],
            self.load_sem.at[len(self.sizes) + i],
        )

    def load_left(self, kind):
        return pltpu.make_async_copy(
            self.left[kind], self.left_v[kind], self.load_sem.at[kind]
        )

    def step_first(self, i, k):
        kind, chunk = self.order[i]
        if self.x_first(i):
            piece, to = 2 * k + 1 - self.x, self.across_x
        else:
            piece, to = 2 * (1 - self.y) + k, self.across_y
        return pltpu.make_async_remote_copy(
            src_ref=self.part[kind].at[chunk, piece],
            dst_ref=self.first[kind].at[chunk, k],
            send_sem=self.first_sem.at[0, i, k],
            recv_sem=self.first_sem.at[1, i, k],
            device_id={"exp": to},
            device_id_type=pl.DeviceIdType.MESH,
        )

    def step_second(self, i):
        kind, chunk = self.order[i]
        if self.x_first(i):
            piece, to = 2 * (1 - self.y) + self.x, self.across_y
        else:
            piece, to = 2 * self.y + 1 - self.x, self.across_x
        return pltpu.make_async_remote_copy(
            src_ref=self.part[kind].at[chunk, piece],
            dst_ref=self.second[kind].at[chunk],
            send_sem=self.second_sem.at[0, i],
            recv_sem=self.second_sem.at[1, i],
            device_id={"exp": to},
            device_id_type=pl.DeviceIdType.MESH,
        )

    def mine(self, i):
        kind, chunk = self.order[i]
        return self.part[kind].at[chunk, 2 * self.y + self.x]

    def step_last(self, i, k, slot):
        kind, chunk = self.order[i]
        to = lax.rem(self.z + k, self.ring)
        rows = self.sizes[kind][1] // self.ring
        return pltpu.make_async_remote_copy(
            src_ref=self.mine(i).at[pl.ds(to * rows, rows)],
            dst_ref=self.last[kind].at[chunk, slot],
            send_sem=self.last_sem.at[0, i, k],
            recv_sem=self.last_sem.at[1, i, k],
            device_id={"ctx": to},
            device_id_type=pl.DeviceIdType.MESH,
        )

    def multiply(self, i):
        kind, chunk = self.order[i]
        self.load(i).wait()

        def piece(p, carry):
            term = lax.dot_general(
                self.left_v[kind][p],
                self.right_v[kind][chunk % 2],
                (((0,), (0,)), ((), ())),
                preferred_element_type=jnp.float32,
            )
            self.part[kind][chunk, p] = term.astype(jnp.bfloat16)
            return carry

        lax.fori_loop(0, 4, piece, 0)
        for k in range(2):
            self.step_first(i, k).start()

    def add_first(self, i):
        kind, chunk = self.order[i]
        for k in range(2):
            self.step_first(i, k).wait_recv()
        for k in range(2):
            piece = 2 * k + self.x if self.x_first(i) else 2 * self.y + k
            self.part[kind][chunk, piece] = (
                self.part[kind][chunk, piece].astype(jnp.float32)
                + self.first[kind][chunk, k].astype(jnp.float32)
            ).astype(jnp.bfloat16)
        self.step_second(i).start()

    def add_second(self, i):
        kind, chunk = self.order[i]
        self.step_second(i).wait_recv()
        piece = 2 * self.y + self.x
        self.part[kind][chunk, piece] = (
            self.part[kind][chunk, piece].astype(jnp.float32)
            + self.second[kind][chunk].astype(jnp.float32)
        ).astype(jnp.bfloat16)
        for k in range(1, self.ring):
            self.step_last(i, k, k).start()

    def add_last(self, i):
        kind, chunk = self.order[i]
        rows, wide = self.sizes[kind][1] // self.ring, self.sizes[kind][3]
        for k in range(1, self.ring):
            self.step_last(i, k, k).wait_recv()
        total = self.part[kind][
            chunk, 2 * self.y + self.x, pl.ds(pl.multiple_of(self.z * rows, rows), rows), :
        ].astype(jnp.float32)
        for k in range(1, self.ring):
            total += self.last[kind][chunk, k].astype(jnp.float32)
        self.out[kind][:, chunk * wide : (chunk + 1) * wide] = total

    def run(self):
        chunks = len(self.order)
        for kind in range(len(self.sizes)):
            self.load_left(kind).start()
        self.load(0).start()
        barrier = pltpu.get_barrier_semaphore()
        for other in (self.across_x, self.across_y):
            pl.semaphore_signal(
                barrier, inc=1, device_id={"exp": other}, device_id_type=pl.DeviceIdType.MESH
            )
        for k in range(1, self.ring):
            pl.semaphore_signal(
                barrier,
                inc=1,
                device_id={"ctx": lax.rem(self.z + k, self.ring)},
                device_id_type=pl.DeviceIdType.MESH,
            )
        pl.semaphore_wait(barrier, self.ring + 1)
        for i in range(chunks + 6):
            if i < chunks:
                if i + 1 < chunks:
                    self.load(i + 1).start()
                if self.order[i][1] == 0:
                    self.load_left(self.order[i][0]).wait()
                self.multiply(i)
            if 0 <= i - 2 < chunks:
                self.add_first(i - 2)
            if 0 <= i - 4 < chunks:
                self.add_second(i - 4)
            if 0 <= i - 6 < chunks:
                self.add_last(i - 6)
        for i in range(chunks):
            for k in range(2):
                self.step_first(i, k).wait_send()
            self.step_second(i).wait_send()
            for k in range(1, self.ring):
                self.step_last(i, k, k).wait_send()


def grad_sums_kernel(ring, sizes, *refs):
    GradSums(ring, sizes, refs).run()


def grad_sums(ring, lefts, rights, wides, number):
    sizes = [
        (left.shape[1], left.shape[2], right.shape[1], wide)
        for left, right, wide in zip(lefts, rights, wides)
    ]
    anywhere = pl.BlockSpec(memory_space=pl.ANY)
    return pl.pallas_call(
        functools.partial(grad_sums_kernel, ring, sizes),
        in_specs=[anywhere] * (2 * len(sizes)),
        out_specs=[pl.BlockSpec(memory_space=pltpu.VMEM)] * len(sizes),
        out_shape=[
            jax.ShapeDtypeStruct((size[1] // ring, size[2]), jnp.float32) for size in sizes
        ],
        scratch_shapes=GradSums.scratch(ring, sizes),
        compiler_params=pltpu.CompilerParams(
            vmem_limit_bytes=60 * 2**20, collective_id=number, has_side_effects=True
        ),
        cost_estimate=SMALL,
    )(*lefts, *rights)


def per_device(
    tokens,
    routes,
    route_weights,
    bounds,
    norm_attn,
    norm_ffn,
    q_gain,
    k_gain,
    w_q,
    w_k,
    w_v,
    w_o,
    w_gate,
    w_up,
    w_down,
    cotangent,
):
    micro = tokens.shape[0]
    local = tokens.shape[2]
    width = tokens.shape[3]
    head_dim = q_gain.shape[0]
    kv_heads = w_k.shape[1] // head_dim
    top = routes.shape[3]
    ring = lax.axis_size("ctx")
    plane = lax.axis_size("exp")
    assert w_gate.shape[0] == 1
    experts = ring * plane
    capacity = max(2, local * top * 5 // (4 * experts))
    seq_len = local * ring
    query_width = w_q.shape[1]
    pair_width = kv_heads * head_dim
    here = lax.axis_index("ctx")
    base = here * local
    cosine, sine = rope_tables(base + jnp.arange(local, dtype=jnp.int32), head_dim)
    gate_weight, up_weight, down_weight = w_gate[0], w_up[0], w_down[0]

    def dot(a, b):
        return jnp.dot(a, b, preferred_element_type=jnp.float32)

    def dot_t(a, b):
        return jnp.einsum("te,de->td", a, b, preferred_element_type=jnp.float32)

    def t_dot(a, b):
        return jnp.einsum("td,te->de", a, b, preferred_element_type=jnp.float32)

    def paired(keys, values):
        rows = keys.shape[0]
        return jnp.stack(
            [keys.reshape(rows, kv_heads, head_dim), values.reshape(rows, kv_heads, head_dim)], 2
        ).reshape(rows, 2 * pair_width)

    in_weight = lax.all_gather(
        jnp.concatenate([w_q, paired(w_k, w_v)], 1), "exp", axis=0, tiled=True
    )
    out_weight = lax.all_gather(w_o, "exp", axis=0, tiled=True)

    meta = jnp.concatenate([routes[:, 0].astype(jnp.float32), route_weights[:, 0]], -1)
    grads_low = [cotangent[step, 0] for step in range(micro)]
    *grad_blocks, meta = line_gather(*grads_low, meta.reshape(-1, 128), number=0)
    meta = meta.reshape(ring, micro, local, 2 * top)
    tables = [
        plane_tables(
            meta[:, step, :, :top].astype(jnp.int32), meta[:, step, :, top:], here * plane, plane
        )
        for step in range(micro)
    ]
    slots = jnp.arange(capacity, dtype=jnp.int32)
    chosen = [
        place.transpose(1, 0, 2)[:, :, None, :] == slots[None, None, :, None] for place, _ in tables
    ]

    def exchange(rows):
        return lax.all_to_all(rows, "exp", split_axis=0, concat_axis=0, tiled=True)

    def pick(blocks, step, weighted):
        return pick_rows(*tables[step], blocks, capacity, weighted)

    def combine(back, step, weighted):
        back = back.reshape(plane, ring, capacity, width)
        factor = chosen[step]
        if weighted:
            weight = tables[step][1].transpose(1, 0, 2)
            factor = jnp.where(factor, weight[:, :, None, :], 0.0)
        part = jnp.einsum(
            "jcst,jcsd->ctd",
            factor.astype(jnp.bfloat16),
            back,
            preferred_element_type=jnp.float32,
        )
        return part.astype(jnp.bfloat16).reshape(seq_len, width)

    def scatter(part):
        return lax.psum_scatter(part, "ctx", scatter_dimension=0, tiled=True).astype(jnp.float32)

    picked = pick_rows(
        jnp.concatenate([place for place, _ in tables]),
        jnp.concatenate([weight for _, weight in tables]),
        jnp.concatenate(grad_blocks),
        capacity,
        True,
    )
    incoming = exchange(picked.reshape(plane, micro * ring * capacity, width)).reshape(
        plane, micro, ring * capacity, width
    )

    rows = tokens[:, 0].astype(jnp.float32).reshape(micro * local, width)
    hidden, first_scale = norm_rows(rows, norm_attn)
    hidden = after(hidden.astype(jnp.bfloat16), picked)
    raw = dot(hidden, in_weight)
    pair_raw = raw[:, query_width:].reshape(micro * local, kv_heads, 2, head_dim)
    key_raw = pair_raw[:, :, 0]
    key_normed, key_scale = norm_rows(key_raw, k_gain)
    key_cos = jnp.tile(cosine, (micro, 1))[:, None, :]
    key_sin = jnp.tile(sine, (micro, 1))[:, None, :]
    keys = (key_normed * key_cos + swap_halves(key_normed) * key_sin).astype(jnp.bfloat16)
    pairs = jnp.stack([keys, pair_raw[:, :, 1].astype(jnp.bfloat16)], 2).reshape(
        micro * local, 2 * pair_width
    )
    gain_row = q_gain[None, :]
    both, places, attended, middles, feeds, scales = [], [], [], [], [], []
    for step in range(micro):
        part = slice(step * local, (step + 1) * local)
        own_pairs = pairs[part]
        if feeds:
            own_pairs = after(own_pairs, feeds[-1])
        (gathered,) = line_gather(own_pairs, number=3 + step)
        both.append(gathered.reshape(ring, local, 2 * pair_width))
        places.append(jnp.stack([base, bounds[step, 0]]).astype(jnp.int32))
        attended.append(attend(raw, both[step], gain_row, cosine, sine, places[step], step))
        middles.append(rows[part] + dot(attended[step], out_weight))
        feed_in, second_scale = norm_rows(middles[step], norm_ffn)
        feeds.append(feed_in.astype(jnp.bfloat16))
        scales.append(second_scale)
    feed_blocks = [lax.all_gather(feed, "ctx", axis=0, tiled=True) for feed in feeds]

    def slotted(rows):
        return rows.reshape(plane, ring * capacity, width)

    received = []
    last = incoming
    for step in range(micro):
        received.append(exchange(after(slotted(pick(feed_blocks[step], step, False)), last)))
        last = received[-1]

    active, gate_grad, up_grad, produced, backs, pair_values = [], [], [], [], [], []
    for step in range(micro):
        parts = run_expert(received[step], incoming, gate_weight, up_weight, down_weight, step)
        for held, item in zip((active, gate_grad, up_grad, produced, backs, pair_values), parts):
            held.append(item)

    returned = []
    for step in range(micro):
        returned.append(exchange(after(slotted(backs[step]), last)))
        last = returned[-1]
    gate_term, up_term, down_term = expert_weight_grads(
        received, incoming, active, gate_grad, up_grad
    )
    returned[-1] = after(returned[-1], down_term)
    parts = [combine(returned[step], step, False) for step in range(micro)]

    branches, raw_grads, middle_grads, gain_list, results = [], [], [], [], []
    waits = (parts[-1],)
    for step in range(micro):
        middle_norm_grad, second_gain = norm_back(
            middles[step], scales[step], norm_ffn, scatter(parts[step])
        )
        middle_grads.append(grads_low[step].astype(jnp.float32) + middle_norm_grad)
        branches.append(middle_grads[step].astype(jnp.bfloat16))
        attended_grad = dot_t(branches[step], out_weight).astype(jnp.bfloat16)
        raw_grad, pair_part, query_gain_part, result = attend_back(
            raw,
            attended_grad,
            both[step],
            gain_row,
            cosine,
            sine,
            places[step],
            step,
            after(slotted(produced[step]), *waits),
        )
        waits = (result,)
        results.append(result)
        raw_grads.append(raw_grad)
        gain_list.append([jnp.sum(second_gain, 0), query_gain_part[0], pair_part])
    pair_grads = []
    key_cos, key_sin = cosine[None], sine[None]
    for step in range(micro):
        part = slice(step * local, (step + 1) * local)
        landed = jnp.sum(gain_list[step][2].astype(jnp.float32), 0).astype(jnp.bfloat16)
        key_grad = landed[..., :head_dim].astype(jnp.float32)
        key_turned = key_grad * key_cos - swap_halves(key_grad) * key_sin
        key_raw_grad, key_gain_part = norm_back(
            key_raw[part].transpose(1, 0, 2), key_scale[part].transpose(1, 0, 2), k_gain, key_turned
        )
        pair_grad = jnp.concatenate(
            [key_raw_grad.astype(jnp.bfloat16), landed[..., head_dim:]], -1
        )
        pair_grads.append(pair_grad.transpose(1, 0, 2).reshape(local, 2 * pair_width))
        gain_list[step][2] = jnp.sum(key_gain_part, (0, 1))

    attended_all, branch_all = jnp.concatenate(attended, 0), jnp.concatenate(branches, 0)
    raw_grad = jnp.concatenate(
        [jnp.concatenate(raw_grads, 0), jnp.concatenate(pair_grads, 0)], 1
    )
    if plane == 8:
        core = lax.rem(lax.axis_index("exp"), 2)

        def swapped(array):
            return lax.ppermute(array, "exp", [(i, i + 1 - 2 * (i % 2)) for i in range(plane)])

        def left_part(array):
            share = array.shape[1] // experts
            array = array.reshape(-1, ring, 2, 2, 2, share).transpose(4, 2, 3, 0, 1, 5)
            array = array.reshape(2, 4, micro * local, ring * share)
            own = lax.dynamic_index_in_dim(array, core, 0, False)
            other = lax.dynamic_index_in_dim(array, 1 - core, 0, False)
            return jnp.concatenate([own, swapped(other)], 1)

        def right_part(array):
            return jnp.concatenate([array, swapped(array)], 0)

        out_total, in_total = grad_sums(
            ring,
            (left_part(attended_all), left_part(hidden)),
            (right_part(branch_all), right_part(raw_grad)),
            (512, 1024),
            5,
        )
    else:

        def sum_over_devices(left, right):
            share = left.shape[1] // experts
            left = left.reshape(-1, ring, plane, share).transpose(0, 2, 1, 3)
            term = t_dot(left.reshape(-1, experts * share), right).astype(jnp.bfloat16)
            term = lax.psum_scatter(term, "exp", scatter_dimension=0, tiled=True)
            return lax.psum_scatter(term, "ctx", scatter_dimension=0, tiled=True).astype(
                jnp.float32
            )

        out_total = sum_over_devices(attended_all, branch_all)
        in_total = sum_over_devices(hidden, raw_grad)
    query_total = in_total[:, :query_width]
    pair_total = in_total[:, query_width:].reshape(-1, kv_heads, 2, head_dim)
    hidden_grad = dot_t(raw_grad, in_weight)
    first_grad, first_gain = norm_back(rows, first_scale, norm_attn, hidden_grad)
    tokens_grad = jnp.concatenate(middle_grads, 0) + first_grad
    gains = jnp.concatenate([jnp.sum(first_gain, 0)] + [sum(parts) for parts in zip(*gain_list)])
    gain_total = jnp.sum(
        lax.all_to_all(
            gains.reshape(experts, -1), ("ctx", "exp"), split_axis=0, concat_axis=0, tiled=True
        ),
        0,
    )

    outputs = [
        (middles[step] + scatter(combine(results[step], step, True))).astype(jnp.bfloat16)
        for step in range(micro)
    ]

    pair_values = lax.all_to_all(
        jnp.stack([v.reshape(plane, ring, capacity) for v in pair_values], 1),
        "exp",
        split_axis=0,
        concat_axis=0,
        tiled=True,
    )
    values = jnp.stack(
        [
            jnp.sum(jnp.where(chosen[step], pair_values[:, step, :, :, None], 0.0), 2)
            for step in range(micro)
        ],
        1,
    )
    values = lax.all_to_all(
        values.transpose(2, 1, 3, 0), "ctx", split_axis=0, concat_axis=0, tiled=True
    )
    values = values.transpose(1, 2, 0, 3).reshape(micro, local, experts)
    match = routes[:, 0, :, :, None] == jnp.arange(experts, dtype=jnp.int32)
    route_grads = jnp.sum(jnp.where(match, values[:, :, None, :], 0.0), -1) / route_weights[:, 0]

    return (
        jnp.stack(outputs)[:, None],
        tokens_grad.reshape(micro, 1, local, width),
        route_grads[:, None],
        query_total,
        pair_total[:, :, 0].reshape(-1, pair_width),
        pair_total[:, :, 1].reshape(-1, pair_width),
        out_total,
        gain_total,
        gate_term,
        up_term,
        down_term,
    )


def solution(mesh):
    in_specs = (
        P(None, "exp", "ctx", None),
        P(None, "exp", "ctx", None),
        P(None, "exp", "ctx", None),
        P(None, "exp"),
        P(),
        P(),
        P(),
        P(),
        P("exp", None),
        P("exp", None),
        P("exp", None),
        P("exp", None),
        P(("ctx", "exp"), None, None),
        P(("ctx", "exp"), None, None),
        P(("ctx", "exp"), None, None),
        P(None, "exp", "ctx", None),
    )
    out_specs = (
        P(None, "exp", "ctx", None),
        P(None, "exp", "ctx", None),
        P(None, "exp", "ctx", None),
        P(("ctx", "exp"), None),
        P(("ctx", "exp"), None),
        P(("ctx", "exp"), None),
        P(("ctx", "exp"), None),
        P(("ctx", "exp")),
        P(("ctx", "exp"), None, None),
        P(("ctx", "exp"), None, None),
        P(("ctx", "exp"), None, None),
    )
    return jax.shard_map(
        per_device, mesh=mesh, in_specs=in_specs, out_specs=out_specs, check_vma=False
    )
```

```python
import functools
import math

import jax
import jax.numpy as jnp
from jax import lax
from jax.experimental import pallas as pl
from jax.experimental.pallas import tpu as pltpu
from jax.sharding import PartitionSpec as P

EPSILON = 1e-06
ROPE_BASE = 1000000.0
MASKED = -1e30
VMEM_BYTES = 56 * 2**20
SMALL = pl.CostEstimate(flops=2**20, bytes_accessed=2**20, transcendentals=0)


def norm_rows(value, gain):
    scale = lax.rsqrt(jnp.mean(value * value, -1, keepdims=True) + EPSILON)
    return (value * scale * gain, scale)


def norm_back(value, scale, gain, grad):
    inner = grad * gain
    first = scale * inner - value * (scale * scale * scale) * jnp.mean(
        inner * value, -1, keepdims=True
    )
    return (first, grad * value * scale)


def rope_tables(positions, width):
    half = width // 2
    inverse = ROPE_BASE ** (-jnp.arange(half, dtype=jnp.float32) * 2.0 / width)
    angle = positions.astype(jnp.float32)[:, None] * inverse[None, :]
    cosine, sine = jnp.cos(angle), jnp.sin(angle)
    return (jnp.concatenate([cosine, cosine], -1), jnp.concatenate([-sine, sine], -1))


def swap_halves(value):
    half = value.shape[-1] // 2
    return jnp.concatenate([value[..., half:], value[..., :half]], -1)


def nothing_kernel(*refs):
    pass


def after(value, *others):
    return pl.pallas_call(
        nothing_kernel,
        in_specs=[pl.BlockSpec(memory_space=pl.ANY)] * (1 + len(others)),
        out_specs=pl.BlockSpec(memory_space=pl.ANY),
        out_shape=jax.ShapeDtypeStruct(value.shape, value.dtype),
        input_output_aliases={0: 0},
    )(value, *others)


def gather_kernel(count, arrays, stacked, *refs):
    own = refs[:arrays]
    full = [refs[arrays].at[i] for i in range(stacked)]
    full += refs[arrays + min(stacked, 1) : -3]
    send_sem, recv_sem, own_sem = refs[-3:]
    me = lax.axis_index("ctx")
    barrier = pltpu.get_barrier_semaphore()
    for other in (lax.rem(me + 1, count), lax.rem(me + count - 1, count)):
        pl.semaphore_signal(
            barrier, inc=1, device_id={"ctx": other}, device_id_type=pl.DeviceIdType.MESH
        )
    pl.semaphore_wait(barrier, 2)

    def block(i, at):
        rows = own[i].shape[0]
        return full[i].at[pl.ds(at * rows, rows)]

    def passing(way, step, i, at):
        return pltpu.make_async_remote_copy(
            src_ref=own[i] if step == 0 else block(i, at),
            dst_ref=block(i, at),
            send_sem=send_sem.at[way, step, i],
            recv_sem=recv_sem.at[way, step, i],
            device_id={"ctx": me + (1 if way == 0 else -1)},
            device_id_type=pl.DeviceIdType.MESH,
        )

    def sends(way, step):
        if way == 0:
            return (me >= step) & (me < count - 1)
        return (me + step < count) & (me > 0)

    def receives(way, step):
        return me >= step + 1 if way == 0 else me + step + 1 < count

    kept = [pltpu.make_async_copy(own[i], block(i, me), own_sem.at[i]) for i in range(arrays)]
    for step in range(count - 1):
        for i in range(arrays):
            for way in (0, 1):
                sign = 1 if way == 0 else -1

                @pl.when(sends(way, step))
                def _():
                    passing(way, step, i, me - sign * step).start()

        if step == 0:
            for copy in kept:
                copy.start()
        for i in range(arrays):
            for way in (0, 1):
                sign = 1 if way == 0 else -1

                @pl.when(receives(way, step))
                def _():
                    passing(way, step, i, me - sign * (step + 1)).wait_recv()

    for copy in kept:
        copy.wait()
    for step in range(count - 1):
        for i in range(arrays):
            for way in (0, 1):
                sign = 1 if way == 0 else -1

                @pl.when(sends(way, step))
                def _():
                    passing(way, step, i, me - sign * step).wait_send()


def line_gather(*blocks, number, stacked=0):
    count = lax.axis_size("ctx")
    arrays = len(blocks)
    shapes = [(count * block.shape[0],) + block.shape[1:] for block in blocks]
    types = [block.dtype for block in blocks]
    if stacked:
        shapes = [(stacked,) + shapes[0]] + shapes[stacked:]
        types = types[:1] + types[stacked:]
    return pl.pallas_call(
        functools.partial(gather_kernel, count, arrays, stacked),
        in_specs=[pl.BlockSpec(memory_space=pl.ANY)] * arrays,
        out_specs=[pl.BlockSpec(memory_space=pl.ANY)] * len(shapes),
        out_shape=[jax.ShapeDtypeStruct(*pair) for pair in zip(shapes, types)],
        scratch_shapes=[
            pltpu.SemaphoreType.DMA((2, count - 1, arrays)),
            pltpu.SemaphoreType.DMA((2, count - 1, arrays)),
            pltpu.SemaphoreType.DMA((arrays,)),
        ],
        compiler_params=pltpu.CompilerParams(collective_id=number, has_side_effects=True),
        cost_estimate=pl.CostEstimate(flops=0, bytes_accessed=200 * 2**20, transcendentals=0),
    )(*blocks)


def expert_kernel(
    rows_ref,
    grad_ref,
    gate_ref,
    up_ref,
    down_ref,
    active_ref,
    gate_grad_ref,
    up_grad_ref,
    out_ref,
    back_ref,
    value_ref,
):
    gate = along(rows_ref[...], gate_ref[...])
    upper = along(rows_ref[...], up_ref[...])
    active_grad = across(grad_ref[...], down_ref[...])
    sigma = jax.nn.sigmoid(gate)
    swish = gate * sigma
    active = (swish * upper).astype(jnp.bfloat16)
    active_ref[...] = active
    out_ref[...] = along(active, down_ref[...]).astype(jnp.bfloat16)
    gate_grad = (active_grad * upper * sigma * (1.0 + gate * (1.0 - sigma))).astype(jnp.bfloat16)
    up_grad = (active_grad * swish).astype(jnp.bfloat16)
    gate_grad_ref[...] = gate_grad
    up_grad_ref[...] = up_grad
    value_ref[...] = jnp.sum(active_grad * active.astype(jnp.float32), -1, keepdims=True)
    back_ref[...] = (across(gate_grad, gate_ref[...]) + across(up_grad, up_ref[...])).astype(
        jnp.bfloat16
    )


def run_expert(rows, grad, gate, up, down, step):
    sources, block, width = rows.shape
    units = gate.shape[1]
    total = sources * block
    wide = pl.BlockSpec((block, width), lambda i: (i, 0))
    narrow = pl.BlockSpec((block, units), lambda i: (i, 0))

    def whole(shape):
        return pl.BlockSpec(shape, lambda i: (0, 0), pipeline_mode=pl.Buffered(1))

    low = jax.ShapeDtypeStruct((total, units), jnp.bfloat16)
    full = jax.ShapeDtypeStruct((total, width), jnp.bfloat16)
    return pl.pallas_call(
        expert_kernel,
        grid=(sources,),
        in_specs=[
            pl.BlockSpec((None, block, width), lambda i: (i, 0, 0)),
            pl.BlockSpec((None, None, block, width), lambda i: (i, step, 0, 0)),
            whole(gate.shape),
            whole(up.shape),
            whole(down.shape),
        ],
        out_specs=(narrow, narrow, narrow, wide, wide, pl.BlockSpec((block, 1), lambda i: (i, 0))),
        out_shape=(low, low, low, full, full, jax.ShapeDtypeStruct((total, 1), jnp.float32)),
        compiler_params=pltpu.CompilerParams(vmem_limit_bytes=VMEM_BYTES),
        cost_estimate=SMALL,
    )(rows, grad, gate, up, down)


def plane_tables(routes_all, weights_all, first, planned):
    hit = routes_all[..., None] == first + jnp.arange(planned, dtype=jnp.int32)
    named = jnp.any(hit, -2)
    weight = jnp.sum(jnp.where(hit, weights_all[..., None], 0.0), -2)
    rows = routes_all.shape[-2]
    earlier = (
        jnp.arange(rows, dtype=jnp.int32)[:, None] > jnp.arange(rows, dtype=jnp.int32)[None, :]
    ).astype(jnp.bfloat16)
    rank = jnp.einsum(
        "tu,cuj->ctj", earlier, named.astype(jnp.bfloat16), preferred_element_type=jnp.float32
    ).astype(jnp.int32)
    place = jnp.where(named, rank, -1)
    return place.transpose(0, 2, 1), weight.transpose(0, 2, 1)


def pick_kernel(planes, place_ref, weight_ref, rows_ref, out_ref, weighted):
    capacity = out_ref.shape[2]
    local = rows_ref.shape[0]
    slots = lax.broadcasted_iota(jnp.int32, (capacity, local), 0)
    if capacity % 16 == 0:
        chosen = [place_ref[0, 0, j : j + 1, :] == slots for j in range(planes)]
        picked = jnp.dot(
            jnp.concatenate([jnp.where(c, 1.0, 0.0).astype(jnp.bfloat16) for c in chosen], 0),
            rows_ref[...],
            preferred_element_type=jnp.float32,
        )
        for j in range(planes):
            rows = picked[j * capacity : (j + 1) * capacity]
            if weighted:
                rows = rows * jnp.sum(
                    jnp.where(chosen[j], weight_ref[0, 0, j : j + 1, :], 0.0), -1, keepdims=True
                )
            out_ref[j, 0] = rows.astype(jnp.bfloat16)
        return
    for j in range(planes):
        chosen = place_ref[0, 0, j : j + 1, :] == slots
        picked = jnp.dot(
            jnp.where(chosen, 1.0, 0.0).astype(jnp.bfloat16),
            rows_ref[...],
            preferred_element_type=jnp.float32,
        )
        if weighted:
            picked = picked * jnp.sum(
                jnp.where(chosen, weight_ref[0, 0, j : j + 1, :], 0.0), -1, keepdims=True
            )
        out_ref[j, 0] = picked.astype(jnp.bfloat16)


def pick_rows(place, weight, blocks, capacity, weighted):
    count, planned, local = place.shape
    width = blocks.shape[1]
    part = 4 if planned % 4 == 0 else planned
    shape = (count, planned // part, part, local)
    return pl.pallas_call(
        functools.partial(pick_kernel, part, weighted=weighted),
        grid=(count, planned // part),
        in_specs=[
            pl.BlockSpec((1, 1, part, local), lambda c, g: (c, g, 0, 0)),
            pl.BlockSpec((1, 1, part, local), lambda c, g: (c, g, 0, 0)),
            pl.BlockSpec((local, width), lambda c, g: (c, 0)),
        ],
        out_specs=pl.BlockSpec((part, 1, capacity, width), lambda c, g: (g, c, 0, 0)),
        out_shape=jax.ShapeDtypeStruct((planned, count, capacity, width), jnp.bfloat16),
        compiler_params=pltpu.CompilerParams(vmem_limit_bytes=VMEM_BYTES),
        cost_estimate=SMALL,
    )(place.reshape(shape), weight.reshape(shape), blocks)


def weight_kernel(steps, micro, *refs):
    rows, (grads_ref,) = refs[:micro], refs[micro : micro + 1]
    actives, gates, ups = (refs[micro * i + 1 : micro * i + 1 + micro] for i in (1, 2, 3))
    outs = refs[4 * micro + 1 : 4 * micro + 4]
    sums, sem = refs[4 * micro + 4 : 4 * micro + 7], refs[-1]
    step = pl.program_id(0)

    def flat(ref):
        count, block, width = ref.shape
        return ref[...].reshape(count * block, width)

    def add(which, fresh):
        x = flat(rows[which])
        for sum_ref, left, right in (
            (sums[0], x, gates[which][...]),
            (sums[1], x, ups[which][...]),
            (sums[2], actives[which][...], flat(grads_ref)),
        ):
            term = lax.dot_general(
                left, right, (((0,), (0,)), ((), ())), preferred_element_type=jnp.float32
            )
            if fresh:
                sum_ref[0] = term
            else:
                sum_ref[0] += term

    pl.when(step == 0)(lambda: add(0, True))
    pl.when((step > 0) & (step < steps))(lambda: add(0, False))
    for which in range(1, micro):
        pl.when((step >= which * steps) & (step < (which + 1) * steps))(
            functools.partial(add, which, False)
        )

    @pl.when(step == micro * steps - 1)
    def _():
        copies = [pltpu.make_async_copy(sums[i], outs[i], sem.at[i]) for i in range(3)]
        for copy in copies:
            copy.start()
        for copy in copies:
            copy.wait()


def expert_weight_grads(rows, grads, actives, gates, ups):
    sources, micro, block, width = grads.shape
    units = gates[0].shape[1]
    steps = sources // 2

    def turn(i, which):
        return jnp.clip(i - which * steps, 0, steps - 1)

    def specs(size):
        return [
            pl.BlockSpec((2 * block, size), functools.partial(lambda w, i: (turn(i, w), 0), which))
            for which in range(micro)
        ]

    def row_specs():
        return [
            pl.BlockSpec(
                (2, block, width), functools.partial(lambda w, i: (turn(i, w), 0, 0), which)
            )
            for which in range(micro)
        ]

    shapes = [(1, width, units), (1, width, units), (1, units, width)]
    return pl.pallas_call(
        functools.partial(weight_kernel, steps, micro),
        grid=(micro * steps,),
        in_specs=row_specs()
        + [
            pl.BlockSpec(
                (2, None, block, width), lambda i: (lax.rem(i, steps), lax.div(i, steps), 0, 0)
            )
        ]
        + specs(units) * 3,
        out_specs=[pl.BlockSpec(memory_space=pl.ANY)] * 3,
        out_shape=[jax.ShapeDtypeStruct(shape, jnp.float32) for shape in shapes],
        scratch_shapes=[pltpu.VMEM(shape, jnp.float32) for shape in shapes]
        + [pltpu.SemaphoreType.DMA((3,))],
        compiler_params=pltpu.CompilerParams(vmem_limit_bytes=VMEM_BYTES),
        cost_estimate=SMALL,
    )(*rows, grads, *actives, *gates, *ups)


def fill_mask(place_ref, mask_ref):
    base, bound = place_ref[0], place_ref[1]
    keys, rows = mask_ref.shape
    key_at = lax.broadcasted_iota(jnp.int32, (keys, rows), 0)
    row_at = lax.broadcasted_iota(jnp.int32, (keys, rows), 1) + base
    least = jnp.where(row_at >= bound, bound, 0)
    mask_ref[...] = jnp.where((key_at <= row_at) & (key_at >= least), 0.0, MASKED)


def head_queries(raw, gain, cosine, sine):
    scale = lax.rsqrt(jnp.mean(raw * raw, -1, keepdims=True) + EPSILON)
    value = raw * scale * gain
    turned = value * cosine + pltpu.roll(value, value.shape[-1] // 2, 1) * sine
    return turned.astype(jnp.bfloat16), scale


def across(a, b):
    return lax.dot_general(a, b, (((1,), (1,)), ((), ())), preferred_element_type=jnp.float32)


def along(a, b):
    return jnp.dot(a, b, preferred_element_type=jnp.float32)


def keyed(both_ref, width, which):
    count, rows = both_ref.shape[:2]
    return both_ref[:, :, which * width : (which + 1) * width].reshape(count * rows, width)


def attend_kernel(
    per, factor, place_ref, raw_ref, both_ref, gain_ref, cos_ref, sin_ref, *rest
):
    out_ref, mask_ref, turned_ref = rest[-3:]
    width = gain_ref.shape[1]
    group_step, step = pl.program_id(0), pl.program_id(1)

    @pl.when((group_step == 0) & (step == 0))
    def _():
        fill_mask(place_ref, mask_ref)

    @pl.when(step == 0)
    def _():
        turned_ref[...] = keyed(both_ref, width, 1).T

    for head in range(per):
        columns = slice(head * width, (head + 1) * width)
        queries, _ = head_queries(raw_ref[:, columns], gain_ref[...], cos_ref[...], sin_ref[...])
        chances = jnp.exp2(across(keyed(both_ref, width, 0), queries) * factor + mask_ref[...])
        total = jnp.sum(chances, 0, keepdims=True)
        result = along(turned_ref[...], chances.astype(jnp.bfloat16)) * (1.0 / total)
        out_ref[:, columns] = result.T.astype(jnp.bfloat16)


class Exchange:
    def __init__(self, axis, rows_ref, out_ref, send_sem, recv_sem, own_sem):
        self.axis, self.count = axis, rows_ref.shape[0]
        self.rows_ref, self.out_ref = rows_ref, out_ref
        self.send_sem, self.recv_sem, self.own_sem = send_sem, recv_sem, own_sem
        self.me = lax.axis_index(axis)

    @staticmethod
    def scratch(count):
        return [
            pltpu.SemaphoreType.DMA((count,)),
            pltpu.SemaphoreType.DMA((count,)),
            pltpu.SemaphoreType.DMA,
        ]

    def passing(self, k, part):
        return pltpu.make_async_remote_copy(
            src_ref=self.rows_ref.at[lax.rem(self.me + k, self.count)],
            dst_ref=self.out_ref.at[part],
            send_sem=self.send_sem.at[k],
            recv_sem=self.recv_sem.at[k],
            device_id={self.axis: lax.rem(self.me + k, self.count)},
            device_id_type=pl.DeviceIdType.MESH,
        )

    def kept(self):
        return pltpu.make_async_copy(
            self.rows_ref.at[self.me], self.out_ref.at[self.me], self.own_sem
        )

    def begin(self):
        for k in range(1, self.count):
            self.passing(k, self.me).start()
        self.kept().start()

    def finish(self):
        self.kept().wait()
        for k in range(1, self.count):
            self.passing(k, lax.rem(self.me + self.count - k, self.count)).wait_recv()
        for k in range(1, self.count):
            self.passing(k, self.me).wait_send()


def greet(**counts):
    barrier = pltpu.get_barrier_semaphore()
    for axis, count in counts.items():
        me = lax.axis_index(axis)
        for k in range(1, count):
            pl.semaphore_signal(
                barrier,
                inc=1,
                device_id={axis: lax.rem(me + k, count)},
                device_id_type=pl.DeviceIdType.MESH,
            )
    pl.semaphore_wait(barrier, sum(counts.values()) - len(counts))


class RowExchange:
    def __init__(self, ring, held_ref, out_ref, send_sem, recv_sem, own_sem):
        self.ring, self.held_ref, self.out_ref = ring, held_ref, out_ref
        self.send_sem, self.recv_sem, self.own_sem = send_sem, recv_sem, own_sem
        self.me = lax.axis_index("ctx")
        self.rows = out_ref.shape[2]

    @staticmethod
    def scratch(ring, groups):
        return [
            pltpu.SemaphoreType.DMA((groups, ring)),
            pltpu.SemaphoreType.DMA((groups, ring)),
            pltpu.SemaphoreType.DMA((groups,)),
        ]

    def held(self, group, at):
        return self.held_ref.at[group, pl.ds(at * self.rows, self.rows)]

    def passing(self, group, k, part):
        to = lax.rem(self.me + k, self.ring)
        return pltpu.make_async_remote_copy(
            src_ref=self.held(group, to),
            dst_ref=self.out_ref.at[part, group],
            send_sem=self.send_sem.at[group, k],
            recv_sem=self.recv_sem.at[group, k],
            device_id={"ctx": to},
            device_id_type=pl.DeviceIdType.MESH,
        )

    def kept(self, group):
        return pltpu.make_async_copy(
            self.held(group, self.me), self.out_ref.at[self.me, group], self.own_sem.at[group]
        )

    def begin(self, group):
        for k in range(1, self.ring):
            self.passing(group, k, self.me).start()
        self.kept(group).start()

    def finish(self):
        for group in range(self.out_ref.shape[1]):
            self.kept(group).wait()
            for k in range(1, self.ring):
                self.passing(group, k, lax.rem(self.me + self.ring - k, self.ring)).wait_recv()
            for k in range(1, self.ring):
                self.passing(group, k, self.me).wait_send()


def attend_back_kernel(
    per,
    steps,
    factor,
    scale,
    count,
    ring,
    extra_axis,
    place_ref,
    raw_ref,
    grad_ref,
    both_ref,
    gain_ref,
    cos_ref,
    sin_ref,
    rows_ref,
    extra_ref,
    raw_grad_ref,
    landed_ref,
    gain_grad_ref,
    moved_ref,
    extra_moved_ref,
    mask_ref,
    turned_ref,
    sums_ref,
    held_ref,
    *sems,
):
    width = gain_ref.shape[1]
    group_step, step = pl.program_id(0), pl.program_id(1)
    moving = Exchange("exp", rows_ref, moved_ref, *sems[:3])
    extra_moving = Exchange(extra_axis, extra_ref, extra_moved_ref, *sems[3:6])
    landing = RowExchange(ring, held_ref, landed_ref, *sems[6:])

    @pl.when((group_step == 0) & (step == 0))
    def _():
        greet(exp=count, ctx=ring)
        moving.begin()
        extra_moving.begin()

    @pl.when((group_step == 0) & (step == 0))
    def _():
        fill_mask(place_ref, mask_ref)
        gain_grad_ref[...] = jnp.zeros_like(gain_grad_ref)

    @pl.when(step == 0)
    def _():
        turned_ref[...] = keyed(both_ref, width, 0).T
        sums_ref[...] = jnp.zeros_like(sums_ref)

    for head in range(per):
        columns = slice(head * width, (head + 1) * width)
        raw = raw_ref[:, columns]
        queries, norm = head_queries(raw, gain_ref[...], cos_ref[...], sin_ref[...])
        grad = grad_ref[:, columns]
        chances = jnp.exp2(across(keyed(both_ref, width, 0), queries) * factor + mask_ref[...])
        chances = chances * (1.0 / jnp.sum(chances, 0, keepdims=True))
        chance_grad = across(keyed(both_ref, width, 1), grad)
        mean = jnp.sum(chances * chance_grad, 0, keepdims=True)
        score_grad = (chances * (chance_grad - mean)).astype(jnp.bfloat16)
        sums_ref[:, :width] += along(score_grad, queries)
        sums_ref[:, width:] += along(chances.astype(jnp.bfloat16), grad)
        query_grad = (along(turned_ref[...], score_grad) * scale).astype(jnp.bfloat16)
        query_grad = query_grad.astype(jnp.float32).T
        back = query_grad * cos_ref[...] - pltpu.roll(query_grad, width // 2, 1) * sin_ref[...]
        inner = back * gain_ref[...]
        first = norm * inner - raw * (norm * norm * norm) * jnp.mean(inner * raw, -1, keepdims=True)
        raw_grad_ref[:, columns] = first.astype(jnp.bfloat16)
        gain_grad_ref[0:1, :] += jnp.sum(back * raw * norm, 0, keepdims=True)

    @pl.when(step == steps - 1)
    def _():
        held_ref[group_step, :, :width] = (sums_ref[:, :width] * scale).astype(jnp.bfloat16)
        held_ref[group_step, :, width:] = sums_ref[:, width:].astype(jnp.bfloat16)
        landing.begin(group_step)

    @pl.when((group_step == pl.num_programs(0) - 1) & (step == steps - 1))
    def _():
        landing.finish()
        extra_moving.finish()
        moving.finish()


def attention_specs(raw, both, width, rows, step, per):
    kv_heads = both.shape[2] // (2 * width)
    heads = raw.shape[1] // width - 2 * kv_heads
    steps = heads // kv_heads // per
    count = both.shape[0]
    keys = count * rows
    wide = pl.BlockSpec((rows, per * width), lambda g, j: (0, g * steps + j))
    specs = dict(
        place=pl.BlockSpec(memory_space=pltpu.SMEM),
        raw=pl.BlockSpec((rows, per * width), lambda g, j: (step, g * steps + j)),
        heads=wide,
        both=pl.BlockSpec((count, rows, 2 * width), lambda g, j: (0, 0, g)),
        gain=pl.BlockSpec((1, width), lambda g, j: (0, 0)),
        table=pl.BlockSpec((rows, width), lambda g, j: (0, 0)),
    )
    params = pltpu.CompilerParams(vmem_limit_bytes=VMEM_BYTES)
    work = 2 * heads * rows * keys * width
    return kv_heads, heads, steps, keys, specs, params, work


def attend(raw, both, gain, cosine, sine, place, step, waits, per=2):
    rows, width = cosine.shape
    kv_heads, heads, steps, keys, specs, params, work = attention_specs(
        raw, both, width, rows, step, per
    )
    return pl.pallas_call(
        functools.partial(attend_kernel, per, width ** (-0.5) * math.log2(math.e)),
        grid=(kv_heads, steps),
        in_specs=[specs[k] for k in ("place", "raw", "both", "gain", "table", "table")]
        + [pl.BlockSpec(memory_space=pl.ANY)] * len(waits),
        out_specs=specs["heads"],
        out_shape=jax.ShapeDtypeStruct((rows, heads * width), jnp.bfloat16),
        scratch_shapes=[
            pltpu.VMEM((keys, rows), jnp.float32),
            pltpu.VMEM((width, keys), jnp.bfloat16),
        ],
        compiler_params=params,
        cost_estimate=SMALL,
    )(place, raw, both, gain, cosine, sine, *waits)


def attend_back(
    raw, grad, both, gain, cosine, sine, place, step, rows_out, extra, extra_axis, per=2
):
    rows, width = cosine.shape
    kv_heads, heads, steps, keys, specs, params, work = attention_specs(
        raw, both, width, rows, step, per
    )
    count = rows_out.shape[0]
    anywhere = pl.BlockSpec(memory_space=pl.ANY)
    return pl.pallas_call(
        functools.partial(
            attend_back_kernel,
            per,
            steps,
            width ** (-0.5) * math.log2(math.e),
            width ** (-0.5),
            count,
            both.shape[0],
            extra_axis,
        ),
        grid=(kv_heads, steps),
        in_specs=[specs[k] for k in ("place", "raw", "heads", "both", "gain", "table", "table")]
        + [anywhere] * 2,
        out_specs=(
            specs["heads"],
            anywhere,
            pl.BlockSpec((8, width), lambda g, j: (0, 0)),
            anywhere,
            anywhere,
        ),
        out_shape=(
            jax.ShapeDtypeStruct((rows, heads * width), jnp.bfloat16),
            jax.ShapeDtypeStruct((both.shape[0], kv_heads, rows, 2 * width), jnp.bfloat16),
            jax.ShapeDtypeStruct((8, width), jnp.float32),
            jax.ShapeDtypeStruct(rows_out.shape, rows_out.dtype),
            jax.ShapeDtypeStruct(extra.shape, extra.dtype),
        ),
        scratch_shapes=[
            pltpu.VMEM((keys, rows), jnp.float32),
            pltpu.VMEM((width, keys), jnp.bfloat16),
            pltpu.VMEM((keys, 2 * width), jnp.float32),
            pltpu.VMEM((kv_heads, keys, 2 * width), jnp.bfloat16),
        ]
        + Exchange.scratch(count) + Exchange.scratch(extra.shape[0])
        + RowExchange.scratch(both.shape[0], kv_heads),
        compiler_params=pltpu.CompilerParams(
            vmem_limit_bytes=VMEM_BYTES, collective_id=1 + step, has_side_effects=True
        ),
        cost_estimate=SMALL,
    )(place, raw, grad, both, gain, cosine, sine, rows_out, extra)


def combine_kernel(place_ref, weight_ref, back_ref, out_ref, *, weighted):
    experts, _, capacity, width = back_ref.shape
    local = out_ref.shape[0]
    slots = lax.broadcasted_iota(jnp.int32, (capacity, local), 0)
    factors = []
    for j in range(experts):
        value = weight_ref[0, j : j + 1, :] if weighted else 1.0
        chosen = place_ref[0, j : j + 1, :] == slots
        factors.append(jnp.where(chosen, value, 0.0).astype(jnp.bfloat16))
    out_ref[...] = lax.dot_general(
        jnp.concatenate(factors, 0),
        back_ref[...].reshape(experts * capacity, width),
        (((0,), (0,)), ((), ())),
        preferred_element_type=jnp.float32,
    ).astype(jnp.bfloat16)


def combine_rows(place, weight, back, weighted):
    count, planned, local = place.shape
    capacity, width = back.shape[2:]
    return pl.pallas_call(
        functools.partial(combine_kernel, weighted=weighted),
        grid=(count,),
        in_specs=[
            pl.BlockSpec((1, planned, local), lambda c: (c, 0, 0)),
            pl.BlockSpec((1, planned, local), lambda c: (c, 0, 0)),
            pl.BlockSpec((planned, 1, capacity, width), lambda c: (0, c, 0, 0)),
        ],
        out_specs=pl.BlockSpec((local, width), lambda c: (c, 0)),
        out_shape=jax.ShapeDtypeStruct((count * local, width), jnp.bfloat16),
        compiler_params=pltpu.CompilerParams(vmem_limit_bytes=VMEM_BYTES),
        cost_estimate=SMALL,
    )(place, weight, back)


class GradSums:
    def __init__(self, ring, micro, sizes, refs):
        self.ring, self.micro, self.sizes = ring, micro, sizes
        self.attended, self.hidden = refs[:micro], refs[micro]
        refs = refs[micro + 1 :]
        self.branch, self.query, self.pair = (
            refs[i * micro : (i + 1) * micro] for i in range(3)
        )
        self.weight = refs[3 * micro]
        self.out = refs[3 * micro + 1 : 3 * micro + 3]
        self.hidden_grad = refs[3 * micro + 3]
        self.far = refs[3 * micro + 4 : 3 * micro + 7]
        scratch = refs[3 * micro + 7 :]
        self.left_v, self.right_v = scratch[:2], scratch[2:4]
        self.part, self.first, self.second, self.last = (
            scratch[4 + 2 * i : 6 + 2 * i] for i in range(4)
        )
        (
            self.left_sem,
            self.far_sem,
            self.load_sem,
            self.first_sem,
            self.second_sem,
            self.last_sem,
            self.weight_sem,
        ) = scratch[12:]
        e = lax.axis_index("exp")
        self.core, self.y, self.x = lax.rem(e, 2), lax.div(e, 4), lax.rem(lax.div(e, 2), 2)
        self.partner = e + 1 - 2 * self.core
        self.across_x, self.across_y = e + 2 - 4 * self.x, e + 4 - 8 * self.y
        self.z = lax.axis_index("ctx")
        self.order = [
            (kind, chunk) for kind, size in enumerate(sizes) for chunk in range(size[2] // size[3])
        ]

    @staticmethod
    def scratch(ring, micro, sizes):
        chunks = [size[2] // size[3] for size in sizes]
        total = sum(chunks)
        shapes = [pltpu.VMEM((4, size[0], size[1]), jnp.bfloat16) for size in sizes]
        shapes += [pltpu.VMEM((2, size[0], size[3]), jnp.bfloat16) for size in sizes]
        for lead, share in (((4,), 1), ((2,), 1), ((), 1), ((ring,), ring)):
            for size, count in zip(sizes, chunks):
                shapes.append(
                    pltpu.VMEM((count,) + lead + (size[1] // share, size[3]), jnp.bfloat16)
                )
        shapes += [
            pltpu.SemaphoreType.DMA((3, micro + 1, 4, ring)),
            pltpu.SemaphoreType.DMA((2, 3, micro)),
            pltpu.SemaphoreType.DMA((total, 2, micro)),
            pltpu.SemaphoreType.DMA((2, total, 2)),
            pltpu.SemaphoreType.DMA((2, total)),
            pltpu.SemaphoreType.DMA((2, total, ring)),
            pltpu.SemaphoreType.DMA((4,)),
        ]
        return shapes

    def weight_loads(self, chunk):
        _, high, wide = self.left_v[0].shape
        return [
            pltpu.make_async_copy(
                self.weight.at[pl.ds(r * high, high), pl.ds((2 * chunk + h) * wide, wide)],
                self.left_v[0].at[2 * r + h],
                self.weight_sem.at[2 * r + h],
            )
            for r in (0, 1)
            for h in (0, 1)
        ]

    def add_hidden(self, chunk):
        _, high, wide = self.left_v[0].shape
        half = self.sizes[1][0] // 2
        for copy in self.weight_loads(chunk):
            copy.wait()
        for r in (0, 1):
            columns = slice(r * high, (r + 1) * high)
            for h in (0, 1):
                term = across(
                    self.right_v[1][chunk % 2, :half, h * wide : (h + 1) * wide],
                    self.left_v[0][2 * r + h],
                )
                if chunk == 0 and h == 0:
                    self.hidden_grad[:, columns] = term
                else:
                    self.hidden_grad[:, columns] += term

    def to_partner(self, src, dst, send_sem, recv_sem):
        return pltpu.make_async_remote_copy(
            src_ref=src,
            dst_ref=dst,
            send_sem=send_sem,
            recv_sem=recv_sem,
            device_id={"exp": self.partner},
            device_id_type=pl.DeviceIdType.MESH,
        )

    def left_copies(self, kind):
        half = self.sizes[kind][0] // 2
        own, sent = [], []
        if kind == 1:
            place = (self.micro, 0, 0)
            own.append(
                pltpu.make_async_copy(
                    self.hidden.at[self.core],
                    self.left_v[1].at[:, pl.ds(0, half)],
                    self.left_sem.at[(0,) + place],
                )
            )
            sent.append(
                self.to_partner(
                    self.hidden.at[1 - self.core],
                    self.left_v[1].at[:, pl.ds(half, half)],
                    self.left_sem.at[(1,) + place],
                    self.left_sem.at[(2,) + place],
                )
            )
            return own, sent
        share = self.sizes[kind][1] // self.ring
        rows = half // self.micro
        for m in range(self.micro):
            for piece in range(4):
                for c in range(self.ring):

                    def columns(core):
                        block = c * 8 + piece * 2 + core
                        return self.attended[m].at[
                            :, pl.ds(pl.multiple_of(block * share, share), share)
                        ]

                    def place(base):
                        return self.left_v[0].at[
                            piece, pl.ds(base + m * rows, rows), pl.ds(c * share, share)
                        ]

                    own.append(
                        pltpu.make_async_copy(
                            columns(self.core), place(0), self.left_sem.at[0, m, piece, c]
                        )
                    )
                    sent.append(
                        self.to_partner(
                            columns(1 - self.core),
                            place(half),
                            self.left_sem.at[1, m, piece, c],
                            self.left_sem.at[2, m, piece, c],
                        )
                    )
        return own, sent

    def right_copies(self, which):
        near = (self.branch, self.query, self.pair)[which]
        return [
            self.to_partner(
                near[m],
                self.far[which].at[m],
                self.far_sem.at[0, which, m],
                self.far_sem.at[1, which, m],
            )
            for m in range(self.micro)
        ]

    def source(self, i):
        kind, chunk = self.order[i]
        wide = self.sizes[kind][3]
        if kind == 0:
            return 0, chunk * wide
        query_width = self.query[0].shape[1]
        if chunk * wide < query_width:
            return 1, chunk * wide
        return 2, chunk * wide - query_width

    def loads(self, i, far):
        kind, chunk = self.order[i]
        which, start = self.source(i)
        wide = self.sizes[kind][3]
        half = self.sizes[kind][0] // 2
        rows = half // self.micro
        near = (self.branch, self.query, self.pair)[which]
        return [
            pltpu.make_async_copy(
                (self.far[which].at[m] if far else near[m]).at[:, pl.ds(start, wide)],
                self.right_v[kind].at[chunk % 2, pl.ds(far * half + m * rows, rows)],
                self.load_sem.at[i, far, m],
            )
            for m in range(self.micro)
        ]

    def start_loads(self, i):
        which, start = self.source(i)
        for copy in self.loads(i, 0):
            copy.start()
        if start == 0:
            for copy in self.right_copies(which):
                copy.wait_recv()
        for copy in self.loads(i, 1):
            copy.start()

    def x_first(self, i):
        return i % 2 == 0

    def step_first(self, i, k):
        kind, chunk = self.order[i]
        if self.x_first(i):
            piece, to = 2 * k + 1 - self.x, self.across_x
        else:
            piece, to = 2 * (1 - self.y) + k, self.across_y
        return pltpu.make_async_remote_copy(
            src_ref=self.part[kind].at[chunk, piece],
            dst_ref=self.first[kind].at[chunk, k],
            send_sem=self.first_sem.at[0, i, k],
            recv_sem=self.first_sem.at[1, i, k],
            device_id={"exp": to},
            device_id_type=pl.DeviceIdType.MESH,
        )

    def step_second(self, i):
        kind, chunk = self.order[i]
        if self.x_first(i):
            piece, to = 2 * (1 - self.y) + self.x, self.across_y
        else:
            piece, to = 2 * self.y + 1 - self.x, self.across_x
        return pltpu.make_async_remote_copy(
            src_ref=self.part[kind].at[chunk, piece],
            dst_ref=self.second[kind].at[chunk],
            send_sem=self.second_sem.at[0, i],
            recv_sem=self.second_sem.at[1, i],
            device_id={"exp": to},
            device_id_type=pl.DeviceIdType.MESH,
        )

    def mine(self, i):
        kind, chunk = self.order[i]
        return self.part[kind].at[chunk, 2 * self.y + self.x]

    def step_last(self, i, k, slot):
        kind, chunk = self.order[i]
        to = lax.rem(self.z + k, self.ring)
        rows = self.sizes[kind][1] // self.ring
        return pltpu.make_async_remote_copy(
            src_ref=self.mine(i).at[pl.ds(to * rows, rows)],
            dst_ref=self.last[kind].at[chunk, slot],
            send_sem=self.last_sem.at[0, i, k],
            recv_sem=self.last_sem.at[1, i, k],
            device_id={"ctx": to},
            device_id_type=pl.DeviceIdType.MESH,
        )

    def multiply(self, i):
        kind, chunk = self.order[i]
        for far in (0, 1):
            for copy in self.loads(i, far):
                copy.wait()

        def piece(p, carry):
            term = lax.dot_general(
                self.left_v[kind][p],
                self.right_v[kind][chunk % 2],
                (((0,), (0,)), ((), ())),
                preferred_element_type=jnp.float32,
            )
            self.part[kind][chunk, p] = term.astype(jnp.bfloat16)
            return carry

        lax.fori_loop(0, 4, piece, 0)
        for k in range(2):
            self.step_first(i, k).start()

    def add_first(self, i):
        kind, chunk = self.order[i]
        for k in range(2):
            self.step_first(i, k).wait_recv()
        for k in range(2):
            piece = 2 * k + self.x if self.x_first(i) else 2 * self.y + k
            self.part[kind][chunk, piece] = (
                self.part[kind][chunk, piece].astype(jnp.float32)
                + self.first[kind][chunk, k].astype(jnp.float32)
            ).astype(jnp.bfloat16)
        self.step_second(i).start()

    def add_second(self, i):
        kind, chunk = self.order[i]
        self.step_second(i).wait_recv()
        piece = 2 * self.y + self.x
        self.part[kind][chunk, piece] = (
            self.part[kind][chunk, piece].astype(jnp.float32)
            + self.second[kind][chunk].astype(jnp.float32)
        ).astype(jnp.bfloat16)
        for k in range(1, self.ring):
            self.step_last(i, k, k).start()

    def add_last(self, i):
        kind, chunk = self.order[i]
        rows, wide = self.sizes[kind][1] // self.ring, self.sizes[kind][3]
        for k in range(1, self.ring):
            self.step_last(i, k, k).wait_recv()
        total = self.part[kind][
            chunk, 2 * self.y + self.x, pl.ds(pl.multiple_of(self.z * rows, rows), rows), :
        ].astype(jnp.float32)
        for k in range(1, self.ring):
            total += self.last[kind][chunk, k].astype(jnp.float32)
        self.out[kind][:, chunk * wide : (chunk + 1) * wide] = total

    def run(self):
        chunks = len(self.order)
        barrier = pltpu.get_barrier_semaphore()
        for other in (self.partner, self.across_x, self.across_y):
            pl.semaphore_signal(
                barrier, inc=1, device_id={"exp": other}, device_id_type=pl.DeviceIdType.MESH
            )
        for k in range(1, self.ring):
            pl.semaphore_signal(
                barrier,
                inc=1,
                device_id={"ctx": lax.rem(self.z + k, self.ring)},
                device_id_type=pl.DeviceIdType.MESH,
            )
        pl.semaphore_wait(barrier, self.ring + 2)
        lefts = [self.left_copies(kind) for kind in (0, 1)]
        rights = [self.right_copies(which) for which in range(3)]
        for copies in (rights[0], lefts[0][1], lefts[0][0], rights[1], *lefts[1], rights[2]):
            for copy in copies:
                copy.start()
        self.start_loads(0)
        for i in range(chunks + 6):
            if i < chunks:
                if i + 1 < chunks:
                    self.start_loads(i + 1)
                kind, chunk = self.order[i]
                if chunk == 0:
                    for copy in lefts[kind][0]:
                        copy.wait()
                    for copy in lefts[kind][1]:
                        copy.wait_recv()
                self.multiply(i)
                if kind == 0 and chunk == self.sizes[0][2] // self.sizes[0][3] - 1:
                    for copy in self.weight_loads(0):
                        copy.start()
                if kind == 1:
                    self.add_hidden(chunk)
                    if i + 1 < chunks:
                        for copy in self.weight_loads(chunk + 1):
                            copy.start()
            if 0 <= i - 2 < chunks:
                self.add_first(i - 2)
            if 0 <= i - 4 < chunks:
                self.add_second(i - 4)
            if 0 <= i - 6 < chunks:
                self.add_last(i - 6)
        for copies in (lefts[0][1], lefts[1][1], *rights):
            for copy in copies:
                copy.wait_send()
        for i in range(chunks):
            for k in range(2):
                self.step_first(i, k).wait_send()
            self.step_second(i).wait_send()
            for k in range(1, self.ring):
                self.step_last(i, k, k).wait_send()


def grad_sums_kernel(ring, micro, sizes, *refs):
    GradSums(ring, micro, sizes, refs).run()


def grad_sums(ring, attended, hidden, branch, query, pair, weight, number):
    micro, rows = len(attended), attended[0].shape[0]
    tokens = 2 * micro * rows
    sizes = [
        (tokens, attended[0].shape[1] // 8, branch[0].shape[1], 512),
        (tokens, hidden.shape[3], query[0].shape[1] + pair[0].shape[1], 1024),
    ]
    anywhere = pl.BlockSpec(memory_space=pl.ANY)
    assert weight.shape[0] == 2 * tokens and sizes[1][3] == 2 * sizes[0][1]
    outs = [
        jax.ShapeDtypeStruct((size[1] // ring, size[2]), jnp.float32) for size in sizes
    ]
    outs.append(jax.ShapeDtypeStruct((micro * rows, weight.shape[0]), jnp.float32))
    outs += [
        jax.ShapeDtypeStruct((micro,) + arrays[0].shape, jnp.bfloat16)
        for arrays in (branch, query, pair)
    ]
    return pl.pallas_call(
        functools.partial(grad_sums_kernel, ring, micro, sizes),
        in_specs=[anywhere] * (4 * micro + 2),
        out_specs=[pl.BlockSpec(memory_space=pltpu.VMEM)] * 3 + [anywhere] * 3,
        out_shape=outs,
        scratch_shapes=GradSums.scratch(ring, micro, sizes),
        compiler_params=pltpu.CompilerParams(
            vmem_limit_bytes=60 * 2**20, collective_id=number, has_side_effects=True
        ),
        cost_estimate=SMALL,
    )(*attended, hidden, *branch, *query, *pair, weight)[:3]


def per_device(
    tokens,
    routes,
    route_weights,
    bounds,
    norm_attn,
    norm_ffn,
    q_gain,
    k_gain,
    w_q,
    w_k,
    w_v,
    w_o,
    w_gate,
    w_up,
    w_down,
    cotangent,
):
    micro = tokens.shape[0]
    local = tokens.shape[2]
    width = tokens.shape[3]
    head_dim = q_gain.shape[0]
    kv_heads = w_k.shape[1] // head_dim
    top = routes.shape[3]
    ring = lax.axis_size("ctx")
    plane = lax.axis_size("exp")
    assert w_gate.shape[0] == 1
    experts = ring * plane
    capacity = max(2, local * top * 5 // (4 * experts))
    seq_len = local * ring
    query_width = w_q.shape[1]
    pair_width = kv_heads * head_dim
    here = lax.axis_index("ctx")
    base = here * local
    cosine, sine = rope_tables(base + jnp.arange(local, dtype=jnp.int32), head_dim)
    gate_weight, up_weight, down_weight = w_gate[0], w_up[0], w_down[0]

    def dot(a, b):
        return jnp.dot(a, b, preferred_element_type=jnp.float32)

    def dot_t(a, b):
        return jnp.einsum("te,de->td", a, b, preferred_element_type=jnp.float32)

    def t_dot(a, b):
        return jnp.einsum("td,te->de", a, b, preferred_element_type=jnp.float32)

    def paired(keys, values):
        rows = keys.shape[0]
        return jnp.stack(
            [keys.reshape(rows, kv_heads, head_dim), values.reshape(rows, kv_heads, head_dim)], 2
        ).reshape(rows, 2 * pair_width)

    in_weight = lax.all_gather(
        jnp.concatenate([w_q, paired(w_k, w_v)], 1), "exp", axis=0, tiled=True
    )
    out_weight = lax.all_gather(w_o, "exp", axis=0, tiled=True)

    meta = jnp.concatenate([routes[:, 0].astype(jnp.float32), route_weights[:, 0]], -1)
    grads_low = [cotangent[step, 0] for step in range(micro)]
    grad_blocks, meta = line_gather(
        *grads_low, meta.reshape(-1, 128), number=0, stacked=micro
    )
    meta = meta.reshape(ring, micro, local, 2 * top)
    tables = [
        plane_tables(
            meta[:, step, :, :top].astype(jnp.int32), meta[:, step, :, top:], here * plane, plane
        )
        for step in range(micro)
    ]
    slots = jnp.arange(capacity, dtype=jnp.int32)
    chosen = [
        place.transpose(1, 0, 2)[:, :, None, :] == slots[None, None, :, None] for place, _ in tables
    ]

    def exchange(rows):
        return lax.all_to_all(rows, "exp", split_axis=0, concat_axis=0, tiled=True)

    def pick(blocks, step, weighted):
        return pick_rows(*tables[step], blocks, capacity, weighted)

    def combine(back, step, weighted):
        back = back.reshape(plane, ring, capacity, width)
        if capacity % 16 == 0:
            return combine_rows(*tables[step], back, weighted)
        factor = chosen[step]
        if weighted:
            weight = tables[step][1].transpose(1, 0, 2)
            factor = jnp.where(factor, weight[:, :, None, :], 0.0)
        part = jnp.einsum(
            "jcst,jcsd->ctd",
            factor.astype(jnp.bfloat16),
            back,
            preferred_element_type=jnp.float32,
        )
        return part.astype(jnp.bfloat16).reshape(seq_len, width)

    def scatter(part):
        return lax.psum_scatter(part, "ctx", scatter_dimension=0, tiled=True)

    picked = pick_rows(
        jnp.concatenate([place for place, _ in tables]),
        jnp.concatenate([weight for _, weight in tables]),
        grad_blocks.reshape(micro * seq_len, width),
        capacity,
        True,
    )
    incoming = exchange(picked.reshape(plane, micro * ring * capacity, width)).reshape(
        plane, micro, ring * capacity, width
    )

    rows = tokens[:, 0].astype(jnp.float32).reshape(micro * local, width)
    hidden, first_scale = norm_rows(rows, norm_attn)
    hidden = after(hidden.astype(jnp.bfloat16), picked)
    raw = dot(hidden, in_weight)
    hidden_parts = hidden.reshape(-1, ring, plane // 2, 2, width // experts)
    hidden_parts = hidden_parts.transpose(3, 2, 0, 1, 4).reshape(
        2, plane // 2, micro * local, ring * width // experts
    )
    pair_raw = raw[:, query_width:].reshape(micro * local, kv_heads, 2, head_dim)
    key_raw = pair_raw[:, :, 0]
    key_normed, key_scale = norm_rows(key_raw, k_gain)
    key_cos = jnp.tile(cosine, (micro, 1))[:, None, :]
    key_sin = jnp.tile(sine, (micro, 1))[:, None, :]
    keys = (key_normed * key_cos + swap_halves(key_normed) * key_sin).astype(jnp.bfloat16)
    pairs = jnp.stack([keys, pair_raw[:, :, 1].astype(jnp.bfloat16)], 2).reshape(
        micro * local, 2 * pair_width
    )
    gain_row = q_gain[None, :]
    both = line_gather(
        *[pairs[step * local : (step + 1) * local] for step in range(micro)], number=3
    )
    both = [gathered.reshape(ring, local, 2 * pair_width) for gathered in both]
    places, attended, middles, feeds, scales = [], [], [], [], []
    for step in range(micro):
        part = slice(step * local, (step + 1) * local)
        places.append(jnp.stack([base, bounds[step, 0]]).astype(jnp.int32))
        attended.append(
            attend(raw, both[step], gain_row, cosine, sine, places[step], step, feeds[-1:])
        )
        middles.append(rows[part] + dot(attended[step], out_weight))
        feed_in, second_scale = norm_rows(middles[step], norm_ffn)
        feeds.append(feed_in.astype(jnp.bfloat16))
        scales.append(second_scale)
    feed_blocks = [lax.all_gather(feed, "ctx", axis=0, tiled=True) for feed in feeds]

    def slotted(rows):
        return rows.reshape(plane, ring * capacity, width)

    received = []
    waits = (incoming,)
    feed_blocks[0] = after(feed_blocks[0], feeds[-1])
    for step in range(micro):
        picked = slotted(pick(feed_blocks[step], step, False))
        received.append(exchange(after(picked, *waits)))
        waits = (received[-1], hidden_parts)

    active, gate_grad, up_grad, produced, backs, pair_values = [], [], [], [], [], []
    for step in range(micro):
        parts = run_expert(received[step], incoming, gate_weight, up_weight, down_weight, step)
        for held, item in zip((active, gate_grad, up_grad, produced, backs, pair_values), parts):
            held.append(item)

    returned = []
    last = received[-1]
    for step in range(micro):
        returned.append(exchange(after(slotted(backs[step]), last)))
        last = returned[-1]
    gate_term, up_term, down_term = expert_weight_grads(
        received, incoming, active, gate_grad, up_grad
    )

    sums = jnp.stack([value.reshape(plane, ring * capacity) for value in pair_values], 1)
    sums = sums.reshape(plane, -1)
    spare = -sums.shape[1] % 1024
    extra = jnp.pad(sums, ((0, 0), (0, spare))).reshape(plane, -1, 128)

    branches, raw_grads, middle_grads, gain_list, results = [], [], [], [], []
    waits = ()
    for step in range(micro):
        if step > 0:
            feed_grad = after(feed_grad, *waits)
        else:
            feed_grad = scatter(combine(after(returned[0], active[-1]), 0, False))
        middle_norm_grad, second_gain = norm_back(
            middles[step], scales[step], norm_ffn, feed_grad.astype(jnp.float32)
        )
        middle_grads.append(grads_low[step].astype(jnp.float32) + middle_norm_grad)
        branches.append(middle_grads[step].astype(jnp.bfloat16))
        attended_grad = dot_t(branches[step], out_weight).astype(jnp.bfloat16)
        if step == 0:
            returned[1] = after(returned[1], down_term, attended_grad)
            part_sums = combine(returned[1], 1, False)
            feed_grad = scatter(part_sums)
            waits = (part_sums,)
        raw_grad, pair_part, query_gain_part, result, extra = attend_back(
            raw,
            attended_grad,
            both[step],
            gain_row,
            cosine,
            sine,
            places[step],
            step,
            after(slotted(produced[step]), *waits),
            extra,
            ("exp", "ctx")[min(step, 1)],
        )
        if step == 0:
            sums = extra.reshape(plane, -1)[:, : micro * ring * capacity]
            sums = sums.reshape(plane, micro, ring, capacity)
            values = [
                jnp.sum(jnp.where(chosen[m], sums[:, m, :, :, None], 0.0), 2) for m in range(micro)
            ]
            values = jnp.stack(values, 1).transpose(2, 1, 0, 3)
            extra = values.reshape(ring, -1, 128)
        waits = (result,)
        results.append(result)
        raw_grads.append(raw_grad)
        gain_list.append([jnp.sum(second_gain, 0), query_gain_part[0], pair_part])
    pair_grads = []
    key_cos, key_sin = cosine[None], sine[None]
    for step in range(micro):
        part = slice(step * local, (step + 1) * local)
        landed = jnp.sum(gain_list[step][2].astype(jnp.float32), 0).astype(jnp.bfloat16)
        key_grad = landed[..., :head_dim].astype(jnp.float32)
        key_turned = key_grad * key_cos - swap_halves(key_grad) * key_sin
        key_raw_grad, key_gain_part = norm_back(
            key_raw[part].transpose(1, 0, 2), key_scale[part].transpose(1, 0, 2), k_gain, key_turned
        )
        pair_grad = jnp.concatenate(
            [key_raw_grad.astype(jnp.bfloat16), landed[..., head_dim:]], -1
        )
        pair_grads.append(pair_grad.transpose(1, 0, 2).reshape(local, 2 * pair_width))
        gain_list[step][2] = jnp.sum(key_gain_part, (0, 1))

    if plane == 8:
        out_total, in_total, hidden_grad = grad_sums(
            ring, attended, hidden_parts, branches, raw_grads, pair_grads, in_weight, 5
        )
    else:

        def sum_over_devices(left, right):
            share = left.shape[1] // experts
            left = left.reshape(-1, ring, plane, share).transpose(0, 2, 1, 3)
            term = t_dot(left.reshape(-1, experts * share), right).astype(jnp.bfloat16)
            term = lax.psum_scatter(term, "exp", scatter_dimension=0, tiled=True)
            return lax.psum_scatter(term, "ctx", scatter_dimension=0, tiled=True).astype(
                jnp.float32
            )

        out_total = sum_over_devices(jnp.concatenate(attended, 0), jnp.concatenate(branches, 0))
        raw_grad = jnp.concatenate(
            [jnp.concatenate(raw_grads, 0), jnp.concatenate(pair_grads, 0)], 1
        )
        in_total = sum_over_devices(hidden, raw_grad)
        hidden_grad = dot_t(raw_grad, in_weight)
    query_total = in_total[:, :query_width]
    pair_total = in_total[:, query_width:].reshape(-1, kv_heads, 2, head_dim)
    first_grad, first_gain = norm_back(rows, first_scale, norm_attn, hidden_grad)
    tokens_grad = jnp.concatenate(middle_grads, 0) + first_grad
    gains = jnp.concatenate([jnp.sum(first_gain, 0)] + [sum(parts) for parts in zip(*gain_list)])
    gain_total = jnp.sum(
        lax.all_to_all(
            gains.reshape(experts, -1), ("ctx", "exp"), split_axis=0, concat_axis=0, tiled=True
        ),
        0,
    )

    outputs = [
        (middles[step] + scatter(combine(results[step], step, True)).astype(jnp.float32)).astype(
            jnp.bfloat16
        )
        for step in range(micro)
    ]

    values = extra.reshape(ring, micro, plane, local).transpose(1, 3, 0, 2)
    values = values.reshape(micro, local, experts)
    match = routes[:, 0, :, :, None] == jnp.arange(experts, dtype=jnp.int32)
    route_grads = jnp.sum(jnp.where(match, values[:, :, None, :], 0.0), -1) / route_weights[:, 0]

    return (
        jnp.stack(outputs)[:, None],
        tokens_grad.reshape(micro, 1, local, width),
        route_grads[:, None],
        query_total,
        pair_total[:, :, 0].reshape(-1, pair_width),
        pair_total[:, :, 1].reshape(-1, pair_width),
        out_total,
        gain_total,
        gate_term,
        up_term,
        down_term,
    )


def solution(mesh):
    in_specs = (
        P(None, "exp", "ctx", None),
        P(None, "exp", "ctx", None),
        P(None, "exp", "ctx", None),
        P(None, "exp"),
        P(),
        P(),
        P(),
        P(),
        P("exp", None),
        P("exp", None),
        P("exp", None),
        P("exp", None),
        P(("ctx", "exp"), None, None),
        P(("ctx", "exp"), None, None),
        P(("ctx", "exp"), None, None),
        P(None, "exp", "ctx", None),
    )
    out_specs = (
        P(None, "exp", "ctx", None),
        P(None, "exp", "ctx", None),
        P(None, "exp", "ctx", None),
        P(("ctx", "exp"), None),
        P(("ctx", "exp"), None),
        P(("ctx", "exp"), None),
        P(("ctx", "exp"), None),
        P(("ctx", "exp")),
        P(("ctx", "exp"), None, None),
        P(("ctx", "exp"), None, None),
        P(("ctx", "exp"), None, None),
    )
    return jax.shard_map(
        per_device, mesh=mesh, in_specs=in_specs, out_specs=out_specs, check_vma=False
    )
```

```python
import functools
import math

import jax
import jax.numpy as jnp
from jax import lax
from jax.experimental import pallas as pl
from jax.experimental.pallas import tpu as pltpu
from jax.sharding import PartitionSpec as P

EPSILON = 1e-06
ROPE_BASE = 1000000.0
MASKED = -1e30
LAGS = (2, 3, 5)
VMEM_BYTES = 56 * 2**20
SMALL = pl.CostEstimate(flops=2**20, bytes_accessed=2**20, transcendentals=0)


def norm_rows(value, gain):
    scale = lax.rsqrt(jnp.mean(value * value, -1, keepdims=True) + EPSILON)
    return (value * scale * gain, scale)


def norm_back(value, scale, gain, grad):
    inner = grad * gain
    first = scale * inner - value * (scale * scale * scale) * jnp.mean(
        inner * value, -1, keepdims=True
    )
    return (first, grad * value * scale)


def rope_tables(positions, width):
    half = width // 2
    inverse = ROPE_BASE ** (-jnp.arange(half, dtype=jnp.float32) * 2.0 / width)
    angle = positions.astype(jnp.float32)[:, None] * inverse[None, :]
    cosine, sine = jnp.cos(angle), jnp.sin(angle)
    return (jnp.concatenate([cosine, cosine], -1), jnp.concatenate([-sine, sine], -1))


def swap_halves(value):
    half = value.shape[-1] // 2
    return jnp.concatenate([value[..., half:], value[..., :half]], -1)


def nothing_kernel(*refs):
    pass


def after(value, *others):
    return pl.pallas_call(
        nothing_kernel,
        in_specs=[pl.BlockSpec(memory_space=pl.ANY)] * (1 + len(others)),
        out_specs=pl.BlockSpec(memory_space=pl.ANY),
        out_shape=jax.ShapeDtypeStruct(value.shape, value.dtype),
        input_output_aliases={0: 0},
    )(value, *others)


def gather_kernel(count, arrays, stacked, *refs):
    own = refs[:arrays]
    full = [refs[arrays].at[i] for i in range(stacked)]
    full += refs[arrays + min(stacked, 1) : -3]
    send_sem, recv_sem, own_sem = refs[-3:]
    me = lax.axis_index("ctx")
    barrier = pltpu.get_barrier_semaphore()
    for other in (lax.rem(me + 1, count), lax.rem(me + count - 1, count)):
        pl.semaphore_signal(
            barrier, inc=1, device_id={"ctx": other}, device_id_type=pl.DeviceIdType.MESH
        )
    pl.semaphore_wait(barrier, 2)

    def block(i, at):
        rows = own[i].shape[0]
        return full[i].at[pl.ds(at * rows, rows)]

    def passing(way, step, i, at):
        return pltpu.make_async_remote_copy(
            src_ref=own[i] if step == 0 else block(i, at),
            dst_ref=block(i, at),
            send_sem=send_sem.at[way, step, i],
            recv_sem=recv_sem.at[way, step, i],
            device_id={"ctx": me + (1 if way == 0 else -1)},
            device_id_type=pl.DeviceIdType.MESH,
        )

    def sends(way, step):
        if way == 0:
            return (me >= step) & (me < count - 1)
        return (me + step < count) & (me > 0)

    def receives(way, step):
        return me >= step + 1 if way == 0 else me + step + 1 < count

    kept = [pltpu.make_async_copy(own[i], block(i, me), own_sem.at[i]) for i in range(arrays)]
    for step in range(count - 1):
        for i in range(arrays):
            for way in (0, 1):
                sign = 1 if way == 0 else -1

                @pl.when(sends(way, step))
                def _():
                    passing(way, step, i, me - sign * step).start()

        if step == 0:
            for copy in kept:
                copy.start()
        for i in range(arrays):
            for way in (0, 1):
                sign = 1 if way == 0 else -1

                @pl.when(receives(way, step))
                def _():
                    passing(way, step, i, me - sign * (step + 1)).wait_recv()

    for copy in kept:
        copy.wait()
    for step in range(count - 1):
        for i in range(arrays):
            for way in (0, 1):
                sign = 1 if way == 0 else -1

                @pl.when(sends(way, step))
                def _():
                    passing(way, step, i, me - sign * step).wait_send()


def line_gather(*blocks, number, stacked=0):
    count = lax.axis_size("ctx")
    arrays = len(blocks)
    shapes = [(count * block.shape[0],) + block.shape[1:] for block in blocks]
    types = [block.dtype for block in blocks]
    if stacked:
        shapes = [(stacked,) + shapes[0]] + shapes[stacked:]
        types = types[:1] + types[stacked:]
    return pl.pallas_call(
        functools.partial(gather_kernel, count, arrays, stacked),
        in_specs=[pl.BlockSpec(memory_space=pl.ANY)] * arrays,
        out_specs=[pl.BlockSpec(memory_space=pl.ANY)] * len(shapes),
        out_shape=[jax.ShapeDtypeStruct(*pair) for pair in zip(shapes, types)],
        scratch_shapes=[
            pltpu.SemaphoreType.DMA((2, count - 1, arrays)),
            pltpu.SemaphoreType.DMA((2, count - 1, arrays)),
            pltpu.SemaphoreType.DMA((arrays,)),
        ],
        compiler_params=pltpu.CompilerParams(collective_id=number, has_side_effects=True),
        cost_estimate=pl.CostEstimate(flops=0, bytes_accessed=200 * 2**20, transcendentals=0),
    )(*blocks)


def expert_kernel(
    rows_ref,
    grad_ref,
    gate_ref,
    up_ref,
    down_ref,
    active_ref,
    gate_grad_ref,
    up_grad_ref,
    out_ref,
    back_ref,
    value_ref,
):
    gate = along(rows_ref[...], gate_ref[...])
    upper = along(rows_ref[...], up_ref[...])
    active_grad = across(grad_ref[...], down_ref[...])
    sigma = jax.nn.sigmoid(gate)
    swish = gate * sigma
    active = (swish * upper).astype(jnp.bfloat16)
    active_ref[...] = active
    out_ref[...] = along(active, down_ref[...]).astype(jnp.bfloat16)
    gate_grad = (active_grad * upper * sigma * (1.0 + gate * (1.0 - sigma))).astype(jnp.bfloat16)
    up_grad = (active_grad * swish).astype(jnp.bfloat16)
    gate_grad_ref[...] = gate_grad
    up_grad_ref[...] = up_grad
    value_ref[...] = jnp.sum(active_grad * active.astype(jnp.float32), -1, keepdims=True)
    back_ref[...] = (across(gate_grad, gate_ref[...]) + across(up_grad, up_ref[...])).astype(
        jnp.bfloat16
    )


def run_expert(rows, grad, gate, up, down, step):
    sources, block, width = rows.shape
    units = gate.shape[1]
    total = sources * block
    wide = pl.BlockSpec((block, width), lambda i: (i, 0))
    narrow = pl.BlockSpec((block, units), lambda i: (i, 0))

    def whole(shape):
        return pl.BlockSpec(shape, lambda i: (0, 0), pipeline_mode=pl.Buffered(1))

    low = jax.ShapeDtypeStruct((total, units), jnp.bfloat16)
    full = jax.ShapeDtypeStruct((total, width), jnp.bfloat16)
    return pl.pallas_call(
        expert_kernel,
        grid=(sources,),
        in_specs=[
            pl.BlockSpec((None, block, width), lambda i: (i, 0, 0)),
            pl.BlockSpec((None, None, block, width), lambda i: (i, step, 0, 0)),
            whole(gate.shape),
            whole(up.shape),
            whole(down.shape),
        ],
        out_specs=(narrow, narrow, narrow, wide, wide, pl.BlockSpec((block, 1), lambda i: (i, 0))),
        out_shape=(low, low, low, full, full, jax.ShapeDtypeStruct((total, 1), jnp.float32)),
        compiler_params=pltpu.CompilerParams(vmem_limit_bytes=VMEM_BYTES),
        cost_estimate=SMALL,
    )(rows, grad, gate, up, down)


def plane_tables(routes_all, weights_all, first, planned):
    hit = routes_all[..., None] == first + jnp.arange(planned, dtype=jnp.int32)
    named = jnp.any(hit, -2)
    weight = jnp.sum(jnp.where(hit, weights_all[..., None], 0.0), -2)
    rows = routes_all.shape[-2]
    earlier = (
        jnp.arange(rows, dtype=jnp.int32)[:, None] > jnp.arange(rows, dtype=jnp.int32)[None, :]
    ).astype(jnp.bfloat16)
    rank = jnp.einsum(
        "tu,cuj->ctj", earlier, named.astype(jnp.bfloat16), preferred_element_type=jnp.float32
    ).astype(jnp.int32)
    place = jnp.where(named, rank, -1)
    return place.transpose(0, 2, 1), weight.transpose(0, 2, 1)


def pick_kernel(planes, place_ref, weight_ref, rows_ref, out_ref, weighted):
    capacity = out_ref.shape[2]
    local = rows_ref.shape[0]
    slots = lax.broadcasted_iota(jnp.int32, (capacity, local), 0)
    if capacity % 16 == 0:
        chosen = [place_ref[0, 0, j : j + 1, :] == slots for j in range(planes)]
        picked = jnp.dot(
            jnp.concatenate([jnp.where(c, 1.0, 0.0).astype(jnp.bfloat16) for c in chosen], 0),
            rows_ref[...],
            preferred_element_type=jnp.float32,
        )
        for j in range(planes):
            rows = picked[j * capacity : (j + 1) * capacity]
            if weighted:
                rows = rows * jnp.sum(
                    jnp.where(chosen[j], weight_ref[0, 0, j : j + 1, :], 0.0), -1, keepdims=True
                )
            out_ref[j, 0] = rows.astype(jnp.bfloat16)
        return
    for j in range(planes):
        chosen = place_ref[0, 0, j : j + 1, :] == slots
        picked = jnp.dot(
            jnp.where(chosen, 1.0, 0.0).astype(jnp.bfloat16),
            rows_ref[...],
            preferred_element_type=jnp.float32,
        )
        if weighted:
            picked = picked * jnp.sum(
                jnp.where(chosen, weight_ref[0, 0, j : j + 1, :], 0.0), -1, keepdims=True
            )
        out_ref[j, 0] = picked.astype(jnp.bfloat16)


def pick_rows(place, weight, blocks, capacity, weighted):
    count, planned, local = place.shape
    width = blocks.shape[1]
    part = 4 if planned % 4 == 0 else planned
    shape = (count, planned // part, part, local)
    return pl.pallas_call(
        functools.partial(pick_kernel, part, weighted=weighted),
        grid=(count, planned // part),
        in_specs=[
            pl.BlockSpec((1, 1, part, local), lambda c, g: (c, g, 0, 0)),
            pl.BlockSpec((1, 1, part, local), lambda c, g: (c, g, 0, 0)),
            pl.BlockSpec((local, width), lambda c, g: (c, 0)),
        ],
        out_specs=pl.BlockSpec((part, 1, capacity, width), lambda c, g: (g, c, 0, 0)),
        out_shape=jax.ShapeDtypeStruct((planned, count, capacity, width), jnp.bfloat16),
        compiler_params=pltpu.CompilerParams(vmem_limit_bytes=VMEM_BYTES),
        cost_estimate=SMALL,
    )(place.reshape(shape), weight.reshape(shape), blocks)


def weight_kernel(steps, micro, *refs):
    rows, (grads_ref,) = refs[:micro], refs[micro : micro + 1]
    actives, gates, ups = (refs[micro * i + 1 : micro * i + 1 + micro] for i in (1, 2, 3))
    outs = refs[4 * micro + 1 : 4 * micro + 4]
    sums, sem = refs[4 * micro + 4 : 4 * micro + 7], refs[-1]
    step = pl.program_id(0)

    def flat(ref):
        count, block, width = ref.shape
        return ref[...].reshape(count * block, width)

    def add(which, fresh):
        x = flat(rows[which])
        for sum_ref, left, right in (
            (sums[0], x, gates[which][...]),
            (sums[1], x, ups[which][...]),
            (sums[2], actives[which][...], flat(grads_ref)),
        ):
            term = lax.dot_general(
                left, right, (((0,), (0,)), ((), ())), preferred_element_type=jnp.float32
            )
            if fresh:
                sum_ref[0] = term
            else:
                sum_ref[0] += term

    pl.when(step == 0)(lambda: add(0, True))
    pl.when((step > 0) & (step < steps))(lambda: add(0, False))
    for which in range(1, micro):
        pl.when((step >= which * steps) & (step < (which + 1) * steps))(
            functools.partial(add, which, False)
        )

    @pl.when(step == micro * steps - 1)
    def _():
        copies = [pltpu.make_async_copy(sums[i], outs[i], sem.at[i]) for i in range(3)]
        for copy in copies:
            copy.start()
        for copy in copies:
            copy.wait()


def expert_weight_grads(rows, grads, actives, gates, ups):
    sources, micro, block, width = grads.shape
    units = gates[0].shape[1]
    steps = sources // 2

    def turn(i, which):
        return jnp.clip(i - which * steps, 0, steps - 1)

    def specs(size):
        return [
            pl.BlockSpec((2 * block, size), functools.partial(lambda w, i: (turn(i, w), 0), which))
            for which in range(micro)
        ]

    def row_specs():
        return [
            pl.BlockSpec(
                (2, block, width), functools.partial(lambda w, i: (turn(i, w), 0, 0), which)
            )
            for which in range(micro)
        ]

    shapes = [(1, width, units), (1, width, units), (1, units, width)]
    return pl.pallas_call(
        functools.partial(weight_kernel, steps, micro),
        grid=(micro * steps,),
        in_specs=row_specs()
        + [
            pl.BlockSpec(
                (2, None, block, width), lambda i: (lax.rem(i, steps), lax.div(i, steps), 0, 0)
            )
        ]
        + specs(units) * 3,
        out_specs=[pl.BlockSpec(memory_space=pl.ANY)] * 3,
        out_shape=[jax.ShapeDtypeStruct(shape, jnp.float32) for shape in shapes],
        scratch_shapes=[pltpu.VMEM(shape, jnp.float32) for shape in shapes]
        + [pltpu.SemaphoreType.DMA((3,))],
        compiler_params=pltpu.CompilerParams(vmem_limit_bytes=VMEM_BYTES),
        cost_estimate=SMALL,
    )(*rows, grads, *actives, *gates, *ups)


def fill_mask(place_ref, mask_ref):
    base, bound = place_ref[0], place_ref[1]
    keys, rows = mask_ref.shape
    key_at = lax.broadcasted_iota(jnp.int32, (keys, rows), 0)
    row_at = lax.broadcasted_iota(jnp.int32, (keys, rows), 1) + base
    least = jnp.where(row_at >= bound, bound, 0)
    mask_ref[...] = jnp.where((key_at <= row_at) & (key_at >= least), 0.0, MASKED)


def head_queries(raw, gain, cosine, sine):
    scale = lax.rsqrt(jnp.mean(raw * raw, -1, keepdims=True) + EPSILON)
    value = raw * scale * gain
    turned = value * cosine + pltpu.roll(value, value.shape[-1] // 2, 1) * sine
    return turned.astype(jnp.bfloat16), scale


def across(a, b):
    return lax.dot_general(a, b, (((1,), (1,)), ((), ())), preferred_element_type=jnp.float32)


def along(a, b):
    return jnp.dot(a, b, preferred_element_type=jnp.float32)


def keyed(both_ref, width, which):
    count, rows = both_ref.shape[:2]
    return both_ref[:, :, which * width : (which + 1) * width].reshape(count * rows, width)


def attend_kernel(
    per, factor, place_ref, raw_ref, both_ref, gain_ref, cos_ref, sin_ref, *rest
):
    out_ref, mask_ref, turned_ref = rest[-3:]
    width = gain_ref.shape[1]
    group_step, step = pl.program_id(0), pl.program_id(1)

    @pl.when((group_step == 0) & (step == 0))
    def _():
        fill_mask(place_ref, mask_ref)

    @pl.when(step == 0)
    def _():
        turned_ref[...] = keyed(both_ref, width, 1).T

    for head in range(per):
        columns = slice(head * width, (head + 1) * width)
        queries, _ = head_queries(raw_ref[:, columns], gain_ref[...], cos_ref[...], sin_ref[...])
        chances = jnp.exp2(across(keyed(both_ref, width, 0), queries) * factor + mask_ref[...])
        total = jnp.sum(chances, 0, keepdims=True)
        result = along(turned_ref[...], chances.astype(jnp.bfloat16)) * (1.0 / total)
        out_ref[:, columns] = result.T.astype(jnp.bfloat16)


class Exchange:
    def __init__(self, axis, rows_ref, out_ref, send_sem, recv_sem, own_sem):
        self.axis, self.count = axis, rows_ref.shape[0]
        self.rows_ref, self.out_ref = rows_ref, out_ref
        self.send_sem, self.recv_sem, self.own_sem = send_sem, recv_sem, own_sem
        self.me = lax.axis_index(axis)

    @staticmethod
    def scratch(count):
        return [
            pltpu.SemaphoreType.DMA((count,)),
            pltpu.SemaphoreType.DMA((count,)),
            pltpu.SemaphoreType.DMA,
        ]

    def passing(self, k, part):
        return pltpu.make_async_remote_copy(
            src_ref=self.rows_ref.at[lax.rem(self.me + k, self.count)],
            dst_ref=self.out_ref.at[part],
            send_sem=self.send_sem.at[k],
            recv_sem=self.recv_sem.at[k],
            device_id={self.axis: lax.rem(self.me + k, self.count)},
            device_id_type=pl.DeviceIdType.MESH,
        )

    def kept(self):
        return pltpu.make_async_copy(
            self.rows_ref.at[self.me], self.out_ref.at[self.me], self.own_sem
        )

    def begin(self):
        for k in range(1, self.count):
            self.passing(k, self.me).start()
        self.kept().start()

    def finish(self):
        self.kept().wait()
        for k in range(1, self.count):
            self.passing(k, lax.rem(self.me + self.count - k, self.count)).wait_recv()
        for k in range(1, self.count):
            self.passing(k, self.me).wait_send()


def greet(**counts):
    barrier = pltpu.get_barrier_semaphore()
    for axis, count in counts.items():
        me = lax.axis_index(axis)
        for k in range(1, count):
            pl.semaphore_signal(
                barrier,
                inc=1,
                device_id={axis: lax.rem(me + k, count)},
                device_id_type=pl.DeviceIdType.MESH,
            )
    pl.semaphore_wait(barrier, sum(counts.values()) - len(counts))


class RowExchange:
    def __init__(self, ring, held_ref, out_ref, send_sem, recv_sem, own_sem):
        self.ring, self.held_ref, self.out_ref = ring, held_ref, out_ref
        self.send_sem, self.recv_sem, self.own_sem = send_sem, recv_sem, own_sem
        self.me = lax.axis_index("ctx")
        self.rows = out_ref.shape[2]

    @staticmethod
    def scratch(ring, groups):
        return [
            pltpu.SemaphoreType.DMA((groups, ring)),
            pltpu.SemaphoreType.DMA((groups, ring)),
            pltpu.SemaphoreType.DMA((groups,)),
        ]

    def held(self, group, at):
        return self.held_ref.at[group, pl.ds(at * self.rows, self.rows)]

    def passing(self, group, k, part):
        to = lax.rem(self.me + k, self.ring)
        return pltpu.make_async_remote_copy(
            src_ref=self.held(group, to),
            dst_ref=self.out_ref.at[part, group],
            send_sem=self.send_sem.at[group, k],
            recv_sem=self.recv_sem.at[group, k],
            device_id={"ctx": to},
            device_id_type=pl.DeviceIdType.MESH,
        )

    def kept(self, group):
        return pltpu.make_async_copy(
            self.held(group, self.me), self.out_ref.at[self.me, group], self.own_sem.at[group]
        )

    def begin(self, group):
        for k in range(1, self.ring):
            self.passing(group, k, self.me).start()
        self.kept(group).start()

    def finish(self):
        for group in range(self.out_ref.shape[1]):
            self.kept(group).wait()
            for k in range(1, self.ring):
                self.passing(group, k, lax.rem(self.me + self.ring - k, self.ring)).wait_recv()
            for k in range(1, self.ring):
                self.passing(group, k, self.me).wait_send()


def attend_back_kernel(
    per,
    steps,
    factor,
    scale,
    count,
    ring,
    extra_axis,
    place_ref,
    raw_ref,
    branch_ref,
    weight_ref,
    both_ref,
    pair_raw_ref,
    gain_ref,
    key_gain_ref,
    cos_ref,
    sin_ref,
    rows_ref,
    extra_ref,
    raw_grad_ref,
    pair_grad_ref,
    gain_grad_ref,
    moved_ref,
    extra_moved_ref,
    mask_ref,
    turned_ref,
    sums_ref,
    held_ref,
    landed_ref,
    *sems,
):
    width = gain_ref.shape[1]
    group_step, step = pl.program_id(0), pl.program_id(1)
    moving = Exchange("exp", rows_ref, moved_ref, *sems[:3])
    extra_moving = Exchange(extra_axis, extra_ref, extra_moved_ref, *sems[3:6])
    landing = RowExchange(ring, held_ref, landed_ref, *sems[6:])

    @pl.when((group_step == 0) & (step == 0))
    def _():
        greet(exp=count, ctx=ring)
        moving.begin()
        extra_moving.begin()
        fill_mask(place_ref, mask_ref)
        gain_grad_ref[...] = jnp.zeros_like(gain_grad_ref)

    @pl.when(step == 0)
    def _():
        turned_ref[...] = keyed(both_ref, width, 0).T
        sums_ref[...] = jnp.zeros_like(sums_ref)

    def turned_back(grad, raw, norm, gain, row):
        back = grad * cos_ref[...] - pltpu.roll(grad, width // 2, 1) * sin_ref[...]
        inner = back * gain
        gain_grad_ref[row : row + 1, :] += jnp.sum(back * raw * norm, 0, keepdims=True)
        return (
            norm * inner - raw * (norm * norm * norm) * jnp.mean(inner * raw, -1, keepdims=True)
        ).astype(jnp.bfloat16)

    grads = across(branch_ref[...], weight_ref[...]).astype(jnp.bfloat16)
    for head in range(per):
        columns = slice(head * width, (head + 1) * width)
        raw = raw_ref[:, columns]
        queries, norm = head_queries(raw, gain_ref[...], cos_ref[...], sin_ref[...])
        grad = grads[:, columns]
        chances = jnp.exp2(across(keyed(both_ref, width, 0), queries) * factor + mask_ref[...])
        chances = chances * (1.0 / jnp.sum(chances, 0, keepdims=True))
        chance_grad = across(keyed(both_ref, width, 1), grad)
        mean = jnp.sum(chances * chance_grad, 0, keepdims=True)
        score_grad = (chances * (chance_grad - mean)).astype(jnp.bfloat16)
        sums_ref[:, :width] += along(score_grad, queries)
        sums_ref[:, width:] += along(chances.astype(jnp.bfloat16), grad)
        query_grad = (along(turned_ref[...], score_grad) * scale).astype(jnp.bfloat16)
        raw_grad_ref[:, columns] = turned_back(
            query_grad.astype(jnp.float32).T, raw, norm, gain_ref[...], 0
        )

    @pl.when(step == steps - 1)
    def _():
        held_ref[group_step, :, :width] = (sums_ref[:, :width] * scale).astype(jnp.bfloat16)
        held_ref[group_step, :, width:] = sums_ref[:, width:].astype(jnp.bfloat16)
        landing.begin(group_step)

    @pl.when((group_step == pl.num_programs(0) - 1) & (step == steps - 1))
    def _():
        landing.finish()
        for group in range(landed_ref.shape[1]):
            total = landed_ref[0, group].astype(jnp.float32)
            for other in range(1, ring):
                total += landed_ref[other, group].astype(jnp.float32)
            total = total.astype(jnp.bfloat16)
            start = 2 * group * width
            raw = pair_raw_ref[:, start : start + width]
            norm = lax.rsqrt(jnp.mean(raw * raw, -1, keepdims=True) + EPSILON)
            pair_grad_ref[:, start : start + width] = turned_back(
                total[:, :width].astype(jnp.float32), raw, norm, key_gain_ref[...], 1
            )
            pair_grad_ref[:, start + width : start + 2 * width] = total[:, width:]
        extra_moving.finish()
        moving.finish()


def attention_specs(raw, both, width, rows, step, per):
    kv_heads = both.shape[2] // (2 * width)
    heads = raw.shape[1] // width - 2 * kv_heads
    steps = heads // kv_heads // per
    count = both.shape[0]
    keys = count * rows
    wide = pl.BlockSpec((rows, per * width), lambda g, j: (0, g * steps + j))
    specs = dict(
        place=pl.BlockSpec(memory_space=pltpu.SMEM),
        raw=pl.BlockSpec((rows, per * width), lambda g, j: (step, g * steps + j)),
        heads=wide,
        both=pl.BlockSpec((count, rows, 2 * width), lambda g, j: (0, 0, g)),
        gain=pl.BlockSpec((1, width), lambda g, j: (0, 0)),
        table=pl.BlockSpec((rows, width), lambda g, j: (0, 0)),
    )
    params = pltpu.CompilerParams(vmem_limit_bytes=VMEM_BYTES)
    work = 2 * heads * rows * keys * width
    return kv_heads, heads, steps, keys, specs, params, work


def attend(raw, both, gain, cosine, sine, place, step, waits, per=2):
    rows, width = cosine.shape
    kv_heads, heads, steps, keys, specs, params, work = attention_specs(
        raw, both, width, rows, step, per
    )
    return pl.pallas_call(
        functools.partial(attend_kernel, per, width ** (-0.5) * math.log2(math.e)),
        grid=(kv_heads, steps),
        in_specs=[specs[k] for k in ("place", "raw", "both", "gain", "table", "table")]
        + [pl.BlockSpec(memory_space=pl.ANY)] * len(waits),
        out_specs=specs["heads"],
        out_shape=jax.ShapeDtypeStruct((rows, heads * width), jnp.bfloat16),
        scratch_shapes=[
            pltpu.VMEM((keys, rows), jnp.float32),
            pltpu.VMEM((width, keys), jnp.bfloat16),
        ],
        compiler_params=params,
        cost_estimate=SMALL,
    )(place, raw, both, gain, cosine, sine, *waits)


def attend_back(
    raw,
    branch,
    weight,
    both,
    gain,
    key_gain,
    cosine,
    sine,
    place,
    step,
    rows_out,
    extra,
    extra_axis,
    per=2,
):
    rows, width = cosine.shape
    kv_heads, heads, steps, keys, specs, params, work = attention_specs(
        raw, both, width, rows, step, per
    )
    count, ring = rows_out.shape[0], both.shape[0]
    anywhere = pl.BlockSpec(memory_space=pl.ANY)
    pairs = 2 * kv_heads * width
    pair_place = heads * width // pairs
    return pl.pallas_call(
        functools.partial(
            attend_back_kernel,
            per,
            steps,
            width ** (-0.5) * math.log2(math.e),
            width ** (-0.5),
            count,
            ring,
            extra_axis,
        ),
        grid=(kv_heads, steps),
        in_specs=[
            specs["place"],
            specs["raw"],
            pl.BlockSpec(branch.shape, lambda g, j: (0, 0)),
            pl.BlockSpec((per * width, weight.shape[1]), lambda g, j: (g * steps + j, 0)),
            specs["both"],
            pl.BlockSpec((rows, pairs), lambda g, j: (step, pair_place)),
            specs["gain"],
            specs["gain"],
            specs["table"],
            specs["table"],
            anywhere,
            anywhere,
        ],
        out_specs=(
            specs["heads"],
            pl.BlockSpec((rows, pairs), lambda g, j: (0, 0)),
            pl.BlockSpec((8, width), lambda g, j: (0, 0)),
            anywhere,
            anywhere,
        ),
        out_shape=(
            jax.ShapeDtypeStruct((rows, heads * width), jnp.bfloat16),
            jax.ShapeDtypeStruct((rows, pairs), jnp.bfloat16),
            jax.ShapeDtypeStruct((8, width), jnp.float32),
            jax.ShapeDtypeStruct(rows_out.shape, rows_out.dtype),
            jax.ShapeDtypeStruct(extra.shape, extra.dtype),
        ),
        scratch_shapes=[
            pltpu.VMEM((keys, rows), jnp.float32),
            pltpu.VMEM((width, keys), jnp.bfloat16),
            pltpu.VMEM((keys, 2 * width), jnp.float32),
            pltpu.VMEM((kv_heads, keys, 2 * width), jnp.bfloat16),
            pltpu.VMEM((ring, kv_heads, rows, 2 * width), jnp.bfloat16),
        ]
        + Exchange.scratch(count)
        + Exchange.scratch(extra.shape[0])
        + RowExchange.scratch(ring, kv_heads),
        compiler_params=pltpu.CompilerParams(
            vmem_limit_bytes=VMEM_BYTES, collective_id=1 + step, has_side_effects=True
        ),
        cost_estimate=SMALL,
    )(
        place,
        raw,
        branch,
        weight,
        both,
        raw,
        gain,
        key_gain,
        cosine,
        sine,
        rows_out,
        extra,
    )


def combine_kernel(place_ref, weight_ref, back_ref, out_ref, *, weighted):
    experts, _, capacity, width = back_ref.shape
    local = out_ref.shape[0]
    slots = lax.broadcasted_iota(jnp.int32, (capacity, local), 0)
    factors = []
    for j in range(experts):
        value = weight_ref[0, j : j + 1, :] if weighted else 1.0
        chosen = place_ref[0, j : j + 1, :] == slots
        factors.append(jnp.where(chosen, value, 0.0).astype(jnp.bfloat16))
    out_ref[...] = lax.dot_general(
        jnp.concatenate(factors, 0),
        back_ref[...].reshape(experts * capacity, width),
        (((0,), (0,)), ((), ())),
        preferred_element_type=jnp.float32,
    ).astype(jnp.bfloat16)


def combine_rows(place, weight, back, weighted):
    count, planned, local = place.shape
    capacity, width = back.shape[2:]
    return pl.pallas_call(
        functools.partial(combine_kernel, weighted=weighted),
        grid=(count,),
        in_specs=[
            pl.BlockSpec((1, planned, local), lambda c: (c, 0, 0)),
            pl.BlockSpec((1, planned, local), lambda c: (c, 0, 0)),
            pl.BlockSpec((planned, 1, capacity, width), lambda c: (0, c, 0, 0)),
        ],
        out_specs=pl.BlockSpec((local, width), lambda c: (c, 0)),
        out_shape=jax.ShapeDtypeStruct((count * local, width), jnp.bfloat16),
        compiler_params=pltpu.CompilerParams(vmem_limit_bytes=VMEM_BYTES),
        cost_estimate=SMALL,
    )(place, weight, back)


class GradSums:
    def __init__(self, ring, micro, head_dim, sizes, refs):
        self.ring, self.micro, self.sizes = ring, micro, sizes
        self.head_dim = head_dim
        self.attended, self.hidden = refs[:micro], refs[micro]
        refs = refs[micro + 1 :]
        self.branch, self.query, self.pair = (
            refs[i * micro : (i + 1) * micro] for i in range(3)
        )
        self.weight = refs[3 * micro]
        self.out = refs[3 * micro + 1 : 3 * micro + 5]
        self.hidden_grad = refs[3 * micro + 5]
        self.far = refs[3 * micro + 6 : 3 * micro + 9]
        scratch = refs[3 * micro + 9 :]
        self.left_v, self.right_v = scratch[:2], scratch[2:4]
        self.part, self.first, self.second, self.last = (
            scratch[4 + 2 * i : 6 + 2 * i] for i in range(4)
        )
        (
            self.left_sem,
            self.far_sem,
            self.load_sem,
            self.first_sem,
            self.second_sem,
            self.last_sem,
            self.weight_sem,
        ) = scratch[12:]
        e = lax.axis_index("exp")
        self.core, self.y, self.x = lax.rem(e, 2), lax.div(e, 4), lax.rem(lax.div(e, 2), 2)
        self.partner = e + 1 - 2 * self.core
        self.across_x, self.across_y = e + 2 - 4 * self.x, e + 4 - 8 * self.y
        self.z = lax.axis_index("ctx")
        self.order = [
            (kind, chunk) for kind, size in enumerate(sizes) for chunk in range(size[2] // size[3])
        ]

    @staticmethod
    def scratch(ring, micro, sizes):
        chunks = [size[2] // size[3] for size in sizes]
        total = sum(chunks)
        shapes = [pltpu.VMEM((4, size[0], size[1]), jnp.bfloat16) for size in sizes]
        shapes += [pltpu.VMEM((2, size[0], size[3]), jnp.bfloat16) for size in sizes]
        for lead, share in (((4,), 1), ((2,), 1), ((), 1), ((ring,), ring)):
            for size, count in zip(sizes, chunks):
                shapes.append(
                    pltpu.VMEM((count,) + lead + (size[1] // share, size[3]), jnp.bfloat16)
                )
        shapes += [
            pltpu.SemaphoreType.DMA((3, micro + 1, 4, ring)),
            pltpu.SemaphoreType.DMA((2, 3, micro)),
            pltpu.SemaphoreType.DMA((total, 2, micro)),
            pltpu.SemaphoreType.DMA((2, total, 2)),
            pltpu.SemaphoreType.DMA((2, total)),
            pltpu.SemaphoreType.DMA((2, total, ring)),
            pltpu.SemaphoreType.DMA((4,)),
        ]
        return shapes

    def weight_loads(self, chunk):
        _, high, wide = self.left_v[0].shape
        return [
            pltpu.make_async_copy(
                self.weight.at[pl.ds(r * high, high), pl.ds(chunk * wide, wide)],
                self.left_v[0].at[2 * (chunk % 2) + r],
                self.weight_sem.at[2 * (chunk % 2) + r],
            )
            for r in (0, 1)
        ]

    def add_hidden(self, chunk):
        high = self.left_v[0].shape[1]
        half = self.sizes[1][0] // 2
        for copy in self.weight_loads(chunk):
            copy.wait()
        for r in (0, 1):
            columns = slice(r * high, (r + 1) * high)
            term = across(
                self.right_v[1][chunk % 2, :half], self.left_v[0][2 * (chunk % 2) + r]
            )
            if chunk == 0:
                self.hidden_grad[:, columns] = term
            else:
                self.hidden_grad[:, columns] += term

    def to_partner(self, src, dst, send_sem, recv_sem):
        return pltpu.make_async_remote_copy(
            src_ref=src,
            dst_ref=dst,
            send_sem=send_sem,
            recv_sem=recv_sem,
            device_id={"exp": self.partner},
            device_id_type=pl.DeviceIdType.MESH,
        )

    def left_copies(self, kind):
        half = self.sizes[kind][0] // 2
        own, sent = [], []
        if kind == 1:
            place = (self.micro, 0, 0)
            own.append(
                pltpu.make_async_copy(
                    self.hidden.at[self.core],
                    self.left_v[1].at[:, pl.ds(0, half)],
                    self.left_sem.at[(0,) + place],
                )
            )
            sent.append(
                self.to_partner(
                    self.hidden.at[1 - self.core],
                    self.left_v[1].at[:, pl.ds(half, half)],
                    self.left_sem.at[(1,) + place],
                    self.left_sem.at[(2,) + place],
                )
            )
            return own, sent
        share = self.sizes[kind][1] // self.ring
        rows = half // self.micro
        for m in range(self.micro):
            for piece in range(4):
                for c in range(self.ring):

                    def columns(core):
                        block = c * 8 + piece * 2 + core
                        return self.attended[m].at[
                            :, pl.ds(pl.multiple_of(block * share, share), share)
                        ]

                    def place(base):
                        return self.left_v[0].at[
                            piece, pl.ds(base + m * rows, rows), pl.ds(c * share, share)
                        ]

                    own.append(
                        pltpu.make_async_copy(
                            columns(self.core), place(0), self.left_sem.at[0, m, piece, c]
                        )
                    )
                    sent.append(
                        self.to_partner(
                            columns(1 - self.core),
                            place(half),
                            self.left_sem.at[1, m, piece, c],
                            self.left_sem.at[2, m, piece, c],
                        )
                    )
        return own, sent

    def right_copies(self, which):
        near = (self.branch, self.query, self.pair)[which]
        return [
            self.to_partner(
                near[m],
                self.far[which].at[m],
                self.far_sem.at[0, which, m],
                self.far_sem.at[1, which, m],
            )
            for m in range(self.micro)
        ]

    def source(self, i):
        kind, chunk = self.order[i]
        wide = self.sizes[kind][3]
        if kind == 0:
            return 0, chunk * wide
        query_width = self.query[0].shape[1]
        if chunk * wide < query_width:
            return 1, chunk * wide
        return 2, chunk * wide - query_width

    def loads(self, i, far):
        kind, chunk = self.order[i]
        which, start = self.source(i)
        wide = self.sizes[kind][3]
        half = self.sizes[kind][0] // 2
        rows = half // self.micro
        near = (self.branch, self.query, self.pair)[which]
        return [
            pltpu.make_async_copy(
                (self.far[which].at[m] if far else near[m]).at[:, pl.ds(start, wide)],
                self.right_v[kind].at[chunk % 2, pl.ds(far * half + m * rows, rows)],
                self.load_sem.at[i, far, m],
            )
            for m in range(self.micro)
        ]

    def start_loads(self, i):
        which, start = self.source(i)
        for copy in self.loads(i, 0):
            copy.start()
        if start == 0:
            for copy in self.right_copies(which):
                copy.wait_recv()
        for copy in self.loads(i, 1):
            copy.start()

    def x_first(self, i):
        return i % 2 == 0

    def step_first(self, i, k):
        kind, chunk = self.order[i]
        if self.x_first(i):
            piece, to = 2 * k + 1 - self.x, self.across_x
        else:
            piece, to = 2 * (1 - self.y) + k, self.across_y
        return pltpu.make_async_remote_copy(
            src_ref=self.part[kind].at[chunk, piece],
            dst_ref=self.first[kind].at[chunk, k],
            send_sem=self.first_sem.at[0, i, k],
            recv_sem=self.first_sem.at[1, i, k],
            device_id={"exp": to},
            device_id_type=pl.DeviceIdType.MESH,
        )

    def step_second(self, i):
        kind, chunk = self.order[i]
        if self.x_first(i):
            piece, to = 2 * (1 - self.y) + self.x, self.across_y
        else:
            piece, to = 2 * self.y + 1 - self.x, self.across_x
        return pltpu.make_async_remote_copy(
            src_ref=self.part[kind].at[chunk, piece],
            dst_ref=self.second[kind].at[chunk],
            send_sem=self.second_sem.at[0, i],
            recv_sem=self.second_sem.at[1, i],
            device_id={"exp": to},
            device_id_type=pl.DeviceIdType.MESH,
        )

    def mine(self, i):
        kind, chunk = self.order[i]
        return self.part[kind].at[chunk, 2 * self.y + self.x]

    def step_last(self, i, k, slot):
        kind, chunk = self.order[i]
        to = lax.rem(self.z + k, self.ring)
        rows = self.sizes[kind][1] // self.ring
        return pltpu.make_async_remote_copy(
            src_ref=self.mine(i).at[pl.ds(to * rows, rows)],
            dst_ref=self.last[kind].at[chunk, slot],
            send_sem=self.last_sem.at[0, i, k],
            recv_sem=self.last_sem.at[1, i, k],
            device_id={"ctx": to},
            device_id_type=pl.DeviceIdType.MESH,
        )

    def multiply(self, i):
        kind, chunk = self.order[i]
        for far in (0, 1):
            for copy in self.loads(i, far):
                copy.wait()

        def piece(p, carry):
            term = lax.dot_general(
                self.left_v[kind][p],
                self.right_v[kind][chunk % 2],
                (((0,), (0,)), ((), ())),
                preferred_element_type=jnp.float32,
            )
            self.part[kind][chunk, p] = term.astype(jnp.bfloat16)
            return carry

        lax.fori_loop(0, 4, piece, 0)
        for k in range(2):
            self.step_first(i, k).start()

    def add_first(self, i):
        kind, chunk = self.order[i]
        for k in range(2):
            self.step_first(i, k).wait_recv()
        for k in range(2):
            piece = 2 * k + self.x if self.x_first(i) else 2 * self.y + k
            self.part[kind][chunk, piece] = (
                self.part[kind][chunk, piece].astype(jnp.float32)
                + self.first[kind][chunk, k].astype(jnp.float32)
            ).astype(jnp.bfloat16)
        self.step_second(i).start()

    def add_second(self, i):
        kind, chunk = self.order[i]
        self.step_second(i).wait_recv()
        piece = 2 * self.y + self.x
        self.part[kind][chunk, piece] = (
            self.part[kind][chunk, piece].astype(jnp.float32)
            + self.second[kind][chunk].astype(jnp.float32)
        ).astype(jnp.bfloat16)
        for k in range(1, self.ring):
            self.step_last(i, k, k).start()

    def add_last(self, i):
        kind, chunk = self.order[i]
        rows, wide = self.sizes[kind][1] // self.ring, self.sizes[kind][3]
        for k in range(1, self.ring):
            self.step_last(i, k, k).wait_recv()
        total = self.part[kind][
            chunk, 2 * self.y + self.x, pl.ds(pl.multiple_of(self.z * rows, rows), rows), :
        ].astype(jnp.float32)
        for k in range(1, self.ring):
            total += self.last[kind][chunk, k].astype(jnp.float32)
        which, start = self.source(i)
        if which < 2:
            self.out[which][:, start : start + wide] = total
            return
        half = self.head_dim
        for at in range(0, wide, 2 * half):
            to = (start + at) // 2
            self.out[2][:, to : to + half] = total[:, at : at + half]
            self.out[3][:, to : to + half] = total[:, at + half : at + 2 * half]

    def run(self):
        chunks = len(self.order)
        barrier = pltpu.get_barrier_semaphore()
        for other in (self.partner, self.across_x, self.across_y):
            pl.semaphore_signal(
                barrier, inc=1, device_id={"exp": other}, device_id_type=pl.DeviceIdType.MESH
            )
        for k in range(1, self.ring):
            pl.semaphore_signal(
                barrier,
                inc=1,
                device_id={"ctx": lax.rem(self.z + k, self.ring)},
                device_id_type=pl.DeviceIdType.MESH,
            )
        pl.semaphore_wait(barrier, self.ring + 2)
        lefts = [self.left_copies(kind) for kind in (0, 1)]
        rights = [self.right_copies(which) for which in range(3)]
        for copies in (rights[0], lefts[0][1], lefts[0][0]):
            for copy in copies:
                copy.start()
        self.start_loads(0)
        for i in range(chunks + LAGS[-1]):
            if i < chunks:
                if i + 1 < chunks:
                    self.start_loads(i + 1)
                kind, chunk = self.order[i]
                if chunk == 0:
                    for copy in lefts[kind][0]:
                        copy.wait()
                    for copy in lefts[kind][1]:
                        copy.wait_recv()
                self.multiply(i)
                if i == 0:
                    for copies in (rights[1], *lefts[1], rights[2]):
                        for copy in copies:
                            copy.start()
                if kind == 0 and chunk == self.sizes[0][2] // self.sizes[0][3] - 1:
                    for copy in self.weight_loads(0):
                        copy.start()
                if kind == 1:
                    if i + 1 < chunks:
                        for copy in self.weight_loads(chunk + 1):
                            copy.start()
                    self.add_hidden(chunk)
            for lag, stage in zip(LAGS, (self.add_first, self.add_second, self.add_last)):
                if 0 <= i - lag < chunks:
                    stage(i - lag)
        for copies in (lefts[0][1], lefts[1][1], *rights):
            for copy in copies:
                copy.wait_send()
        for i in range(chunks):
            for k in range(2):
                self.step_first(i, k).wait_send()
            self.step_second(i).wait_send()
            for k in range(1, self.ring):
                self.step_last(i, k, k).wait_send()


def grad_sums_kernel(ring, micro, head_dim, sizes, *refs):
    GradSums(ring, micro, head_dim, sizes, refs).run()


def grad_sums(ring, head_dim, attended, hidden, branch, query, pair, weight, number):
    micro, rows = len(attended), attended[0].shape[0]
    tokens = 2 * micro * rows
    sizes = [
        (tokens, attended[0].shape[1] // 8, branch[0].shape[1], 256),
        (tokens, hidden.shape[3], query[0].shape[1] + pair[0].shape[1], 512),
    ]
    anywhere = pl.BlockSpec(memory_space=pl.ANY)
    assert weight.shape[0] == 2 * tokens and sizes[1][3] == sizes[0][1]
    share = sizes[1][1] // ring
    outs = [
        jax.ShapeDtypeStruct(shape, jnp.float32)
        for shape in (
            (sizes[0][1] // ring, sizes[0][2]),
            (share, query[0].shape[1]),
            (share, pair[0].shape[1] // 2),
            (share, pair[0].shape[1] // 2),
            (micro * rows, weight.shape[0]),
        )
    ]
    outs += [
        jax.ShapeDtypeStruct((micro,) + arrays[0].shape, jnp.bfloat16)
        for arrays in (branch, query, pair)
    ]
    return pl.pallas_call(
        functools.partial(grad_sums_kernel, ring, micro, head_dim, sizes),
        in_specs=[anywhere] * (4 * micro + 2),
        out_specs=[pl.BlockSpec(memory_space=pltpu.VMEM)] * 5 + [anywhere] * 3,
        out_shape=outs,
        scratch_shapes=GradSums.scratch(ring, micro, sizes),
        compiler_params=pltpu.CompilerParams(
            vmem_limit_bytes=60 * 2**20, collective_id=number, has_side_effects=True
        ),
        cost_estimate=SMALL,
    )(*attended, hidden, *branch, *query, *pair, weight)[:5]


def per_device(
    tokens,
    routes,
    route_weights,
    bounds,
    norm_attn,
    norm_ffn,
    q_gain,
    k_gain,
    w_q,
    w_k,
    w_v,
    w_o,
    w_gate,
    w_up,
    w_down,
    cotangent,
):
    micro = tokens.shape[0]
    local = tokens.shape[2]
    width = tokens.shape[3]
    head_dim = q_gain.shape[0]
    kv_heads = w_k.shape[1] // head_dim
    top = routes.shape[3]
    ring = lax.axis_size("ctx")
    plane = lax.axis_size("exp")
    assert w_gate.shape[0] == 1
    experts = ring * plane
    capacity = max(2, local * top * 5 // (4 * experts))
    seq_len = local * ring
    query_width = w_q.shape[1]
    pair_width = kv_heads * head_dim
    here = lax.axis_index("ctx")
    base = here * local
    cosine, sine = rope_tables(base + jnp.arange(local, dtype=jnp.int32), head_dim)
    gate_weight, up_weight, down_weight = w_gate[0], w_up[0], w_down[0]

    def dot(a, b):
        return jnp.dot(a, b, preferred_element_type=jnp.float32)

    def dot_t(a, b):
        return jnp.einsum("te,de->td", a, b, preferred_element_type=jnp.float32)

    def t_dot(a, b):
        return jnp.einsum("td,te->de", a, b, preferred_element_type=jnp.float32)

    def paired(keys, values):
        rows = keys.shape[0]
        return jnp.stack(
            [keys.reshape(rows, kv_heads, head_dim), values.reshape(rows, kv_heads, head_dim)], 2
        ).reshape(rows, 2 * pair_width)

    in_weight = lax.all_gather(
        jnp.concatenate([w_q, paired(w_k, w_v)], 1), "exp", axis=0, tiled=True
    )
    out_weight = lax.all_gather(w_o, "exp", axis=0, tiled=True)

    meta = jnp.concatenate([routes[:, 0].astype(jnp.float32), route_weights[:, 0]], -1)
    grads_low = [cotangent[step, 0] for step in range(micro)]
    grad_blocks, meta = line_gather(
        *grads_low, meta.reshape(-1, 128), number=0, stacked=micro
    )
    meta = meta.reshape(ring, micro, local, 2 * top)
    tables = [
        plane_tables(
            meta[:, step, :, :top].astype(jnp.int32), meta[:, step, :, top:], here * plane, plane
        )
        for step in range(micro)
    ]
    slots = jnp.arange(capacity, dtype=jnp.int32)
    chosen = [
        place.transpose(1, 0, 2)[:, :, None, :] == slots[None, None, :, None] for place, _ in tables
    ]

    def exchange(rows):
        return lax.all_to_all(rows, "exp", split_axis=0, concat_axis=0, tiled=True)

    def pick(blocks, step, weighted):
        return pick_rows(*tables[step], blocks, capacity, weighted)

    def combine(back, step, weighted):
        back = back.reshape(plane, ring, capacity, width)
        if capacity % 16 == 0:
            return combine_rows(*tables[step], back, weighted)
        factor = chosen[step]
        if weighted:
            weight = tables[step][1].transpose(1, 0, 2)
            factor = jnp.where(factor, weight[:, :, None, :], 0.0)
        part = jnp.einsum(
            "jcst,jcsd->ctd",
            factor.astype(jnp.bfloat16),
            back,
            preferred_element_type=jnp.float32,
        )
        return part.astype(jnp.bfloat16).reshape(seq_len, width)

    def scatter(part):
        return lax.psum_scatter(part, "ctx", scatter_dimension=0, tiled=True)

    picked = pick_rows(
        jnp.concatenate([place for place, _ in tables]),
        jnp.concatenate([weight for _, weight in tables]),
        grad_blocks.reshape(micro * seq_len, width),
        capacity,
        True,
    )
    incoming = exchange(picked.reshape(plane, micro * ring * capacity, width)).reshape(
        plane, micro, ring * capacity, width
    )

    rows = tokens[:, 0].astype(jnp.float32).reshape(micro * local, width)
    hidden, first_scale = norm_rows(rows, norm_attn)
    hidden = after(hidden.astype(jnp.bfloat16), picked)
    raw = dot(hidden, in_weight)
    hidden_parts = hidden.reshape(-1, ring, plane // 2, 2, width // experts)
    hidden_parts = hidden_parts.transpose(3, 2, 0, 1, 4).reshape(
        2, plane // 2, micro * local, ring * width // experts
    )
    pair_raw = raw[:, query_width:].reshape(micro * local, kv_heads, 2, head_dim)
    key_raw = pair_raw[:, :, 0]
    key_normed, key_scale = norm_rows(key_raw, k_gain)
    key_cos = jnp.tile(cosine, (micro, 1))[:, None, :]
    key_sin = jnp.tile(sine, (micro, 1))[:, None, :]
    keys = (key_normed * key_cos + swap_halves(key_normed) * key_sin).astype(jnp.bfloat16)
    pairs = jnp.stack([keys, pair_raw[:, :, 1].astype(jnp.bfloat16)], 2).reshape(
        micro * local, 2 * pair_width
    )
    gain_row = q_gain[None, :]
    both = list(line_gather(pairs[:local], number=3))
    both += [
        lax.all_gather(
            after(pairs[step * local : (step + 1) * local], both[0]), "ctx", axis=0, tiled=True
        )
        for step in range(1, micro)
    ]
    both = [gathered.reshape(ring, local, 2 * pair_width) for gathered in both]
    places, attended, middles, feeds, scales = [], [], [], [], []
    for step in range(micro):
        part = slice(step * local, (step + 1) * local)
        places.append(jnp.stack([base, bounds[step, 0]]).astype(jnp.int32))
        attended.append(
            attend(raw, both[step], gain_row, cosine, sine, places[step], step, feeds[-1:])
        )
        middles.append(rows[part] + dot(attended[step], out_weight))
        feed_in, second_scale = norm_rows(middles[step], norm_ffn)
        feeds.append(feed_in.astype(jnp.bfloat16))
        scales.append(second_scale)
    feed_blocks = [lax.all_gather(feed, "ctx", axis=0, tiled=True) for feed in feeds]

    def slotted(rows):
        return rows.reshape(plane, ring * capacity, width)

    received = []
    waits = (incoming,)
    feed_blocks[0] = after(feed_blocks[0], feeds[-1])
    for step in range(micro):
        picked = slotted(pick(feed_blocks[step], step, False))
        received.append(exchange(after(picked, *waits)))
        waits = (received[-1], hidden_parts)

    active, gate_grad, up_grad, produced, backs, pair_values = [], [], [], [], [], []
    for step in range(micro):
        parts = run_expert(received[step], incoming, gate_weight, up_weight, down_weight, step)
        for held, item in zip((active, gate_grad, up_grad, produced, backs, pair_values), parts):
            held.append(item)

    returned = []
    last = received[-1]
    for step in range(micro):
        returned.append(exchange(after(slotted(backs[step]), last)))
        last = returned[-1]
    gate_term, up_term, down_term = expert_weight_grads(
        received, incoming, active, gate_grad, up_grad
    )

    sums = jnp.stack([value.reshape(plane, ring * capacity) for value in pair_values], 1)
    sums = sums.reshape(plane, -1)
    spare = -sums.shape[1] % 1024
    extra = jnp.pad(sums, ((0, 0), (0, spare))).reshape(plane, -1, 128)

    branches, raw_grads, pair_grads = [], [], []
    middle_grads, gain_list, results = [], [], []
    waits = ()
    for step in range(micro):
        if step > 0:
            feed_grad = after(feed_grad, *waits)
        else:
            feed_grad = scatter(combine(after(returned[0], active[-1]), 0, False))
        middle_norm_grad, second_gain = norm_back(
            middles[step], scales[step], norm_ffn, feed_grad.astype(jnp.float32)
        )
        middle_grads.append(grads_low[step].astype(jnp.float32) + middle_norm_grad)
        branches.append(middle_grads[step].astype(jnp.bfloat16))
        if step == 0:
            returned[1] = after(returned[1], down_term, branches[0])
            part_sums = combine(returned[1], 1, False)
            feed_grad = scatter(part_sums)
            waits = (part_sums,)
        raw_grad, pair_grad, gain_part, result, extra = attend_back(
            raw,
            branches[step],
            out_weight,
            both[step],
            gain_row,
            k_gain[None, :],
            cosine,
            sine,
            places[step],
            step,
            after(slotted(produced[step]), *waits),
            extra,
            ("exp", "ctx")[min(step, 1)],
        )
        if step == 0:
            sums = extra.reshape(plane, -1)[:, : micro * ring * capacity]
            sums = sums.reshape(plane, micro, ring, capacity)
            values = [
                jnp.sum(jnp.where(chosen[m], sums[:, m, :, :, None], 0.0), 2) for m in range(micro)
            ]
            values = jnp.stack(values, 1).transpose(2, 1, 0, 3)
            extra = values.reshape(ring, -1, 128)
        waits = (result,)
        results.append(result)
        raw_grads.append(raw_grad)
        pair_grads.append(pair_grad)
        gain_list.append((jnp.sum(second_gain, 0), gain_part[0], gain_part[1]))
    if plane == 8:
        out_total, query_total, key_total, value_total, hidden_grad = grad_sums(
            ring, head_dim, attended, hidden_parts, branches, raw_grads, pair_grads, in_weight, 5
        )
    else:

        def sum_over_devices(left, right):
            share = left.shape[1] // experts
            left = left.reshape(-1, ring, plane, share).transpose(0, 2, 1, 3)
            term = t_dot(left.reshape(-1, experts * share), right).astype(jnp.bfloat16)
            term = lax.psum_scatter(term, "exp", scatter_dimension=0, tiled=True)
            return lax.psum_scatter(term, "ctx", scatter_dimension=0, tiled=True).astype(
                jnp.float32
            )

        out_total = sum_over_devices(jnp.concatenate(attended, 0), jnp.concatenate(branches, 0))
        raw_grad = jnp.concatenate(
            [jnp.concatenate(raw_grads, 0), jnp.concatenate(pair_grads, 0)], 1
        )
        in_total = sum_over_devices(hidden, raw_grad)
        hidden_grad = dot_t(raw_grad, in_weight)
        query_total = in_total[:, :query_width]
        pair_total = in_total[:, query_width:].reshape(-1, kv_heads, 2, head_dim)
        key_total = pair_total[:, :, 0].reshape(-1, pair_width)
        value_total = pair_total[:, :, 1].reshape(-1, pair_width)
    first_grad, first_gain = norm_back(rows, first_scale, norm_attn, hidden_grad)
    tokens_grad = jnp.concatenate(middle_grads, 0) + first_grad
    gains = jnp.concatenate([jnp.sum(first_gain, 0)] + [sum(parts) for parts in zip(*gain_list)])
    gain_total = jnp.sum(
        lax.all_to_all(
            gains.reshape(experts, -1), ("ctx", "exp"), split_axis=0, concat_axis=0, tiled=True
        ),
        0,
    )

    outputs = [
        (middles[step] + scatter(combine(results[step], step, True)).astype(jnp.float32)).astype(
            jnp.bfloat16
        )
        for step in range(micro)
    ]

    values = extra.reshape(ring, micro, plane, local).transpose(1, 3, 0, 2)
    values = values.reshape(micro, local, experts)
    match = routes[:, 0, :, :, None] == jnp.arange(experts, dtype=jnp.int32)
    route_grads = jnp.sum(jnp.where(match, values[:, :, None, :], 0.0), -1) / route_weights[:, 0]

    return (
        jnp.stack(outputs)[:, None],
        tokens_grad.reshape(micro, 1, local, width),
        route_grads[:, None],
        query_total,
        key_total,
        value_total,
        out_total,
        gain_total,
        gate_term,
        up_term,
        down_term,
    )


def solution(mesh):
    in_specs = (
        P(None, "exp", "ctx", None),
        P(None, "exp", "ctx", None),
        P(None, "exp", "ctx", None),
        P(None, "exp"),
        P(),
        P(),
        P(),
        P(),
        P("exp", None),
        P("exp", None),
        P("exp", None),
        P("exp", None),
        P(("ctx", "exp"), None, None),
        P(("ctx", "exp"), None, None),
        P(("ctx", "exp"), None, None),
        P(None, "exp", "ctx", None),
    )
    out_specs = (
        P(None, "exp", "ctx", None),
        P(None, "exp", "ctx", None),
        P(None, "exp", "ctx", None),
        P(("ctx", "exp"), None),
        P(("ctx", "exp"), None),
        P(("ctx", "exp"), None),
        P(("ctx", "exp"), None),
        P(("ctx", "exp")),
        P(("ctx", "exp"), None, None),
        P(("ctx", "exp"), None, None),
        P(("ctx", "exp"), None, None),
    )
    return jax.shard_map(
        per_device, mesh=mesh, in_specs=in_specs, out_specs=out_specs, check_vma=False
    )
```

```python
import functools
import math

import jax
import jax.numpy as jnp
from jax import lax
from jax.experimental import pallas as pl
from jax.experimental.pallas import tpu as pltpu
from jax.sharding import PartitionSpec as P

EPSILON = 1e-06
ROPE_BASE = 1000000.0
MASKED = -1e30
LAGS = (2, 3, 8)
VMEM_BYTES = 56 * 2**20
SMALL = pl.CostEstimate(flops=2**20, bytes_accessed=2**20, transcendentals=0)


def norm_rows(value, gain):
    scale = lax.rsqrt(jnp.mean(value * value, -1, keepdims=True) + EPSILON)
    return (value * scale * gain, scale)


def norm_back(value, scale, gain, grad):
    inner = grad * gain
    first = scale * inner - value * (scale * scale * scale) * jnp.mean(
        inner * value, -1, keepdims=True
    )
    return (first, grad * value * scale)


def rope_tables(positions, width):
    half = width // 2
    inverse = ROPE_BASE ** (-jnp.arange(half, dtype=jnp.float32) * 2.0 / width)
    angle = positions.astype(jnp.float32)[:, None] * inverse[None, :]
    cosine, sine = jnp.cos(angle), jnp.sin(angle)
    return (jnp.concatenate([cosine, cosine], -1), jnp.concatenate([-sine, sine], -1))


def swap_halves(value):
    half = value.shape[-1] // 2
    return jnp.concatenate([value[..., half:], value[..., :half]], -1)


def nothing_kernel(*refs):
    pass


def after(value, *others):
    return pl.pallas_call(
        nothing_kernel,
        in_specs=[pl.BlockSpec(memory_space=pl.ANY)] * (1 + len(others)),
        out_specs=pl.BlockSpec(memory_space=pl.ANY),
        out_shape=jax.ShapeDtypeStruct(value.shape, value.dtype),
        input_output_aliases={0: 0},
    )(value, *others)


def gather_kernel(count, arrays, stacked, *refs):
    own = refs[:arrays]
    full = [refs[arrays].at[i] for i in range(stacked)]
    full += refs[arrays + min(stacked, 1) : -3]
    send_sem, recv_sem, own_sem = refs[-3:]
    me = lax.axis_index("ctx")
    barrier = pltpu.get_barrier_semaphore()
    for other in (lax.rem(me + 1, count), lax.rem(me + count - 1, count)):
        pl.semaphore_signal(
            barrier, inc=1, device_id={"ctx": other}, device_id_type=pl.DeviceIdType.MESH
        )
    pl.semaphore_wait(barrier, 2)

    def block(i, at):
        rows = own[i].shape[0]
        return full[i].at[pl.ds(at * rows, rows)]

    def passing(way, step, i, at):
        return pltpu.make_async_remote_copy(
            src_ref=own[i] if step == 0 else block(i, at),
            dst_ref=block(i, at),
            send_sem=send_sem.at[way, step, i],
            recv_sem=recv_sem.at[way, step, i],
            device_id={"ctx": me + (1 if way == 0 else -1)},
            device_id_type=pl.DeviceIdType.MESH,
        )

    def sends(way, step):
        if way == 0:
            return (me >= step) & (me < count - 1)
        return (me + step < count) & (me > 0)

    def receives(way, step):
        return me >= step + 1 if way == 0 else me + step + 1 < count

    kept = [pltpu.make_async_copy(own[i], block(i, me), own_sem.at[i]) for i in range(arrays)]
    for step in range(count - 1):
        for i in range(arrays):
            for way in (0, 1):
                sign = 1 if way == 0 else -1

                @pl.when(sends(way, step))
                def _():
                    passing(way, step, i, me - sign * step).start()

        if step == 0:
            for copy in kept:
                copy.start()
        for i in range(arrays):
            for way in (0, 1):
                sign = 1 if way == 0 else -1

                @pl.when(receives(way, step))
                def _():
                    passing(way, step, i, me - sign * (step + 1)).wait_recv()

    for copy in kept:
        copy.wait()
    for step in range(count - 1):
        for i in range(arrays):
            for way in (0, 1):
                sign = 1 if way == 0 else -1

                @pl.when(sends(way, step))
                def _():
                    passing(way, step, i, me - sign * step).wait_send()


def line_gather(*blocks, number, stacked=0):
    count = lax.axis_size("ctx")
    arrays = len(blocks)
    shapes = [(count * block.shape[0],) + block.shape[1:] for block in blocks]
    types = [block.dtype for block in blocks]
    if stacked:
        shapes = [(stacked,) + shapes[0]] + shapes[stacked:]
        types = types[:1] + types[stacked:]
    return pl.pallas_call(
        functools.partial(gather_kernel, count, arrays, stacked),
        in_specs=[pl.BlockSpec(memory_space=pl.ANY)] * arrays,
        out_specs=[pl.BlockSpec(memory_space=pl.ANY)] * len(shapes),
        out_shape=[jax.ShapeDtypeStruct(*pair) for pair in zip(shapes, types)],
        scratch_shapes=[
            pltpu.SemaphoreType.DMA((2, count - 1, arrays)),
            pltpu.SemaphoreType.DMA((2, count - 1, arrays)),
            pltpu.SemaphoreType.DMA((arrays,)),
        ],
        compiler_params=pltpu.CompilerParams(collective_id=number, has_side_effects=True),
        cost_estimate=pl.CostEstimate(flops=0, bytes_accessed=200 * 2**20, transcendentals=0),
    )(*blocks)


def expert_kernel(
    rows_ref,
    grad_ref,
    gate_ref,
    up_ref,
    down_ref,
    active_ref,
    gate_grad_ref,
    up_grad_ref,
    out_ref,
    back_ref,
    value_ref,
):
    gate = along(rows_ref[...], gate_ref[...])
    upper = along(rows_ref[...], up_ref[...])
    active_grad = across(grad_ref[...], down_ref[...])
    sigma = jax.nn.sigmoid(gate)
    swish = gate * sigma
    active = (swish * upper).astype(jnp.bfloat16)
    active_ref[...] = active
    out_ref[...] = along(active, down_ref[...]).astype(jnp.bfloat16)
    gate_grad = (active_grad * upper * sigma * (1.0 + gate * (1.0 - sigma))).astype(jnp.bfloat16)
    up_grad = (active_grad * swish).astype(jnp.bfloat16)
    gate_grad_ref[...] = gate_grad
    up_grad_ref[...] = up_grad
    value_ref[...] = jnp.sum(active_grad * active.astype(jnp.float32), -1, keepdims=True)
    back_ref[...] = (across(gate_grad, gate_ref[...]) + across(up_grad, up_ref[...])).astype(
        jnp.bfloat16
    )


def run_expert(rows, grad, gate, up, down, step):
    sources, block, width = rows.shape
    units = gate.shape[1]
    total = sources * block
    wide = pl.BlockSpec((block, width), lambda i: (i, 0))
    narrow = pl.BlockSpec((block, units), lambda i: (i, 0))

    def whole(shape):
        return pl.BlockSpec(shape, lambda i: (0, 0), pipeline_mode=pl.Buffered(1))

    low = jax.ShapeDtypeStruct((total, units), jnp.bfloat16)
    full = jax.ShapeDtypeStruct((total, width), jnp.bfloat16)
    return pl.pallas_call(
        expert_kernel,
        grid=(sources,),
        in_specs=[
            pl.BlockSpec((None, block, width), lambda i: (i, 0, 0)),
            pl.BlockSpec((None, None, block, width), lambda i: (i, step, 0, 0)),
            whole(gate.shape),
            whole(up.shape),
            whole(down.shape),
        ],
        out_specs=(narrow, narrow, narrow, wide, wide, pl.BlockSpec((block, 1), lambda i: (i, 0))),
        out_shape=(low, low, low, full, full, jax.ShapeDtypeStruct((total, 1), jnp.float32)),
        compiler_params=pltpu.CompilerParams(vmem_limit_bytes=VMEM_BYTES),
        cost_estimate=SMALL,
    )(rows, grad, gate, up, down)


def plane_tables(routes_all, weights_all, first, planned):
    hit = routes_all[..., None] == first + jnp.arange(planned, dtype=jnp.int32)
    named = jnp.any(hit, -2)
    weight = jnp.sum(jnp.where(hit, weights_all[..., None], 0.0), -2)
    rows = routes_all.shape[-2]
    earlier = (
        jnp.arange(rows, dtype=jnp.int32)[:, None] > jnp.arange(rows, dtype=jnp.int32)[None, :]
    ).astype(jnp.bfloat16)
    rank = jnp.einsum(
        "tu,cuj->ctj", earlier, named.astype(jnp.bfloat16), preferred_element_type=jnp.float32
    ).astype(jnp.int32)
    place = jnp.where(named, rank, -1)
    return place.transpose(0, 2, 1), weight.transpose(0, 2, 1)


def pick_kernel(planes, place_ref, weight_ref, rows_ref, out_ref, weighted):
    capacity = out_ref.shape[2]
    local = rows_ref.shape[0]
    slots = lax.broadcasted_iota(jnp.int32, (capacity, local), 0)
    if capacity % 16 == 0:
        chosen = [place_ref[0, 0, j : j + 1, :] == slots for j in range(planes)]
        picked = jnp.dot(
            jnp.concatenate([jnp.where(c, 1.0, 0.0).astype(jnp.bfloat16) for c in chosen], 0),
            rows_ref[...],
            preferred_element_type=jnp.float32,
        )
        for j in range(planes):
            rows = picked[j * capacity : (j + 1) * capacity]
            if weighted:
                rows = rows * jnp.sum(
                    jnp.where(chosen[j], weight_ref[0, 0, j : j + 1, :], 0.0), -1, keepdims=True
                )
            out_ref[j, 0] = rows.astype(jnp.bfloat16)
        return
    for j in range(planes):
        chosen = place_ref[0, 0, j : j + 1, :] == slots
        picked = jnp.dot(
            jnp.where(chosen, 1.0, 0.0).astype(jnp.bfloat16),
            rows_ref[...],
            preferred_element_type=jnp.float32,
        )
        if weighted:
            picked = picked * jnp.sum(
                jnp.where(chosen, weight_ref[0, 0, j : j + 1, :], 0.0), -1, keepdims=True
            )
        out_ref[j, 0] = picked.astype(jnp.bfloat16)


def pick_rows(place, weight, blocks, capacity, weighted):
    count, planned, local = place.shape
    width = blocks.shape[1]
    part = 4 if planned % 4 == 0 else planned
    shape = (count, planned // part, part, local)
    return pl.pallas_call(
        functools.partial(pick_kernel, part, weighted=weighted),
        grid=(count, planned // part),
        in_specs=[
            pl.BlockSpec((1, 1, part, local), lambda c, g: (c, g, 0, 0)),
            pl.BlockSpec((1, 1, part, local), lambda c, g: (c, g, 0, 0)),
            pl.BlockSpec((local, width), lambda c, g: (c, 0)),
        ],
        out_specs=pl.BlockSpec((part, 1, capacity, width), lambda c, g: (g, c, 0, 0)),
        out_shape=jax.ShapeDtypeStruct((planned, count, capacity, width), jnp.bfloat16),
        compiler_params=pltpu.CompilerParams(vmem_limit_bytes=VMEM_BYTES),
        cost_estimate=SMALL,
    )(place.reshape(shape), weight.reshape(shape), blocks)


def weight_kernel(steps, micro, *refs):
    rows, (grads_ref,) = refs[:micro], refs[micro : micro + 1]
    actives, gates, ups = (refs[micro * i + 1 : micro * i + 1 + micro] for i in (1, 2, 3))
    outs = refs[4 * micro + 1 : 4 * micro + 4]
    sums, sem = refs[4 * micro + 4 : 4 * micro + 7], refs[-1]
    step = pl.program_id(0)

    def flat(ref):
        count, block, width = ref.shape
        return ref[...].reshape(count * block, width)

    def add(which, fresh):
        x = flat(rows[which])
        for sum_ref, left, right in (
            (sums[0], x, gates[which][...]),
            (sums[1], x, ups[which][...]),
            (sums[2], actives[which][...], flat(grads_ref)),
        ):
            term = lax.dot_general(
                left, right, (((0,), (0,)), ((), ())), preferred_element_type=jnp.float32
            )
            if fresh:
                sum_ref[0] = term
            else:
                sum_ref[0] += term

    pl.when(step == 0)(lambda: add(0, True))
    pl.when((step > 0) & (step < steps))(lambda: add(0, False))
    for which in range(1, micro):
        pl.when((step >= which * steps) & (step < (which + 1) * steps))(
            functools.partial(add, which, False)
        )

    @pl.when(step == micro * steps - 1)
    def _():
        copies = [pltpu.make_async_copy(sums[i], outs[i], sem.at[i]) for i in range(3)]
        for copy in copies:
            copy.start()
        for copy in copies:
            copy.wait()


def expert_weight_grads(rows, grads, actives, gates, ups):
    sources, micro, block, width = grads.shape
    units = gates[0].shape[1]
    steps = sources // 2

    def turn(i, which):
        return jnp.clip(i - which * steps, 0, steps - 1)

    def specs(size):
        return [
            pl.BlockSpec((2 * block, size), functools.partial(lambda w, i: (turn(i, w), 0), which))
            for which in range(micro)
        ]

    def row_specs():
        return [
            pl.BlockSpec(
                (2, block, width), functools.partial(lambda w, i: (turn(i, w), 0, 0), which)
            )
            for which in range(micro)
        ]

    shapes = [(1, width, units), (1, width, units), (1, units, width)]
    return pl.pallas_call(
        functools.partial(weight_kernel, steps, micro),
        grid=(micro * steps,),
        in_specs=row_specs()
        + [
            pl.BlockSpec(
                (2, None, block, width), lambda i: (lax.rem(i, steps), lax.div(i, steps), 0, 0)
            )
        ]
        + specs(units) * 3,
        out_specs=[pl.BlockSpec(memory_space=pl.ANY)] * 3,
        out_shape=[jax.ShapeDtypeStruct(shape, jnp.float32) for shape in shapes],
        scratch_shapes=[pltpu.VMEM(shape, jnp.float32) for shape in shapes]
        + [pltpu.SemaphoreType.DMA((3,))],
        compiler_params=pltpu.CompilerParams(vmem_limit_bytes=VMEM_BYTES),
        cost_estimate=SMALL,
    )(*rows, grads, *actives, *gates, *ups)


def fill_mask(place_ref, mask_ref):
    base, bound = place_ref[0], place_ref[1]
    keys, rows = mask_ref.shape
    key_at = lax.broadcasted_iota(jnp.int32, (keys, rows), 0)
    row_at = lax.broadcasted_iota(jnp.int32, (keys, rows), 1) + base
    least = jnp.where(row_at >= bound, bound, 0)
    mask_ref[...] = jnp.where((key_at <= row_at) & (key_at >= least), 0.0, MASKED)


def head_queries(raw, gain, cosine, sine):
    scale = lax.rsqrt(jnp.mean(raw * raw, -1, keepdims=True) + EPSILON)
    value = raw * scale * gain
    turned = value * cosine + pltpu.roll(value, value.shape[-1] // 2, 1) * sine
    return turned.astype(jnp.bfloat16), scale


def across(a, b):
    return lax.dot_general(a, b, (((1,), (1,)), ((), ())), preferred_element_type=jnp.float32)


def along(a, b):
    return jnp.dot(a, b, preferred_element_type=jnp.float32)


def keyed(both_ref, width, which):
    count, rows = both_ref.shape[:2]
    return both_ref[:, :, which * width : (which + 1) * width].reshape(count * rows, width)


def attend_kernel(
    per, factor, place_ref, raw_ref, both_ref, gain_ref, cos_ref, sin_ref, *rest
):
    out_ref, mask_ref, turned_ref = rest[-3:]
    width = gain_ref.shape[1]
    group_step, step = pl.program_id(0), pl.program_id(1)

    @pl.when((group_step == 0) & (step == 0))
    def _():
        fill_mask(place_ref, mask_ref)

    @pl.when(step == 0)
    def _():
        turned_ref[...] = keyed(both_ref, width, 1).T

    for head in range(per):
        columns = slice(head * width, (head + 1) * width)
        queries, _ = head_queries(raw_ref[:, columns], gain_ref[...], cos_ref[...], sin_ref[...])
        chances = jnp.exp2(across(keyed(both_ref, width, 0), queries) * factor + mask_ref[...])
        total = jnp.sum(chances, 0, keepdims=True)
        result = along(turned_ref[...], chances.astype(jnp.bfloat16)) * (1.0 / total)
        out_ref[:, columns] = result.T.astype(jnp.bfloat16)


class Exchange:
    def __init__(self, axis, rows_ref, out_ref, send_sem, recv_sem, own_sem):
        self.axis, self.count = axis, rows_ref.shape[0]
        self.rows_ref, self.out_ref = rows_ref, out_ref
        self.send_sem, self.recv_sem, self.own_sem = send_sem, recv_sem, own_sem
        self.me = lax.axis_index(axis)

    @staticmethod
    def scratch(count):
        return [
            pltpu.SemaphoreType.DMA((count,)),
            pltpu.SemaphoreType.DMA((count,)),
            pltpu.SemaphoreType.DMA,
        ]

    def passing(self, k, part):
        return pltpu.make_async_remote_copy(
            src_ref=self.rows_ref.at[lax.rem(self.me + k, self.count)],
            dst_ref=self.out_ref.at[part],
            send_sem=self.send_sem.at[k],
            recv_sem=self.recv_sem.at[k],
            device_id={self.axis: lax.rem(self.me + k, self.count)},
            device_id_type=pl.DeviceIdType.MESH,
        )

    def kept(self):
        return pltpu.make_async_copy(
            self.rows_ref.at[self.me], self.out_ref.at[self.me], self.own_sem
        )

    def begin(self):
        for k in range(1, self.count):
            self.passing(k, self.me).start()
        self.kept().start()

    def finish(self):
        self.kept().wait()
        for k in range(1, self.count):
            self.passing(k, lax.rem(self.me + self.count - k, self.count)).wait_recv()
        for k in range(1, self.count):
            self.passing(k, self.me).wait_send()


def greet(**counts):
    barrier = pltpu.get_barrier_semaphore()
    for axis, count in counts.items():
        me = lax.axis_index(axis)
        for k in range(1, count):
            pl.semaphore_signal(
                barrier,
                inc=1,
                device_id={axis: lax.rem(me + k, count)},
                device_id_type=pl.DeviceIdType.MESH,
            )
    pl.semaphore_wait(barrier, sum(counts.values()) - len(counts))


class RowExchange:
    def __init__(self, ring, held_ref, out_ref, send_sem, recv_sem, own_sem):
        self.ring, self.held_ref, self.out_ref = ring, held_ref, out_ref
        self.send_sem, self.recv_sem, self.own_sem = send_sem, recv_sem, own_sem
        self.me = lax.axis_index("ctx")
        self.rows = out_ref.shape[2]

    @staticmethod
    def scratch(ring, groups):
        return [
            pltpu.SemaphoreType.DMA((groups, ring)),
            pltpu.SemaphoreType.DMA((groups, ring)),
            pltpu.SemaphoreType.DMA((groups,)),
        ]

    def held(self, group, at):
        return self.held_ref.at[group, pl.ds(at * self.rows, self.rows)]

    def passing(self, group, k, part):
        to = lax.rem(self.me + k, self.ring)
        return pltpu.make_async_remote_copy(
            src_ref=self.held(group, to),
            dst_ref=self.out_ref.at[part, group],
            send_sem=self.send_sem.at[group, k],
            recv_sem=self.recv_sem.at[group, k],
            device_id={"ctx": to},
            device_id_type=pl.DeviceIdType.MESH,
        )

    def kept(self, group):
        return pltpu.make_async_copy(
            self.held(group, self.me), self.out_ref.at[self.me, group], self.own_sem.at[group]
        )

    def begin(self, group):
        for k in range(1, self.ring):
            self.passing(group, k, self.me).start()
        self.kept(group).start()

    def finish(self):
        for group in range(self.out_ref.shape[1]):
            self.kept(group).wait()
            for k in range(1, self.ring):
                self.passing(group, k, lax.rem(self.me + self.ring - k, self.ring)).wait_recv()
            for k in range(1, self.ring):
                self.passing(group, k, self.me).wait_send()


def attend_back_kernel(
    per,
    steps,
    factor,
    scale,
    count,
    ring,
    extra_axis,
    place_ref,
    raw_ref,
    feed_grad_ref,
    middle_ref,
    out_grad_ref,
    norm_ref,
    weight_ref,
    both_ref,
    pair_raw_ref,
    gain_ref,
    key_gain_ref,
    cos_ref,
    sin_ref,
    rows_ref,
    extra_ref,
    raw_grad_ref,
    pair_grad_ref,
    gain_grad_ref,
    branch_ref,
    middle_grad_ref,
    norm_grad_ref,
    moved_ref,
    extra_moved_ref,
    mask_ref,
    turned_ref,
    sums_ref,
    held_ref,
    landed_ref,
    *sems,
):
    width = gain_ref.shape[1]
    group_step, step = pl.program_id(0), pl.program_id(1)
    moving = Exchange("exp", rows_ref, moved_ref, *sems[:3])
    extra_moving = Exchange(extra_axis, extra_ref, extra_moved_ref, *sems[3:6])
    landing = RowExchange(ring, held_ref, landed_ref, *sems[6:])

    @pl.when((group_step == 0) & (step == 0))
    def _():
        greet(exp=count, ctx=ring)
        moving.begin()
        extra_moving.begin()
        fill_mask(place_ref, mask_ref)
        gain_grad_ref[...] = jnp.zeros_like(gain_grad_ref)
        norm_grad_ref[...] = jnp.zeros_like(norm_grad_ref)
        rows = middle_ref.shape[0]
        for at in range(0, rows, 64):
            part = slice(at, at + 64)
            value, grad = middle_ref[part, :], feed_grad_ref[part, :].astype(jnp.float32)
            norm = lax.rsqrt(jnp.mean(value * value, -1, keepdims=True) + EPSILON)
            first, gain_part = norm_back(value, norm, norm_ref[...], grad)
            total = out_grad_ref[part, :].astype(jnp.float32) + first
            middle_grad_ref[part, :] = total
            branch_ref[part, :] = total.astype(jnp.bfloat16)
            norm_grad_ref[0:1, :] += jnp.sum(gain_part, 0, keepdims=True)

    @pl.when(step == 0)
    def _():
        turned_ref[...] = keyed(both_ref, width, 0).T
        sums_ref[...] = jnp.zeros_like(sums_ref)

    def turned_back(grad, raw, norm, gain, row):
        back = grad * cos_ref[...] - pltpu.roll(grad, width // 2, 1) * sin_ref[...]
        inner = back * gain
        gain_grad_ref[row : row + 1, :] += jnp.sum(back * raw * norm, 0, keepdims=True)
        return (
            norm * inner - raw * (norm * norm * norm) * jnp.mean(inner * raw, -1, keepdims=True)
        ).astype(jnp.bfloat16)

    grads = across(branch_ref[...], weight_ref[...]).astype(jnp.bfloat16)
    for head in range(per):
        columns = slice(head * width, (head + 1) * width)
        raw = raw_ref[:, columns]
        queries, norm = head_queries(raw, gain_ref[...], cos_ref[...], sin_ref[...])
        grad = grads[:, columns]
        chances = jnp.exp2(across(keyed(both_ref, width, 0), queries) * factor + mask_ref[...])
        chances = chances * (1.0 / jnp.sum(chances, 0, keepdims=True))
        chance_grad = across(keyed(both_ref, width, 1), grad)
        mean = jnp.sum(chances * chance_grad, 0, keepdims=True)
        score_grad = (chances * (chance_grad - mean)).astype(jnp.bfloat16)
        sums_ref[:, :width] += along(score_grad, queries)
        sums_ref[:, width:] += along(chances.astype(jnp.bfloat16), grad)
        query_grad = (along(turned_ref[...], score_grad) * scale).astype(jnp.bfloat16)
        raw_grad_ref[:, columns] = turned_back(
            query_grad.astype(jnp.float32).T, raw, norm, gain_ref[...], 0
        )

    @pl.when(step == steps - 1)
    def _():
        held_ref[group_step, :, :width] = (sums_ref[:, :width] * scale).astype(jnp.bfloat16)
        held_ref[group_step, :, width:] = sums_ref[:, width:].astype(jnp.bfloat16)
        landing.begin(group_step)

    @pl.when((group_step == pl.num_programs(0) - 1) & (step == steps - 1))
    def _():
        landing.finish()
        for group in range(landed_ref.shape[1]):
            total = landed_ref[0, group].astype(jnp.float32)
            for other in range(1, ring):
                total += landed_ref[other, group].astype(jnp.float32)
            total = total.astype(jnp.bfloat16)
            start = 2 * group * width
            raw = pair_raw_ref[:, start : start + width]
            norm = lax.rsqrt(jnp.mean(raw * raw, -1, keepdims=True) + EPSILON)
            pair_grad_ref[:, start : start + width] = turned_back(
                total[:, :width].astype(jnp.float32), raw, norm, key_gain_ref[...], 1
            )
            pair_grad_ref[:, start + width : start + 2 * width] = total[:, width:]
        extra_moving.finish()
        moving.finish()


def attention_specs(raw, both, width, rows, step, per):
    kv_heads = both.shape[2] // (2 * width)
    heads = raw.shape[1] // width - 2 * kv_heads
    steps = heads // kv_heads // per
    count = both.shape[0]
    keys = count * rows
    wide = pl.BlockSpec((rows, per * width), lambda g, j: (0, g * steps + j))
    specs = dict(
        place=pl.BlockSpec(memory_space=pltpu.SMEM),
        raw=pl.BlockSpec((rows, per * width), lambda g, j: (step, g * steps + j)),
        heads=wide,
        both=pl.BlockSpec((count, rows, 2 * width), lambda g, j: (0, 0, g)),
        gain=pl.BlockSpec((1, width), lambda g, j: (0, 0)),
        table=pl.BlockSpec((rows, width), lambda g, j: (0, 0)),
    )
    params = pltpu.CompilerParams(vmem_limit_bytes=VMEM_BYTES)
    work = 2 * heads * rows * keys * width
    return kv_heads, heads, steps, keys, specs, params, work


def attend(raw, both, gain, cosine, sine, place, step, waits, per=2):
    rows, width = cosine.shape
    kv_heads, heads, steps, keys, specs, params, work = attention_specs(
        raw, both, width, rows, step, per
    )
    return pl.pallas_call(
        functools.partial(attend_kernel, per, width ** (-0.5) * math.log2(math.e)),
        grid=(kv_heads, steps),
        in_specs=[specs[k] for k in ("place", "raw", "both", "gain", "table", "table")]
        + [pl.BlockSpec(memory_space=pl.ANY)] * len(waits),
        out_specs=specs["heads"],
        out_shape=jax.ShapeDtypeStruct((rows, heads * width), jnp.bfloat16),
        scratch_shapes=[
            pltpu.VMEM((keys, rows), jnp.float32),
            pltpu.VMEM((width, keys), jnp.bfloat16),
        ],
        compiler_params=params,
        cost_estimate=SMALL,
    )(place, raw, both, gain, cosine, sine, *waits)


def attend_back(
    raw,
    feed_grad,
    middle,
    out_grad,
    norm,
    weight,
    both,
    gain,
    key_gain,
    cosine,
    sine,
    place,
    step,
    rows_out,
    extra,
    extra_axis,
    per=2,
):
    rows, width = cosine.shape
    kv_heads, heads, steps, keys, specs, params, work = attention_specs(
        raw, both, width, rows, step, per
    )
    count, ring = rows_out.shape[0], both.shape[0]
    anywhere = pl.BlockSpec(memory_space=pl.ANY)
    pairs = 2 * kv_heads * width
    pair_place = heads * width // pairs
    return pl.pallas_call(
        functools.partial(
            attend_back_kernel,
            per,
            steps,
            width ** (-0.5) * math.log2(math.e),
            width ** (-0.5),
            count,
            ring,
            extra_axis,
        ),
        grid=(kv_heads, steps),
        in_specs=[
            specs["place"],
            specs["raw"],
            pl.BlockSpec(middle.shape, lambda g, j: (0, 0)),
            pl.BlockSpec(middle.shape, lambda g, j: (0, 0)),
            pl.BlockSpec(middle.shape, lambda g, j: (0, 0)),
            pl.BlockSpec(norm.shape, lambda g, j: (0, 0)),
            pl.BlockSpec((per * width, weight.shape[1]), lambda g, j: (g * steps + j, 0)),
            specs["both"],
            pl.BlockSpec((rows, pairs), lambda g, j: (step, pair_place)),
            specs["gain"],
            specs["gain"],
            specs["table"],
            specs["table"],
            anywhere,
            anywhere,
        ],
        out_specs=(
            specs["heads"],
            pl.BlockSpec((rows, pairs), lambda g, j: (0, 0)),
            pl.BlockSpec((8, width), lambda g, j: (0, 0)),
            pl.BlockSpec(middle.shape, lambda g, j: (0, 0)),
            pl.BlockSpec(middle.shape, lambda g, j: (0, 0)),
            pl.BlockSpec((8, middle.shape[1]), lambda g, j: (0, 0)),
            anywhere,
            anywhere,
        ),
        out_shape=(
            jax.ShapeDtypeStruct((rows, heads * width), jnp.bfloat16),
            jax.ShapeDtypeStruct((rows, pairs), jnp.bfloat16),
            jax.ShapeDtypeStruct((8, width), jnp.float32),
            jax.ShapeDtypeStruct(middle.shape, jnp.bfloat16),
            jax.ShapeDtypeStruct(middle.shape, jnp.float32),
            jax.ShapeDtypeStruct((8, middle.shape[1]), jnp.float32),
            jax.ShapeDtypeStruct(rows_out.shape, rows_out.dtype),
            jax.ShapeDtypeStruct(extra.shape, extra.dtype),
        ),
        scratch_shapes=[
            pltpu.VMEM((keys, rows), jnp.float32),
            pltpu.VMEM((width, keys), jnp.bfloat16),
            pltpu.VMEM((keys, 2 * width), jnp.float32),
            pltpu.VMEM((kv_heads, keys, 2 * width), jnp.bfloat16),
            pltpu.VMEM((ring, kv_heads, rows, 2 * width), jnp.bfloat16),
        ]
        + Exchange.scratch(count)
        + Exchange.scratch(extra.shape[0])
        + RowExchange.scratch(ring, kv_heads),
        compiler_params=pltpu.CompilerParams(
            vmem_limit_bytes=VMEM_BYTES, collective_id=1 + step, has_side_effects=True
        ),
        cost_estimate=SMALL,
    )(
        place,
        raw,
        feed_grad,
        middle,
        out_grad,
        norm,
        weight,
        both,
        raw,
        gain,
        key_gain,
        cosine,
        sine,
        rows_out,
        extra,
    )


def combine_kernel(place_ref, weight_ref, back_ref, out_ref, *, weighted):
    experts, _, capacity, width = back_ref.shape
    local = out_ref.shape[0]
    slots = lax.broadcasted_iota(jnp.int32, (capacity, local), 0)
    factors = []
    for j in range(experts):
        value = weight_ref[0, j : j + 1, :] if weighted else 1.0
        chosen = place_ref[0, j : j + 1, :] == slots
        factors.append(jnp.where(chosen, value, 0.0).astype(jnp.bfloat16))
    out_ref[...] = lax.dot_general(
        jnp.concatenate(factors, 0),
        back_ref[...].reshape(experts * capacity, width),
        (((0,), (0,)), ((), ())),
        preferred_element_type=jnp.float32,
    ).astype(jnp.bfloat16)


def combine_rows(place, weight, back, weighted):
    count, planned, local = place.shape
    capacity, width = back.shape[2:]
    return pl.pallas_call(
        functools.partial(combine_kernel, weighted=weighted),
        grid=(count,),
        in_specs=[
            pl.BlockSpec((1, planned, local), lambda c: (c, 0, 0)),
            pl.BlockSpec((1, planned, local), lambda c: (c, 0, 0)),
            pl.BlockSpec((planned, 1, capacity, width), lambda c: (0, c, 0, 0)),
        ],
        out_specs=pl.BlockSpec((local, width), lambda c: (c, 0)),
        out_shape=jax.ShapeDtypeStruct((count * local, width), jnp.bfloat16),
        compiler_params=pltpu.CompilerParams(vmem_limit_bytes=VMEM_BYTES),
        cost_estimate=SMALL,
    )(place, weight, back)


class GradSums:
    def __init__(self, ring, micro, head_dim, sizes, refs):
        self.ring, self.micro, self.sizes = ring, micro, sizes
        self.head_dim = head_dim
        self.attended, self.hidden = refs[:micro], refs[micro]
        refs = refs[micro + 1 :]
        self.branch, self.query, self.pair = (
            refs[i * micro : (i + 1) * micro] for i in range(3)
        )
        self.weight = refs[3 * micro]
        self.out = refs[3 * micro + 1 : 3 * micro + 5]
        self.hidden_grad = refs[3 * micro + 5]
        self.far = refs[3 * micro + 6 : 3 * micro + 9]
        scratch = refs[3 * micro + 9 :]
        self.left_v, self.right_v = scratch[:2], scratch[2:4]
        self.part, self.first, self.second, self.last = (
            scratch[4 + 2 * i : 6 + 2 * i] for i in range(4)
        )
        (
            self.left_sem,
            self.far_sem,
            self.load_sem,
            self.first_sem,
            self.second_sem,
            self.last_sem,
            self.weight_sem,
        ) = scratch[12:]
        e = lax.axis_index("exp")
        self.core, self.y, self.x = lax.rem(e, 2), lax.div(e, 4), lax.rem(lax.div(e, 2), 2)
        self.partner = e + 1 - 2 * self.core
        self.across_x, self.across_y = e + 2 - 4 * self.x, e + 4 - 8 * self.y
        self.z = lax.axis_index("ctx")
        self.order = [
            (kind, chunk) for kind, size in enumerate(sizes) for chunk in range(size[2] // size[3])
        ]

    @staticmethod
    def scratch(ring, micro, sizes):
        chunks = [size[2] // size[3] for size in sizes]
        total = sum(chunks)
        shapes = [pltpu.VMEM((4, size[0], size[1]), jnp.bfloat16) for size in sizes]
        shapes += [pltpu.VMEM((2, size[0], size[3]), jnp.bfloat16) for size in sizes]
        for lead, share in (((4,), 1), ((2,), 1), ((), 1), ((ring,), ring)):
            for size, count in zip(sizes, chunks):
                shapes.append(
                    pltpu.VMEM((count,) + lead + (size[1] // share, size[3]), jnp.bfloat16)
                )
        shapes += [
            pltpu.SemaphoreType.DMA((3, micro + 1, 4, ring)),
            pltpu.SemaphoreType.DMA((2, 3, micro)),
            pltpu.SemaphoreType.DMA((total, 2, micro)),
            pltpu.SemaphoreType.DMA((2, total, 2)),
            pltpu.SemaphoreType.DMA((2, total)),
            pltpu.SemaphoreType.DMA((2, total, ring)),
            pltpu.SemaphoreType.DMA((4,)),
        ]
        return shapes

    def weight_loads(self, chunk):
        _, high, wide = self.left_v[0].shape
        return [
            pltpu.make_async_copy(
                self.weight.at[pl.ds(r * high, high), pl.ds(chunk * wide, wide)],
                self.left_v[0].at[2 * (chunk % 2) + r],
                self.weight_sem.at[2 * (chunk % 2) + r],
            )
            for r in (0, 1)
        ]

    def add_hidden(self, chunk):
        high = self.left_v[0].shape[1]
        half = self.sizes[1][0] // 2
        for copy in self.weight_loads(chunk):
            copy.wait()
        for r in (0, 1):
            columns = slice(r * high, (r + 1) * high)
            term = across(
                self.right_v[1][chunk % 2, :half], self.left_v[0][2 * (chunk % 2) + r]
            )
            if chunk == 0:
                self.hidden_grad[:, columns] = term
            else:
                self.hidden_grad[:, columns] += term

    def to_partner(self, src, dst, send_sem, recv_sem):
        return pltpu.make_async_remote_copy(
            src_ref=src,
            dst_ref=dst,
            send_sem=send_sem,
            recv_sem=recv_sem,
            device_id={"exp": self.partner},
            device_id_type=pl.DeviceIdType.MESH,
        )

    def left_copies(self, kind):
        half = self.sizes[kind][0] // 2
        own, sent = [], []
        if kind == 1:
            place = (self.micro, 0, 0)
            own.append(
                pltpu.make_async_copy(
                    self.hidden.at[self.core],
                    self.left_v[1].at[:, pl.ds(0, half)],
                    self.left_sem.at[(0,) + place],
                )
            )
            sent.append(
                self.to_partner(
                    self.hidden.at[1 - self.core],
                    self.left_v[1].at[:, pl.ds(half, half)],
                    self.left_sem.at[(1,) + place],
                    self.left_sem.at[(2,) + place],
                )
            )
            return own, sent
        share = self.sizes[kind][1] // self.ring
        rows = half // self.micro
        for m in range(self.micro):
            for piece in range(4):
                for c in range(self.ring):

                    def columns(core):
                        block = c * 8 + piece * 2 + core
                        return self.attended[m].at[
                            :, pl.ds(pl.multiple_of(block * share, share), share)
                        ]

                    def place(base):
                        return self.left_v[0].at[
                            piece, pl.ds(base + m * rows, rows), pl.ds(c * share, share)
                        ]

                    own.append(
                        pltpu.make_async_copy(
                            columns(self.core), place(0), self.left_sem.at[0, m, piece, c]
                        )
                    )
                    sent.append(
                        self.to_partner(
                            columns(1 - self.core),
                            place(half),
                            self.left_sem.at[1, m, piece, c],
                            self.left_sem.at[2, m, piece, c],
                        )
                    )
        return own, sent

    def right_copies(self, which):
        near = (self.branch, self.query, self.pair)[which]
        return [
            self.to_partner(
                near[m],
                self.far[which].at[m],
                self.far_sem.at[0, which, m],
                self.far_sem.at[1, which, m],
            )
            for m in range(self.micro)
        ]

    def source(self, i):
        kind, chunk = self.order[i]
        wide = self.sizes[kind][3]
        if kind == 0:
            return 0, chunk * wide
        query_width = self.query[0].shape[1]
        if chunk * wide < query_width:
            return 1, chunk * wide
        return 2, chunk * wide - query_width

    def loads(self, i, far):
        kind, chunk = self.order[i]
        which, start = self.source(i)
        wide = self.sizes[kind][3]
        half = self.sizes[kind][0] // 2
        rows = half // self.micro
        near = (self.branch, self.query, self.pair)[which]
        return [
            pltpu.make_async_copy(
                (self.far[which].at[m] if far else near[m]).at[:, pl.ds(start, wide)],
                self.right_v[kind].at[chunk % 2, pl.ds(far * half + m * rows, rows)],
                self.load_sem.at[i, far, m],
            )
            for m in range(self.micro)
        ]

    def start_loads(self, i):
        which, start = self.source(i)
        for copy in self.loads(i, 0):
            copy.start()
        if start == 0:
            for copy in self.right_copies(which):
                copy.wait_recv()
        for copy in self.loads(i, 1):
            copy.start()

    def x_first(self, i):
        return i % 2 == 0

    def step_first(self, i, k):
        kind, chunk = self.order[i]
        if self.x_first(i):
            piece, to = 2 * k + 1 - self.x, self.across_x
        else:
            piece, to = 2 * (1 - self.y) + k, self.across_y
        return pltpu.make_async_remote_copy(
            src_ref=self.part[kind].at[chunk, piece],
            dst_ref=self.first[kind].at[chunk, k],
            send_sem=self.first_sem.at[0, i, k],
            recv_sem=self.first_sem.at[1, i, k],
            device_id={"exp": to},
            device_id_type=pl.DeviceIdType.MESH,
        )

    def step_second(self, i):
        kind, chunk = self.order[i]
        if self.x_first(i):
            piece, to = 2 * (1 - self.y) + self.x, self.across_y
        else:
            piece, to = 2 * self.y + 1 - self.x, self.across_x
        return pltpu.make_async_remote_copy(
            src_ref=self.part[kind].at[chunk, piece],
            dst_ref=self.second[kind].at[chunk],
            send_sem=self.second_sem.at[0, i],
            recv_sem=self.second_sem.at[1, i],
            device_id={"exp": to},
            device_id_type=pl.DeviceIdType.MESH,
        )

    def mine(self, i):
        kind, chunk = self.order[i]
        return self.part[kind].at[chunk, 2 * self.y + self.x]

    def step_last(self, i, k, slot):
        kind, chunk = self.order[i]
        to = lax.rem(self.z + k, self.ring)
        rows = self.sizes[kind][1] // self.ring
        return pltpu.make_async_remote_copy(
            src_ref=self.mine(i).at[pl.ds(to * rows, rows)],
            dst_ref=self.last[kind].at[chunk, slot],
            send_sem=self.last_sem.at[0, i, k],
            recv_sem=self.last_sem.at[1, i, k],
            device_id={"ctx": to},
            device_id_type=pl.DeviceIdType.MESH,
        )

    def multiply(self, i):
        kind, chunk = self.order[i]
        for far in (0, 1):
            for copy in self.loads(i, far):
                copy.wait()

        def piece(p, carry):
            term = lax.dot_general(
                self.left_v[kind][p],
                self.right_v[kind][chunk % 2],
                (((0,), (0,)), ((), ())),
                preferred_element_type=jnp.float32,
            )
            self.part[kind][chunk, p] = term.astype(jnp.bfloat16)
            return carry

        lax.fori_loop(0, 4, piece, 0)
        for k in range(2):
            self.step_first(i, k).start()

    def add_first(self, i):
        kind, chunk = self.order[i]
        for k in range(2):
            self.step_first(i, k).wait_recv()
        for k in range(2):
            piece = 2 * k + self.x if self.x_first(i) else 2 * self.y + k
            self.part[kind][chunk, piece] = (
                self.part[kind][chunk, piece].astype(jnp.float32)
                + self.first[kind][chunk, k].astype(jnp.float32)
            ).astype(jnp.bfloat16)
        self.step_second(i).start()

    def add_second(self, i):
        kind, chunk = self.order[i]
        self.step_second(i).wait_recv()
        piece = 2 * self.y + self.x
        self.part[kind][chunk, piece] = (
            self.part[kind][chunk, piece].astype(jnp.float32)
            + self.second[kind][chunk].astype(jnp.float32)
        ).astype(jnp.bfloat16)
        for k in range(1, self.ring):
            self.step_last(i, k, k).start()

    def add_last(self, i):
        kind, chunk = self.order[i]
        rows, wide = self.sizes[kind][1] // self.ring, self.sizes[kind][3]
        for k in range(1, self.ring):
            self.step_last(i, k, k).wait_recv()
        total = self.part[kind][
            chunk, 2 * self.y + self.x, pl.ds(pl.multiple_of(self.z * rows, rows), rows), :
        ].astype(jnp.float32)
        for k in range(1, self.ring):
            total += self.last[kind][chunk, k].astype(jnp.float32)
        which, start = self.source(i)
        if which < 2:
            self.out[which][:, start : start + wide] = total
            return
        half = self.head_dim
        for at in range(0, wide, 2 * half):
            to = (start + at) // 2
            self.out[2][:, to : to + half] = total[:, at : at + half]
            self.out[3][:, to : to + half] = total[:, at + half : at + 2 * half]

    def run(self):
        chunks = len(self.order)
        barrier = pltpu.get_barrier_semaphore()
        for other in (self.partner, self.across_x, self.across_y):
            pl.semaphore_signal(
                barrier, inc=1, device_id={"exp": other}, device_id_type=pl.DeviceIdType.MESH
            )
        for k in range(1, self.ring):
            pl.semaphore_signal(
                barrier,
                inc=1,
                device_id={"ctx": lax.rem(self.z + k, self.ring)},
                device_id_type=pl.DeviceIdType.MESH,
            )
        pl.semaphore_wait(barrier, self.ring + 2)
        lefts = [self.left_copies(kind) for kind in (0, 1)]
        rights = [self.right_copies(which) for which in range(3)]
        for copies in (rights[0], lefts[0][1], lefts[0][0]):
            for copy in copies:
                copy.start()
        self.start_loads(0)
        for i in range(chunks + LAGS[-1]):
            if i < chunks:
                if i + 1 < chunks:
                    self.start_loads(i + 1)
                kind, chunk = self.order[i]
                if chunk == 0:
                    for copy in lefts[kind][0]:
                        copy.wait()
                    for copy in lefts[kind][1]:
                        copy.wait_recv()
                self.multiply(i)
                if i == 0:
                    for copies in (rights[1], *lefts[1], rights[2]):
                        for copy in copies:
                            copy.start()
                if kind == 0 and chunk == self.sizes[0][2] // self.sizes[0][3] - 1:
                    for copy in self.weight_loads(0):
                        copy.start()
                if kind == 1:
                    if i + 1 < chunks:
                        for copy in self.weight_loads(chunk + 1):
                            copy.start()
                    self.add_hidden(chunk)
            for lag, stage in zip(LAGS, (self.add_first, self.add_second, self.add_last)):
                if 0 <= i - lag < chunks:
                    stage(i - lag)
        for copies in (lefts[0][1], lefts[1][1], *rights):
            for copy in copies:
                copy.wait_send()
        for i in range(chunks):
            for k in range(2):
                self.step_first(i, k).wait_send()
            self.step_second(i).wait_send()
            for k in range(1, self.ring):
                self.step_last(i, k, k).wait_send()


def grad_sums_kernel(ring, micro, head_dim, sizes, *refs):
    GradSums(ring, micro, head_dim, sizes, refs).run()


def grad_sums(ring, head_dim, attended, hidden, branch, query, pair, weight, number):
    micro, rows = len(attended), attended[0].shape[0]
    tokens = 2 * micro * rows
    sizes = [
        (tokens, attended[0].shape[1] // 8, branch[0].shape[1], 256),
        (tokens, hidden.shape[3], query[0].shape[1] + pair[0].shape[1], 512),
    ]
    anywhere = pl.BlockSpec(memory_space=pl.ANY)
    assert weight.shape[0] == 2 * tokens and sizes[1][3] == sizes[0][1]
    share = sizes[1][1] // ring
    outs = [
        jax.ShapeDtypeStruct(shape, jnp.float32)
        for shape in (
            (sizes[0][1] // ring, sizes[0][2]),
            (share, query[0].shape[1]),
            (share, pair[0].shape[1] // 2),
            (share, pair[0].shape[1] // 2),
            (micro * rows, weight.shape[0]),
        )
    ]
    outs += [
        jax.ShapeDtypeStruct((micro,) + arrays[0].shape, jnp.bfloat16)
        for arrays in (branch, query, pair)
    ]
    return pl.pallas_call(
        functools.partial(grad_sums_kernel, ring, micro, head_dim, sizes),
        in_specs=[anywhere] * (4 * micro + 2),
        out_specs=[pl.BlockSpec(memory_space=pltpu.VMEM)] * 5 + [anywhere] * 3,
        out_shape=outs,
        scratch_shapes=GradSums.scratch(ring, micro, sizes),
        compiler_params=pltpu.CompilerParams(
            vmem_limit_bytes=60 * 2**20, collective_id=number, has_side_effects=True
        ),
        cost_estimate=SMALL,
    )(*attended, hidden, *branch, *query, *pair, weight)[:5]


def per_device(
    tokens,
    routes,
    route_weights,
    bounds,
    norm_attn,
    norm_ffn,
    q_gain,
    k_gain,
    w_q,
    w_k,
    w_v,
    w_o,
    w_gate,
    w_up,
    w_down,
    cotangent,
):
    micro = tokens.shape[0]
    local = tokens.shape[2]
    width = tokens.shape[3]
    head_dim = q_gain.shape[0]
    kv_heads = w_k.shape[1] // head_dim
    top = routes.shape[3]
    ring = lax.axis_size("ctx")
    plane = lax.axis_size("exp")
    assert w_gate.shape[0] == 1
    experts = ring * plane
    capacity = max(2, local * top * 5 // (4 * experts))
    seq_len = local * ring
    query_width = w_q.shape[1]
    pair_width = kv_heads * head_dim
    here = lax.axis_index("ctx")
    base = here * local
    cosine, sine = rope_tables(base + jnp.arange(local, dtype=jnp.int32), head_dim)
    gate_weight, up_weight, down_weight = w_gate[0], w_up[0], w_down[0]

    def dot(a, b):
        return jnp.dot(a, b, preferred_element_type=jnp.float32)

    def dot_t(a, b):
        return jnp.einsum("te,de->td", a, b, preferred_element_type=jnp.float32)

    def t_dot(a, b):
        return jnp.einsum("td,te->de", a, b, preferred_element_type=jnp.float32)

    def paired(keys, values):
        rows = keys.shape[0]
        return jnp.stack(
            [keys.reshape(rows, kv_heads, head_dim), values.reshape(rows, kv_heads, head_dim)], 2
        ).reshape(rows, 2 * pair_width)

    in_weight = lax.all_gather(
        jnp.concatenate([w_q, paired(w_k, w_v)], 1), "exp", axis=0, tiled=True
    )
    out_weight = lax.all_gather(w_o, "exp", axis=0, tiled=True)

    meta = jnp.concatenate([routes[:, 0].astype(jnp.float32), route_weights[:, 0]], -1)
    grads_low = [cotangent[step, 0] for step in range(micro)]
    grad_blocks, meta = line_gather(
        *grads_low, meta.reshape(-1, 128), number=0, stacked=micro
    )
    meta = meta.reshape(ring, micro, local, 2 * top)
    tables = [
        plane_tables(
            meta[:, step, :, :top].astype(jnp.int32), meta[:, step, :, top:], here * plane, plane
        )
        for step in range(micro)
    ]
    slots = jnp.arange(capacity, dtype=jnp.int32)
    chosen = [
        place.transpose(1, 0, 2)[:, :, None, :] == slots[None, None, :, None] for place, _ in tables
    ]

    def exchange(rows):
        return lax.all_to_all(rows, "exp", split_axis=0, concat_axis=0, tiled=True)

    def pick(blocks, step, weighted):
        return pick_rows(*tables[step], blocks, capacity, weighted)

    def combine(back, step, weighted):
        back = back.reshape(plane, ring, capacity, width)
        if capacity % 16 == 0:
            return combine_rows(*tables[step], back, weighted)
        factor = chosen[step]
        if weighted:
            weight = tables[step][1].transpose(1, 0, 2)
            factor = jnp.where(factor, weight[:, :, None, :], 0.0)
        part = jnp.einsum(
            "jcst,jcsd->ctd",
            factor.astype(jnp.bfloat16),
            back,
            preferred_element_type=jnp.float32,
        )
        return part.astype(jnp.bfloat16).reshape(seq_len, width)

    def scatter(part):
        return lax.psum_scatter(part, "ctx", scatter_dimension=0, tiled=True)

    picked = pick_rows(
        jnp.concatenate([place for place, _ in tables]),
        jnp.concatenate([weight for _, weight in tables]),
        grad_blocks.reshape(micro * seq_len, width),
        capacity,
        True,
    )
    incoming = exchange(picked.reshape(plane, micro * ring * capacity, width)).reshape(
        plane, micro, ring * capacity, width
    )

    rows = tokens[:, 0].astype(jnp.float32).reshape(micro * local, width)
    hidden, first_scale = norm_rows(rows, norm_attn)
    hidden = after(hidden.astype(jnp.bfloat16), picked)
    raw = dot(hidden, in_weight)
    hidden_parts = hidden.reshape(-1, ring, plane // 2, 2, width // experts)
    hidden_parts = hidden_parts.transpose(3, 2, 0, 1, 4).reshape(
        2, plane // 2, micro * local, ring * width // experts
    )
    pair_raw = raw[:, query_width:].reshape(micro * local, kv_heads, 2, head_dim)
    key_raw = pair_raw[:, :, 0]
    key_normed, key_scale = norm_rows(key_raw, k_gain)
    key_cos = jnp.tile(cosine, (micro, 1))[:, None, :]
    key_sin = jnp.tile(sine, (micro, 1))[:, None, :]
    keys = (key_normed * key_cos + swap_halves(key_normed) * key_sin).astype(jnp.bfloat16)
    pairs = jnp.stack([keys, pair_raw[:, :, 1].astype(jnp.bfloat16)], 2).reshape(
        micro * local, 2 * pair_width
    )
    gain_row = q_gain[None, :]
    both = list(line_gather(pairs[:local], number=3))
    both += [
        lax.all_gather(
            after(pairs[step * local : (step + 1) * local], both[0]), "ctx", axis=0, tiled=True
        )
        for step in range(1, micro)
    ]
    both = [gathered.reshape(ring, local, 2 * pair_width) for gathered in both]
    places, attended, middles, feeds, scales = [], [], [], [], []
    for step in range(micro):
        part = slice(step * local, (step + 1) * local)
        places.append(jnp.stack([base, bounds[step, 0]]).astype(jnp.int32))
        attended.append(
            attend(raw, both[step], gain_row, cosine, sine, places[step], step, feeds[-1:])
        )
        middles.append(rows[part] + dot(attended[step], out_weight))
        feed_in, second_scale = norm_rows(middles[step], norm_ffn)
        feeds.append(feed_in.astype(jnp.bfloat16))
        scales.append(second_scale)
    feed_blocks = [lax.all_gather(feed, "ctx", axis=0, tiled=True) for feed in feeds]

    def slotted(rows):
        return rows.reshape(plane, ring * capacity, width)

    received = []
    waits = (incoming,)
    feed_blocks[0] = after(feed_blocks[0], feeds[-1])
    for step in range(micro):
        picked = slotted(pick(feed_blocks[step], step, False))
        received.append(exchange(after(picked, *waits)))
        waits = (received[-1], hidden_parts)

    active, gate_grad, up_grad, produced, backs, pair_values = [], [], [], [], [], []
    for step in range(micro):
        parts = run_expert(received[step], incoming, gate_weight, up_weight, down_weight, step)
        for held, item in zip((active, gate_grad, up_grad, produced, backs, pair_values), parts):
            held.append(item)

    returned = []
    last = received[-1]
    for step in range(micro):
        returned.append(exchange(after(slotted(backs[step]), last)))
        last = returned[-1]
    gate_term, up_term, down_term = expert_weight_grads(
        received, incoming, active, gate_grad, up_grad
    )

    sums = jnp.stack([value.reshape(plane, ring * capacity) for value in pair_values], 1)
    sums = sums.reshape(plane, -1)
    spare = -sums.shape[1] % 1024
    extra = jnp.pad(sums, ((0, 0), (0, spare))).reshape(plane, -1, 128)

    branches, raw_grads, pair_grads = [], [], []
    middle_grads, gain_list, results = [], [], []
    waits = ()
    for step in range(micro):
        if step > 0:
            own_feed_grad = after(feed_grad, *waits)
        else:
            own_feed_grad = scatter(combine(after(returned[0], active[-1]), 0, False))
        if step == 0:
            returned[1] = after(returned[1], down_term)
            part_sums = combine(returned[1], 1, False)
            feed_grad = scatter(part_sums)
            waits = (part_sums,)
        raw_grad, pair_grad, gain_part, branch, middle_grad, norm_part, result, extra = attend_back(
            raw,
            own_feed_grad,
            middles[step],
            grads_low[step],
            norm_ffn[None, :],
            out_weight,
            both[step],
            gain_row,
            k_gain[None, :],
            cosine,
            sine,
            places[step],
            step,
            after(slotted(produced[step]), *waits),
            extra,
            ("exp", "ctx")[min(step, 1)],
        )
        if step == 0:
            sums = extra.reshape(plane, -1)[:, : micro * ring * capacity]
            sums = sums.reshape(plane, micro, ring, capacity)
            values = [
                jnp.sum(jnp.where(chosen[m], sums[:, m, :, :, None], 0.0), 2) for m in range(micro)
            ]
            values = jnp.stack(values, 1).transpose(2, 1, 0, 3)
            extra = values.reshape(ring, -1, 128)
        waits = (result,)
        results.append(result)
        raw_grads.append(raw_grad)
        pair_grads.append(pair_grad)
        branches.append(branch)
        middle_grads.append(middle_grad)
        gain_list.append((norm_part[0], gain_part[0], gain_part[1]))
    if plane == 8:
        out_total, query_total, key_total, value_total, hidden_grad = grad_sums(
            ring, head_dim, attended, hidden_parts, branches, raw_grads, pair_grads, in_weight, 5
        )
    else:

        def sum_over_devices(left, right):
            share = left.shape[1] // experts
            left = left.reshape(-1, ring, plane, share).transpose(0, 2, 1, 3)
            term = t_dot(left.reshape(-1, experts * share), right).astype(jnp.bfloat16)
            term = lax.psum_scatter(term, "exp", scatter_dimension=0, tiled=True)
            return lax.psum_scatter(term, "ctx", scatter_dimension=0, tiled=True).astype(
                jnp.float32
            )

        out_total = sum_over_devices(jnp.concatenate(attended, 0), jnp.concatenate(branches, 0))
        raw_grad = jnp.concatenate(
            [jnp.concatenate(raw_grads, 0), jnp.concatenate(pair_grads, 0)], 1
        )
        in_total = sum_over_devices(hidden, raw_grad)
        hidden_grad = dot_t(raw_grad, in_weight)
        query_total = in_total[:, :query_width]
        pair_total = in_total[:, query_width:].reshape(-1, kv_heads, 2, head_dim)
        key_total = pair_total[:, :, 0].reshape(-1, pair_width)
        value_total = pair_total[:, :, 1].reshape(-1, pair_width)
    first_grad, first_gain = norm_back(rows, first_scale, norm_attn, hidden_grad)
    tokens_grad = jnp.concatenate(middle_grads, 0) + first_grad
    gains = jnp.concatenate([jnp.sum(first_gain, 0)] + [sum(parts) for parts in zip(*gain_list)])
    gain_total = jnp.sum(
        lax.all_to_all(
            gains.reshape(experts, -1), ("ctx", "exp"), split_axis=0, concat_axis=0, tiled=True
        ),
        0,
    )

    outputs = [
        (middles[step] + scatter(combine(results[step], step, True)).astype(jnp.float32)).astype(
            jnp.bfloat16
        )
        for step in range(micro)
    ]

    values = extra.reshape(ring, micro, plane, local).transpose(1, 3, 0, 2)
    values = values.reshape(micro, local, experts)
    match = routes[:, 0, :, :, None] == jnp.arange(experts, dtype=jnp.int32)
    route_grads = jnp.sum(jnp.where(match, values[:, :, None, :], 0.0), -1) / route_weights[:, 0]

    return (
        jnp.stack(outputs)[:, None],
        tokens_grad.reshape(micro, 1, local, width),
        route_grads[:, None],
        query_total,
        key_total,
        value_total,
        out_total,
        gain_total,
        gate_term,
        up_term,
        down_term,
    )


def solution(mesh):
    in_specs = (
        P(None, "exp", "ctx", None),
        P(None, "exp", "ctx", None),
        P(None, "exp", "ctx", None),
        P(None, "exp"),
        P(),
        P(),
        P(),
        P(),
        P("exp", None),
        P("exp", None),
        P("exp", None),
        P("exp", None),
        P(("ctx", "exp"), None, None),
        P(("ctx", "exp"), None, None),
        P(("ctx", "exp"), None, None),
        P(None, "exp", "ctx", None),
    )
    out_specs = (
        P(None, "exp", "ctx", None),
        P(None, "exp", "ctx", None),
        P(None, "exp", "ctx", None),
        P(("ctx", "exp"), None),
        P(("ctx", "exp"), None),
        P(("ctx", "exp"), None),
        P(("ctx", "exp"), None),
        P(("ctx", "exp")),
        P(("ctx", "exp"), None, None),
        P(("ctx", "exp"), None, None),
        P(("ctx", "exp"), None, None),
    )
    return jax.shard_map(
        per_device, mesh=mesh, in_specs=in_specs, out_specs=out_specs, check_vma=False
    )
```

```python
import functools
import math

import jax
import jax.numpy as jnp
from jax import lax
from jax.experimental import pallas as pl
from jax.experimental.pallas import tpu as pltpu
from jax.sharding import PartitionSpec as P

EPSILON = 1e-06
ROPE_BASE = 1000000.0
MASKED = -1e30
LAGS = (2, 3, 8)
VMEM_BYTES = 56 * 2**20
SMALL = pl.CostEstimate(flops=2**20, bytes_accessed=2**20, transcendentals=0)


def norm_rows(value, gain):
    scale = lax.rsqrt(jnp.mean(value * value, -1, keepdims=True) + EPSILON)
    return (value * scale * gain, scale)


def norm_back(value, scale, gain, grad):
    inner = grad * gain
    first = scale * inner - value * (scale * scale * scale) * jnp.mean(
        inner * value, -1, keepdims=True
    )
    return (first, grad * value * scale)


def rope_tables(positions, width):
    half = width // 2
    inverse = ROPE_BASE ** (-jnp.arange(half, dtype=jnp.float32) * 2.0 / width)
    angle = positions.astype(jnp.float32)[:, None] * inverse[None, :]
    cosine, sine = jnp.cos(angle), jnp.sin(angle)
    return (jnp.concatenate([cosine, cosine], -1), jnp.concatenate([-sine, sine], -1))


def swap_halves(value):
    half = value.shape[-1] // 2
    return jnp.concatenate([value[..., half:], value[..., :half]], -1)


def nothing_kernel(*refs):
    pass


def after(value, *others):
    return pl.pallas_call(
        nothing_kernel,
        in_specs=[pl.BlockSpec(memory_space=pl.ANY)] * (1 + len(others)),
        out_specs=pl.BlockSpec(memory_space=pl.ANY),
        out_shape=jax.ShapeDtypeStruct(value.shape, value.dtype),
        input_output_aliases={0: 0},
    )(value, *others)


def gather_kernel(count, arrays, stacked, *refs):
    own = refs[:arrays]
    full = [refs[arrays].at[i] for i in range(stacked)]
    full += refs[arrays + min(stacked, 1) : -3]
    send_sem, recv_sem, own_sem = refs[-3:]
    me = lax.axis_index("ctx")
    barrier = pltpu.get_barrier_semaphore()
    for other in (lax.rem(me + 1, count), lax.rem(me + count - 1, count)):
        pl.semaphore_signal(
            barrier, inc=1, device_id={"ctx": other}, device_id_type=pl.DeviceIdType.MESH
        )
    pl.semaphore_wait(barrier, 2)

    def block(i, at):
        rows = own[i].shape[0]
        return full[i].at[pl.ds(at * rows, rows)]

    def passing(way, step, i, at):
        return pltpu.make_async_remote_copy(
            src_ref=own[i] if step == 0 else block(i, at),
            dst_ref=block(i, at),
            send_sem=send_sem.at[way, step, i],
            recv_sem=recv_sem.at[way, step, i],
            device_id={"ctx": lax.rem(me + (1 if way == 0 else count - 1), count)},
            device_id_type=pl.DeviceIdType.MESH,
        )

    def sends(way, step):
        if way == 0:
            return (me >= step) & (me < count - 1)
        return (me + step < count) & (me > 0)

    def receives(way, step):
        return me >= step + 1 if way == 0 else me + step + 1 < count

    kept = [pltpu.make_async_copy(own[i], block(i, me), own_sem.at[i]) for i in range(arrays)]
    for step in range(count - 1):
        for i in range(arrays):
            for way in (0, 1):
                sign = 1 if way == 0 else -1

                @pl.when(sends(way, step))
                def _():
                    passing(way, step, i, me - sign * step).start()

        if step == 0:
            for copy in kept:
                copy.start()
        for i in range(arrays):
            for way in (0, 1):
                sign = 1 if way == 0 else -1

                @pl.when(receives(way, step))
                def _():
                    passing(way, step, i, me - sign * (step + 1)).wait_recv()

    for copy in kept:
        copy.wait()
    for step in range(count - 1):
        for i in range(arrays):
            for way in (0, 1):
                sign = 1 if way == 0 else -1

                @pl.when(sends(way, step))
                def _():
                    passing(way, step, i, me - sign * step).wait_send()


def line_gather(*blocks, number, stacked=0):
    count = lax.axis_size("ctx")
    arrays = len(blocks)
    shapes = [(count * block.shape[0],) + block.shape[1:] for block in blocks]
    types = [block.dtype for block in blocks]
    if stacked:
        shapes = [(stacked,) + shapes[0]] + shapes[stacked:]
        types = types[:1] + types[stacked:]
    return pl.pallas_call(
        functools.partial(gather_kernel, count, arrays, stacked),
        in_specs=[pl.BlockSpec(memory_space=pl.ANY)] * arrays,
        out_specs=[pl.BlockSpec(memory_space=pl.ANY)] * len(shapes),
        out_shape=[jax.ShapeDtypeStruct(*pair) for pair in zip(shapes, types)],
        scratch_shapes=[
            pltpu.SemaphoreType.DMA((2, count - 1, arrays)),
            pltpu.SemaphoreType.DMA((2, count - 1, arrays)),
            pltpu.SemaphoreType.DMA((arrays,)),
        ],
        compiler_params=pltpu.CompilerParams(collective_id=number, has_side_effects=True),
        cost_estimate=pl.CostEstimate(flops=0, bytes_accessed=200 * 2**20, transcendentals=0),
    )(*blocks)


def expert_kernel(
    rows_ref,
    grad_ref,
    gate_ref,
    up_ref,
    down_ref,
    active_ref,
    gate_grad_ref,
    up_grad_ref,
    out_ref,
    back_ref,
    value_ref,
):
    gate = along(rows_ref[...], gate_ref[...])
    upper = along(rows_ref[...], up_ref[...])
    active_grad = across(grad_ref[...], down_ref[...])
    sigma = jax.nn.sigmoid(gate)
    swish = gate * sigma
    active = (swish * upper).astype(jnp.bfloat16)
    active_ref[...] = active
    out_ref[...] = along(active, down_ref[...]).astype(jnp.bfloat16)
    gate_grad = (active_grad * upper * sigma * (1.0 + gate * (1.0 - sigma))).astype(jnp.bfloat16)
    up_grad = (active_grad * swish).astype(jnp.bfloat16)
    gate_grad_ref[...] = gate_grad
    up_grad_ref[...] = up_grad
    value_ref[...] = jnp.sum(active_grad * active.astype(jnp.float32), -1, keepdims=True)
    back_ref[...] = (across(gate_grad, gate_ref[...]) + across(up_grad, up_ref[...])).astype(
        jnp.bfloat16
    )


def run_expert(rows, grad, gate, up, down, step):
    sources, block, width = rows.shape
    units = gate.shape[1]
    total = sources * block
    wide = pl.BlockSpec((block, width), lambda i: (i, 0))
    narrow = pl.BlockSpec((block, units), lambda i: (i, 0))

    def whole(shape):
        return pl.BlockSpec(shape, lambda i: (0, 0), pipeline_mode=pl.Buffered(1))

    low = jax.ShapeDtypeStruct((total, units), jnp.bfloat16)
    full = jax.ShapeDtypeStruct((total, width), jnp.bfloat16)
    return pl.pallas_call(
        expert_kernel,
        grid=(sources,),
        in_specs=[
            pl.BlockSpec((None, block, width), lambda i: (i, 0, 0)),
            pl.BlockSpec((None, None, block, width), lambda i: (i, step, 0, 0)),
            whole(gate.shape),
            whole(up.shape),
            whole(down.shape),
        ],
        out_specs=(narrow, narrow, narrow, wide, wide, pl.BlockSpec((block, 1), lambda i: (i, 0))),
        out_shape=(low, low, low, full, full, jax.ShapeDtypeStruct((total, 1), jnp.float32)),
        compiler_params=pltpu.CompilerParams(vmem_limit_bytes=VMEM_BYTES),
        cost_estimate=SMALL,
    )(rows, grad, gate, up, down)


def plane_tables(routes_all, weights_all, first, planned):
    hit = routes_all[..., None] == first + jnp.arange(planned, dtype=jnp.int32)
    named = jnp.any(hit, -2)
    weight = jnp.sum(jnp.where(hit, weights_all[..., None], 0.0), -2)
    rows = routes_all.shape[-2]
    earlier = (
        jnp.arange(rows, dtype=jnp.int32)[:, None] > jnp.arange(rows, dtype=jnp.int32)[None, :]
    ).astype(jnp.bfloat16)
    rank = jnp.einsum(
        "tu,cuj->ctj", earlier, named.astype(jnp.bfloat16), preferred_element_type=jnp.float32
    ).astype(jnp.int32)
    place = jnp.where(named, rank, -1)
    return place.transpose(0, 2, 1), weight.transpose(0, 2, 1)


def pick_kernel(planes, place_ref, weight_ref, rows_ref, out_ref, weighted):
    capacity = out_ref.shape[2]
    local = rows_ref.shape[0]
    slots = lax.broadcasted_iota(jnp.int32, (capacity, local), 0)
    if capacity % 16 == 0:
        chosen = [place_ref[0, 0, j : j + 1, :] == slots for j in range(planes)]
        picked = jnp.dot(
            jnp.concatenate([jnp.where(c, 1.0, 0.0).astype(jnp.bfloat16) for c in chosen], 0),
            rows_ref[...],
            preferred_element_type=jnp.float32,
        )
        for j in range(planes):
            rows = picked[j * capacity : (j + 1) * capacity]
            if weighted:
                rows = rows * jnp.sum(
                    jnp.where(chosen[j], weight_ref[0, 0, j : j + 1, :], 0.0), -1, keepdims=True
                )
            out_ref[j, 0] = rows.astype(jnp.bfloat16)
        return
    for j in range(planes):
        chosen = place_ref[0, 0, j : j + 1, :] == slots
        picked = jnp.dot(
            jnp.where(chosen, 1.0, 0.0).astype(jnp.bfloat16),
            rows_ref[...],
            preferred_element_type=jnp.float32,
        )
        if weighted:
            picked = picked * jnp.sum(
                jnp.where(chosen, weight_ref[0, 0, j : j + 1, :], 0.0), -1, keepdims=True
            )
        out_ref[j, 0] = picked.astype(jnp.bfloat16)


def pick_rows(place, weight, blocks, capacity, weighted):
    count, planned, local = place.shape
    width = blocks.shape[1]
    part = 4 if planned % 4 == 0 else planned
    shape = (count, planned // part, part, local)
    return pl.pallas_call(
        functools.partial(pick_kernel, part, weighted=weighted),
        grid=(count, planned // part),
        in_specs=[
            pl.BlockSpec((1, 1, part, local), lambda c, g: (c, g, 0, 0)),
            pl.BlockSpec((1, 1, part, local), lambda c, g: (c, g, 0, 0)),
            pl.BlockSpec((local, width), lambda c, g: (c, 0)),
        ],
        out_specs=pl.BlockSpec((part, 1, capacity, width), lambda c, g: (g, c, 0, 0)),
        out_shape=jax.ShapeDtypeStruct((planned, count, capacity, width), jnp.bfloat16),
        compiler_params=pltpu.CompilerParams(vmem_limit_bytes=VMEM_BYTES),
        cost_estimate=SMALL,
    )(place.reshape(shape), weight.reshape(shape), blocks)


def weight_kernel(steps, micro, *refs):
    rows, (grads_ref,) = refs[:micro], refs[micro : micro + 1]
    actives, gates, ups = (refs[micro * i + 1 : micro * i + 1 + micro] for i in (1, 2, 3))
    outs = refs[4 * micro + 1 : 4 * micro + 4]
    sums, sem = refs[4 * micro + 4 : 4 * micro + 7], refs[-1]
    step = pl.program_id(0)

    def flat(ref):
        count, block, width = ref.shape
        return ref[...].reshape(count * block, width)

    def add(which, fresh):
        x = flat(rows[which])
        for sum_ref, left, right in (
            (sums[0], x, gates[which][...]),
            (sums[1], x, ups[which][...]),
            (sums[2], actives[which][...], flat(grads_ref)),
        ):
            term = lax.dot_general(
                left, right, (((0,), (0,)), ((), ())), preferred_element_type=jnp.float32
            )
            if fresh:
                sum_ref[0] = term
            else:
                sum_ref[0] += term

    pl.when(step == 0)(lambda: add(0, True))
    pl.when((step > 0) & (step < steps))(lambda: add(0, False))
    for which in range(1, micro):
        pl.when((step >= which * steps) & (step < (which + 1) * steps))(
            functools.partial(add, which, False)
        )

    @pl.when(step == micro * steps - 1)
    def _():
        copies = [pltpu.make_async_copy(sums[i], outs[i], sem.at[i]) for i in range(3)]
        for copy in copies:
            copy.start()
        for copy in copies:
            copy.wait()


def expert_weight_grads(rows, grads, actives, gates, ups):
    sources, micro, block, width = grads.shape
    units = gates[0].shape[1]
    steps = sources // 2

    def turn(i, which):
        return jnp.clip(i - which * steps, 0, steps - 1)

    def specs(size):
        return [
            pl.BlockSpec((2 * block, size), functools.partial(lambda w, i: (turn(i, w), 0), which))
            for which in range(micro)
        ]

    def row_specs():
        return [
            pl.BlockSpec(
                (2, block, width), functools.partial(lambda w, i: (turn(i, w), 0, 0), which)
            )
            for which in range(micro)
        ]

    shapes = [(1, width, units), (1, width, units), (1, units, width)]
    return pl.pallas_call(
        functools.partial(weight_kernel, steps, micro),
        grid=(micro * steps,),
        in_specs=row_specs()
        + [
            pl.BlockSpec(
                (2, None, block, width), lambda i: (lax.rem(i, steps), lax.div(i, steps), 0, 0)
            )
        ]
        + specs(units) * 3,
        out_specs=[pl.BlockSpec(memory_space=pl.ANY)] * 3,
        out_shape=[jax.ShapeDtypeStruct(shape, jnp.float32) for shape in shapes],
        scratch_shapes=[pltpu.VMEM(shape, jnp.float32) for shape in shapes]
        + [pltpu.SemaphoreType.DMA((3,))],
        compiler_params=pltpu.CompilerParams(vmem_limit_bytes=VMEM_BYTES),
        cost_estimate=SMALL,
    )(*rows, grads, *actives, *gates, *ups)


def fill_mask(place_ref, mask_ref):
    base, bound = place_ref[0], place_ref[1]
    keys, rows = mask_ref.shape
    key_at = lax.broadcasted_iota(jnp.int32, (keys, rows), 0)
    row_at = lax.broadcasted_iota(jnp.int32, (keys, rows), 1) + base
    least = jnp.where(row_at >= bound, bound, 0)
    mask_ref[...] = jnp.where((key_at <= row_at) & (key_at >= least), 0.0, MASKED)


def head_queries(raw, gain, cosine, sine):
    scale = lax.rsqrt(jnp.mean(raw * raw, -1, keepdims=True) + EPSILON)
    value = raw * scale * gain
    turned = value * cosine + pltpu.roll(value, value.shape[-1] // 2, 1) * sine
    return turned.astype(jnp.bfloat16), scale


def across(a, b):
    return lax.dot_general(a, b, (((1,), (1,)), ((), ())), preferred_element_type=jnp.float32)


def along(a, b):
    return jnp.dot(a, b, preferred_element_type=jnp.float32)


def keyed(both_ref, width, which):
    count, rows = both_ref.shape[:2]
    return both_ref[:, :, which * width : (which + 1) * width].reshape(count * rows, width)


def attend_kernel(
    per, factor, place_ref, raw_ref, both_ref, gain_ref, cos_ref, sin_ref, *rest
):
    out_ref, mask_ref, turned_ref = rest[-3:]
    width = gain_ref.shape[1]
    group_step, step = pl.program_id(0), pl.program_id(1)

    @pl.when((group_step == 0) & (step == 0))
    def _():
        fill_mask(place_ref, mask_ref)

    @pl.when(step == 0)
    def _():
        turned_ref[...] = keyed(both_ref, width, 1).T

    for head in range(per):
        columns = slice(head * width, (head + 1) * width)
        queries, _ = head_queries(raw_ref[:, columns], gain_ref[...], cos_ref[...], sin_ref[...])
        chances = jnp.exp2(across(keyed(both_ref, width, 0), queries) * factor + mask_ref[...])
        total = jnp.sum(chances, 0, keepdims=True)
        result = along(turned_ref[...], chances.astype(jnp.bfloat16)) * (1.0 / total)
        out_ref[:, columns] = result.T.astype(jnp.bfloat16)


class Exchange:
    def __init__(self, axis, rows_ref, out_ref, send_sem, recv_sem, own_sem):
        self.axis, self.count = axis, rows_ref.shape[0]
        self.rows_ref, self.out_ref = rows_ref, out_ref
        self.send_sem, self.recv_sem, self.own_sem = send_sem, recv_sem, own_sem
        self.me = lax.axis_index(axis)

    @staticmethod
    def scratch(count):
        return [
            pltpu.SemaphoreType.DMA((count,)),
            pltpu.SemaphoreType.DMA((count,)),
            pltpu.SemaphoreType.DMA,
        ]

    def passing(self, k, part):
        return pltpu.make_async_remote_copy(
            src_ref=self.rows_ref.at[lax.rem(self.me + k, self.count)],
            dst_ref=self.out_ref.at[part],
            send_sem=self.send_sem.at[k],
            recv_sem=self.recv_sem.at[k],
            device_id={self.axis: lax.rem(self.me + k, self.count)},
            device_id_type=pl.DeviceIdType.MESH,
        )

    def kept(self):
        return pltpu.make_async_copy(
            self.rows_ref.at[self.me], self.out_ref.at[self.me], self.own_sem
        )

    def begin(self):
        for k in range(1, self.count):
            self.passing(k, self.me).start()
        self.kept().start()

    def finish(self):
        self.kept().wait()
        for k in range(1, self.count):
            self.passing(k, lax.rem(self.me + self.count - k, self.count)).wait_recv()
        for k in range(1, self.count):
            self.passing(k, self.me).wait_send()


def greet(**counts):
    barrier = pltpu.get_barrier_semaphore()
    for axis, count in counts.items():
        me = lax.axis_index(axis)
        for k in range(1, count):
            pl.semaphore_signal(
                barrier,
                inc=1,
                device_id={axis: lax.rem(me + k, count)},
                device_id_type=pl.DeviceIdType.MESH,
            )
    pl.semaphore_wait(barrier, sum(counts.values()) - len(counts))


class RowExchange:
    def __init__(self, ring, held_ref, out_ref, send_sem, recv_sem, own_sem):
        self.ring, self.held_ref, self.out_ref = ring, held_ref, out_ref
        self.send_sem, self.recv_sem, self.own_sem = send_sem, recv_sem, own_sem
        self.me = lax.axis_index("ctx")
        self.rows = out_ref.shape[2]

    @staticmethod
    def scratch(ring, groups):
        return [
            pltpu.SemaphoreType.DMA((groups, ring)),
            pltpu.SemaphoreType.DMA((groups, ring)),
            pltpu.SemaphoreType.DMA((groups,)),
        ]

    def held(self, group, at):
        return self.held_ref.at[group, pl.ds(at * self.rows, self.rows)]

    def passing(self, group, k, part):
        to = lax.rem(self.me + k, self.ring)
        return pltpu.make_async_remote_copy(
            src_ref=self.held(group, to),
            dst_ref=self.out_ref.at[part, group],
            send_sem=self.send_sem.at[group, k],
            recv_sem=self.recv_sem.at[group, k],
            device_id={"ctx": to},
            device_id_type=pl.DeviceIdType.MESH,
        )

    def kept(self, group):
        return pltpu.make_async_copy(
            self.held(group, self.me), self.out_ref.at[self.me, group], self.own_sem.at[group]
        )

    def begin(self, group):
        for k in range(1, self.ring):
            self.passing(group, k, self.me).start()
        self.kept(group).start()

    def finish(self):
        for group in range(self.out_ref.shape[1]):
            self.kept(group).wait()
            for k in range(1, self.ring):
                self.passing(group, k, lax.rem(self.me + self.ring - k, self.ring)).wait_recv()
            for k in range(1, self.ring):
                self.passing(group, k, self.me).wait_send()


def attend_back_kernel(
    per,
    steps,
    factor,
    scale,
    count,
    ring,
    extra_axis,
    place_ref,
    raw_ref,
    feed_grad_ref,
    middle_ref,
    out_grad_ref,
    norm_ref,
    weight_ref,
    both_ref,
    pair_raw_ref,
    gain_ref,
    key_gain_ref,
    cos_ref,
    sin_ref,
    rows_ref,
    extra_ref,
    raw_grad_ref,
    pair_grad_ref,
    gain_grad_ref,
    branch_ref,
    middle_grad_ref,
    norm_grad_ref,
    moved_ref,
    extra_moved_ref,
    mask_ref,
    turned_ref,
    sums_ref,
    held_ref,
    landed_ref,
    *sems,
):
    width = gain_ref.shape[1]
    group_step, step = pl.program_id(0), pl.program_id(1)
    moving = Exchange("exp", rows_ref, moved_ref, *sems[:3])
    extra_moving = Exchange(extra_axis, extra_ref, extra_moved_ref, *sems[3:6])
    landing = RowExchange(ring, held_ref, landed_ref, *sems[6:])

    @pl.when((group_step == 0) & (step == 0))
    def _():
        greet(exp=count, ctx=ring)
        moving.begin()
        extra_moving.begin()
        fill_mask(place_ref, mask_ref)
        gain_grad_ref[...] = jnp.zeros_like(gain_grad_ref)
        norm_grad_ref[...] = jnp.zeros_like(norm_grad_ref)
        rows = middle_ref.shape[0]
        for at in range(0, rows, 64):
            part = slice(at, at + 64)
            value, grad = middle_ref[part, :], feed_grad_ref[part, :].astype(jnp.float32)
            norm = lax.rsqrt(jnp.mean(value * value, -1, keepdims=True) + EPSILON)
            first, gain_part = norm_back(value, norm, norm_ref[...], grad)
            total = out_grad_ref[part, :].astype(jnp.float32) + first
            middle_grad_ref[part, :] = total
            branch_ref[part, :] = total.astype(jnp.bfloat16)
            norm_grad_ref[0:1, :] += jnp.sum(gain_part, 0, keepdims=True)

    @pl.when(step == 0)
    def _():
        turned_ref[...] = keyed(both_ref, width, 0).T
        sums_ref[...] = jnp.zeros_like(sums_ref)

    def turned_back(grad, raw, norm, gain, row):
        back = grad * cos_ref[...] - pltpu.roll(grad, width // 2, 1) * sin_ref[...]
        inner = back * gain
        gain_grad_ref[row : row + 1, :] += jnp.sum(back * raw * norm, 0, keepdims=True)
        return (
            norm * inner - raw * (norm * norm * norm) * jnp.mean(inner * raw, -1, keepdims=True)
        ).astype(jnp.bfloat16)

    grads = across(branch_ref[...], weight_ref[...]).astype(jnp.bfloat16)
    for head in range(per):
        columns = slice(head * width, (head + 1) * width)
        raw = raw_ref[:, columns]
        queries, norm = head_queries(raw, gain_ref[...], cos_ref[...], sin_ref[...])
        grad = grads[:, columns]
        chances = jnp.exp2(across(keyed(both_ref, width, 0), queries) * factor + mask_ref[...])
        chances = chances * (1.0 / jnp.sum(chances, 0, keepdims=True))
        chance_grad = across(keyed(both_ref, width, 1), grad)
        mean = jnp.sum(chances * chance_grad, 0, keepdims=True)
        score_grad = (chances * (chance_grad - mean)).astype(jnp.bfloat16)
        sums_ref[:, :width] += along(score_grad, queries)
        sums_ref[:, width:] += along(chances.astype(jnp.bfloat16), grad)
        query_grad = (along(turned_ref[...], score_grad) * scale).astype(jnp.bfloat16)
        raw_grad_ref[:, columns] = turned_back(
            query_grad.astype(jnp.float32).T, raw, norm, gain_ref[...], 0
        )

    @pl.when(step == steps - 1)
    def _():
        held_ref[group_step, :, :width] = (sums_ref[:, :width] * scale).astype(jnp.bfloat16)
        held_ref[group_step, :, width:] = sums_ref[:, width:].astype(jnp.bfloat16)
        landing.begin(group_step)

    @pl.when((group_step == pl.num_programs(0) - 1) & (step == steps - 1))
    def _():
        landing.finish()
        for group in range(landed_ref.shape[1]):
            total = landed_ref[0, group].astype(jnp.float32)
            for other in range(1, ring):
                total += landed_ref[other, group].astype(jnp.float32)
            total = total.astype(jnp.bfloat16)
            start = 2 * group * width
            raw = pair_raw_ref[:, start : start + width]
            norm = lax.rsqrt(jnp.mean(raw * raw, -1, keepdims=True) + EPSILON)
            pair_grad_ref[:, start : start + width] = turned_back(
                total[:, :width].astype(jnp.float32), raw, norm, key_gain_ref[...], 1
            )
            pair_grad_ref[:, start + width : start + 2 * width] = total[:, width:]
        extra_moving.finish()
        moving.finish()


def attention_specs(raw, both, width, rows, step, per):
    kv_heads = both.shape[2] // (2 * width)
    heads = raw.shape[1] // width - 2 * kv_heads
    steps = heads // kv_heads // per
    count = both.shape[0]
    keys = count * rows
    wide = pl.BlockSpec((rows, per * width), lambda g, j: (0, g * steps + j))
    specs = dict(
        place=pl.BlockSpec(memory_space=pltpu.SMEM),
        raw=pl.BlockSpec((rows, per * width), lambda g, j: (step, g * steps + j)),
        heads=wide,
        both=pl.BlockSpec((count, rows, 2 * width), lambda g, j: (0, 0, g)),
        gain=pl.BlockSpec((1, width), lambda g, j: (0, 0)),
        table=pl.BlockSpec((rows, width), lambda g, j: (0, 0)),
    )
    params = pltpu.CompilerParams(vmem_limit_bytes=VMEM_BYTES)
    work = 2 * heads * rows * keys * width
    return kv_heads, heads, steps, keys, specs, params, work


def attend(raw, both, gain, cosine, sine, place, step, waits, per=2):
    rows, width = cosine.shape
    kv_heads, heads, steps, keys, specs, params, work = attention_specs(
        raw, both, width, rows, step, per
    )
    return pl.pallas_call(
        functools.partial(attend_kernel, per, width ** (-0.5) * math.log2(math.e)),
        grid=(kv_heads, steps),
        in_specs=[specs[k] for k in ("place", "raw", "both", "gain", "table", "table")]
        + [pl.BlockSpec(memory_space=pl.ANY)] * len(waits),
        out_specs=specs["heads"],
        out_shape=jax.ShapeDtypeStruct((rows, heads * width), jnp.bfloat16),
        scratch_shapes=[
            pltpu.VMEM((keys, rows), jnp.float32),
            pltpu.VMEM((width, keys), jnp.bfloat16),
        ],
        compiler_params=params,
        cost_estimate=SMALL,
    )(place, raw, both, gain, cosine, sine, *waits)


def attend_back(
    raw,
    feed_grad,
    middle,
    out_grad,
    norm,
    weight,
    both,
    gain,
    key_gain,
    cosine,
    sine,
    place,
    step,
    rows_out,
    extra,
    extra_axis,
    per=2,
):
    rows, width = cosine.shape
    kv_heads, heads, steps, keys, specs, params, work = attention_specs(
        raw, both, width, rows, step, per
    )
    count, ring = rows_out.shape[0], both.shape[0]
    anywhere = pl.BlockSpec(memory_space=pl.ANY)
    pairs = 2 * kv_heads * width
    pair_place = heads * width // pairs
    return pl.pallas_call(
        functools.partial(
            attend_back_kernel,
            per,
            steps,
            width ** (-0.5) * math.log2(math.e),
            width ** (-0.5),
            count,
            ring,
            extra_axis,
        ),
        grid=(kv_heads, steps),
        in_specs=[
            specs["place"],
            specs["raw"],
            pl.BlockSpec(middle.shape, lambda g, j: (0, 0)),
            pl.BlockSpec(middle.shape, lambda g, j: (0, 0)),
            pl.BlockSpec(middle.shape, lambda g, j: (0, 0)),
            pl.BlockSpec(norm.shape, lambda g, j: (0, 0)),
            pl.BlockSpec((per * width, weight.shape[1]), lambda g, j: (g * steps + j, 0)),
            specs["both"],
            pl.BlockSpec((rows, pairs), lambda g, j: (step, pair_place)),
            specs["gain"],
            specs["gain"],
            specs["table"],
            specs["table"],
            anywhere,
            anywhere,
        ],
        out_specs=(
            specs["heads"],
            pl.BlockSpec((rows, pairs), lambda g, j: (0, 0)),
            pl.BlockSpec((8, width), lambda g, j: (0, 0)),
            pl.BlockSpec(middle.shape, lambda g, j: (0, 0)),
            pl.BlockSpec(middle.shape, lambda g, j: (0, 0)),
            pl.BlockSpec((8, middle.shape[1]), lambda g, j: (0, 0)),
            anywhere,
            anywhere,
        ),
        out_shape=(
            jax.ShapeDtypeStruct((rows, heads * width), jnp.bfloat16),
            jax.ShapeDtypeStruct((rows, pairs), jnp.bfloat16),
            jax.ShapeDtypeStruct((8, width), jnp.float32),
            jax.ShapeDtypeStruct(middle.shape, jnp.bfloat16),
            jax.ShapeDtypeStruct(middle.shape, jnp.float32),
            jax.ShapeDtypeStruct((8, middle.shape[1]), jnp.float32),
            jax.ShapeDtypeStruct(rows_out.shape, rows_out.dtype),
            jax.ShapeDtypeStruct(extra.shape, extra.dtype),
        ),
        scratch_shapes=[
            pltpu.VMEM((keys, rows), jnp.float32),
            pltpu.VMEM((width, keys), jnp.bfloat16),
            pltpu.VMEM((keys, 2 * width), jnp.float32),
            pltpu.VMEM((kv_heads, keys, 2 * width), jnp.bfloat16),
            pltpu.VMEM((ring, kv_heads, rows, 2 * width), jnp.bfloat16),
        ]
        + Exchange.scratch(count)
        + Exchange.scratch(extra.shape[0])
        + RowExchange.scratch(ring, kv_heads),
        compiler_params=pltpu.CompilerParams(
            vmem_limit_bytes=VMEM_BYTES, collective_id=1 + step, has_side_effects=True
        ),
        cost_estimate=SMALL,
    )(
        place,
        raw,
        feed_grad,
        middle,
        out_grad,
        norm,
        weight,
        both,
        raw,
        gain,
        key_gain,
        cosine,
        sine,
        rows_out,
        extra,
    )


def combine_kernel(place_ref, weight_ref, back_ref, out_ref, *, weighted):
    experts, _, capacity, width = back_ref.shape
    local = out_ref.shape[0]
    slots = lax.broadcasted_iota(jnp.int32, (capacity, local), 0)
    factors = []
    for j in range(experts):
        value = weight_ref[0, j : j + 1, :] if weighted else 1.0
        chosen = place_ref[0, j : j + 1, :] == slots
        factors.append(jnp.where(chosen, value, 0.0).astype(jnp.bfloat16))
    out_ref[...] = lax.dot_general(
        jnp.concatenate(factors, 0),
        back_ref[...].reshape(experts * capacity, width),
        (((0,), (0,)), ((), ())),
        preferred_element_type=jnp.float32,
    ).astype(jnp.bfloat16)


def combine_rows(place, weight, back, weighted):
    count, planned, local = place.shape
    capacity, width = back.shape[2:]
    return pl.pallas_call(
        functools.partial(combine_kernel, weighted=weighted),
        grid=(count,),
        in_specs=[
            pl.BlockSpec((1, planned, local), lambda c: (c, 0, 0)),
            pl.BlockSpec((1, planned, local), lambda c: (c, 0, 0)),
            pl.BlockSpec((planned, 1, capacity, width), lambda c: (0, c, 0, 0)),
        ],
        out_specs=pl.BlockSpec((local, width), lambda c: (c, 0)),
        out_shape=jax.ShapeDtypeStruct((count * local, width), jnp.bfloat16),
        compiler_params=pltpu.CompilerParams(vmem_limit_bytes=VMEM_BYTES),
        cost_estimate=SMALL,
    )(place, weight, back)


class GradSums:
    def __init__(self, ring, micro, head_dim, sizes, refs):
        self.ring, self.micro, self.sizes = ring, micro, sizes
        self.head_dim = head_dim
        self.attended, self.hidden = refs[:micro], refs[micro]
        refs = refs[micro + 1 :]
        self.branch, self.query, self.pair = (
            refs[i * micro : (i + 1) * micro] for i in range(3)
        )
        self.weight = refs[3 * micro]
        self.out = refs[3 * micro + 1 : 3 * micro + 5]
        self.hidden_grad = refs[3 * micro + 5]
        self.far = refs[3 * micro + 6 : 3 * micro + 9]
        scratch = refs[3 * micro + 9 :]
        self.left_v, self.right_v = scratch[:2], scratch[2:4]
        self.part, self.first, self.second, self.last = (
            scratch[4 + 2 * i : 6 + 2 * i] for i in range(4)
        )
        (
            self.left_sem,
            self.far_sem,
            self.load_sem,
            self.first_sem,
            self.second_sem,
            self.last_sem,
            self.weight_sem,
        ) = scratch[12:]
        e = lax.axis_index("exp")
        self.core, self.y, self.x = lax.rem(e, 2), lax.div(e, 4), lax.rem(lax.div(e, 2), 2)
        self.partner = e + 1 - 2 * self.core
        self.across_x, self.across_y = e + 2 - 4 * self.x, e + 4 - 8 * self.y
        self.z = lax.axis_index("ctx")
        self.order = [
            (kind, chunk) for kind, size in enumerate(sizes) for chunk in range(size[2] // size[3])
        ]

    @staticmethod
    def scratch(ring, micro, sizes):
        chunks = [size[2] // size[3] for size in sizes]
        total = sum(chunks)
        shapes = [pltpu.VMEM((4, size[0], size[1]), jnp.bfloat16) for size in sizes]
        shapes += [pltpu.VMEM((2, size[0], size[3]), jnp.bfloat16) for size in sizes]
        for lead, share in (((4,), 1), ((2,), 1), ((), 1), ((ring,), ring)):
            for size, count in zip(sizes, chunks):
                shapes.append(
                    pltpu.VMEM((count,) + lead + (size[1] // share, size[3]), jnp.bfloat16)
                )
        shapes += [
            pltpu.SemaphoreType.DMA((3, micro + 1, 4, ring)),
            pltpu.SemaphoreType.DMA((2, 3, micro)),
            pltpu.SemaphoreType.DMA((total, 2, micro)),
            pltpu.SemaphoreType.DMA((2, total, 2)),
            pltpu.SemaphoreType.DMA((2, total)),
            pltpu.SemaphoreType.DMA((2, total, ring)),
            pltpu.SemaphoreType.DMA((4,)),
        ]
        return shapes

    def weight_loads(self, chunk):
        _, high, wide = self.left_v[0].shape
        return [
            pltpu.make_async_copy(
                self.weight.at[pl.ds(r * high, high), pl.ds(chunk * wide, wide)],
                self.left_v[0].at[2 * (chunk % 2) + r],
                self.weight_sem.at[2 * (chunk % 2) + r],
            )
            for r in (0, 1)
        ]

    def add_hidden(self, chunk):
        high = self.left_v[0].shape[1]
        half = self.sizes[1][0] // 2
        for copy in self.weight_loads(chunk):
            copy.wait()
        for r in (0, 1):
            columns = slice(r * high, (r + 1) * high)
            term = across(
                self.right_v[1][chunk % 2, :half], self.left_v[0][2 * (chunk % 2) + r]
            )
            if chunk == 0:
                self.hidden_grad[:, columns] = term
            else:
                self.hidden_grad[:, columns] += term

    def to_partner(self, src, dst, send_sem, recv_sem):
        return pltpu.make_async_remote_copy(
            src_ref=src,
            dst_ref=dst,
            send_sem=send_sem,
            recv_sem=recv_sem,
            device_id={"exp": self.partner},
            device_id_type=pl.DeviceIdType.MESH,
        )

    def left_copies(self, kind):
        half = self.sizes[kind][0] // 2
        own, sent = [], []
        if kind == 1:
            place = (self.micro, 0, 0)
            own.append(
                pltpu.make_async_copy(
                    self.hidden.at[self.core],
                    self.left_v[1].at[:, pl.ds(0, half)],
                    self.left_sem.at[(0,) + place],
                )
            )
            sent.append(
                self.to_partner(
                    self.hidden.at[1 - self.core],
                    self.left_v[1].at[:, pl.ds(half, half)],
                    self.left_sem.at[(1,) + place],
                    self.left_sem.at[(2,) + place],
                )
            )
            return own, sent
        share = self.sizes[kind][1] // self.ring
        rows = half // self.micro
        for m in range(self.micro):
            for piece in range(4):
                for c in range(self.ring):

                    def columns(core):
                        block = c * 8 + piece * 2 + core
                        return self.attended[m].at[
                            :, pl.ds(pl.multiple_of(block * share, share), share)
                        ]

                    def place(base):
                        return self.left_v[0].at[
                            piece, pl.ds(base + m * rows, rows), pl.ds(c * share, share)
                        ]

                    own.append(
                        pltpu.make_async_copy(
                            columns(self.core), place(0), self.left_sem.at[0, m, piece, c]
                        )
                    )
                    sent.append(
                        self.to_partner(
                            columns(1 - self.core),
                            place(half),
                            self.left_sem.at[1, m, piece, c],
                            self.left_sem.at[2, m, piece, c],
                        )
                    )
        return own, sent

    def right_copies(self, which):
        near = (self.branch, self.query, self.pair)[which]
        return [
            self.to_partner(
                near[m],
                self.far[which].at[m],
                self.far_sem.at[0, which, m],
                self.far_sem.at[1, which, m],
            )
            for m in range(self.micro)
        ]

    def source(self, i):
        kind, chunk = self.order[i]
        wide = self.sizes[kind][3]
        if kind == 0:
            return 0, chunk * wide
        query_width = self.query[0].shape[1]
        if chunk * wide < query_width:
            return 1, chunk * wide
        return 2, chunk * wide - query_width

    def loads(self, i, far):
        kind, chunk = self.order[i]
        which, start = self.source(i)
        wide = self.sizes[kind][3]
        half = self.sizes[kind][0] // 2
        rows = half // self.micro
        near = (self.branch, self.query, self.pair)[which]
        return [
            pltpu.make_async_copy(
                (self.far[which].at[m] if far else near[m]).at[:, pl.ds(start, wide)],
                self.right_v[kind].at[chunk % 2, pl.ds(far * half + m * rows, rows)],
                self.load_sem.at[i, far, m],
            )
            for m in range(self.micro)
        ]

    def start_loads(self, i):
        which, start = self.source(i)
        for copy in self.loads(i, 0):
            copy.start()
        if start == 0:
            for copy in self.right_copies(which):
                copy.wait_recv()
        for copy in self.loads(i, 1):
            copy.start()

    def x_first(self, i):
        return i % 2 == 0

    def step_first(self, i, k):
        kind, chunk = self.order[i]
        if self.x_first(i):
            piece, to = 2 * k + 1 - self.x, self.across_x
        else:
            piece, to = 2 * (1 - self.y) + k, self.across_y
        return pltpu.make_async_remote_copy(
            src_ref=self.part[kind].at[chunk, piece],
            dst_ref=self.first[kind].at[chunk, k],
            send_sem=self.first_sem.at[0, i, k],
            recv_sem=self.first_sem.at[1, i, k],
            device_id={"exp": to},
            device_id_type=pl.DeviceIdType.MESH,
        )

    def step_second(self, i):
        kind, chunk = self.order[i]
        if self.x_first(i):
            piece, to = 2 * (1 - self.y) + self.x, self.across_y
        else:
            piece, to = 2 * self.y + 1 - self.x, self.across_x
        return pltpu.make_async_remote_copy(
            src_ref=self.part[kind].at[chunk, piece],
            dst_ref=self.second[kind].at[chunk],
            send_sem=self.second_sem.at[0, i],
            recv_sem=self.second_sem.at[1, i],
            device_id={"exp": to},
            device_id_type=pl.DeviceIdType.MESH,
        )

    def mine(self, i):
        kind, chunk = self.order[i]
        return self.part[kind].at[chunk, 2 * self.y + self.x]

    def step_last(self, i, k, slot):
        kind, chunk = self.order[i]
        to = lax.rem(self.z + k, self.ring)
        rows = self.sizes[kind][1] // self.ring
        return pltpu.make_async_remote_copy(
            src_ref=self.mine(i).at[pl.ds(to * rows, rows)],
            dst_ref=self.last[kind].at[chunk, slot],
            send_sem=self.last_sem.at[0, i, k],
            recv_sem=self.last_sem.at[1, i, k],
            device_id={"ctx": to},
            device_id_type=pl.DeviceIdType.MESH,
        )

    def multiply(self, i):
        kind, chunk = self.order[i]
        for far in (0, 1):
            for copy in self.loads(i, far):
                copy.wait()

        def piece(p, carry):
            term = lax.dot_general(
                self.left_v[kind][p],
                self.right_v[kind][chunk % 2],
                (((0,), (0,)), ((), ())),
                preferred_element_type=jnp.float32,
            )
            self.part[kind][chunk, p] = term.astype(jnp.bfloat16)
            return carry

        lax.fori_loop(0, 4, piece, 0)
        for k in range(2):
            self.step_first(i, k).start()

    def add_first(self, i):
        kind, chunk = self.order[i]
        for k in range(2):
            self.step_first(i, k).wait_recv()
        for k in range(2):
            piece = 2 * k + self.x if self.x_first(i) else 2 * self.y + k
            self.part[kind][chunk, piece] = (
                self.part[kind][chunk, piece].astype(jnp.float32)
                + self.first[kind][chunk, k].astype(jnp.float32)
            ).astype(jnp.bfloat16)
        self.step_second(i).start()

    def add_second(self, i):
        kind, chunk = self.order[i]
        self.step_second(i).wait_recv()
        piece = 2 * self.y + self.x
        self.part[kind][chunk, piece] = (
            self.part[kind][chunk, piece].astype(jnp.float32)
            + self.second[kind][chunk].astype(jnp.float32)
        ).astype(jnp.bfloat16)
        for k in range(1, self.ring):
            self.step_last(i, k, k).start()

    def add_last(self, i):
        kind, chunk = self.order[i]
        rows, wide = self.sizes[kind][1] // self.ring, self.sizes[kind][3]
        for k in range(1, self.ring):
            self.step_last(i, k, k).wait_recv()
        total = self.part[kind][
            chunk, 2 * self.y + self.x, pl.ds(pl.multiple_of(self.z * rows, rows), rows), :
        ].astype(jnp.float32)
        for k in range(1, self.ring):
            total += self.last[kind][chunk, k].astype(jnp.float32)
        which, start = self.source(i)
        if which < 2:
            self.out[which][:, start : start + wide] = total
            return
        half = self.head_dim
        for at in range(0, wide, 2 * half):
            to = (start + at) // 2
            self.out[2][:, to : to + half] = total[:, at : at + half]
            self.out[3][:, to : to + half] = total[:, at + half : at + 2 * half]

    def run(self):
        chunks = len(self.order)
        barrier = pltpu.get_barrier_semaphore()
        for other in (self.partner, self.across_x, self.across_y):
            pl.semaphore_signal(
                barrier, inc=1, device_id={"exp": other}, device_id_type=pl.DeviceIdType.MESH
            )
        for k in range(1, self.ring):
            pl.semaphore_signal(
                barrier,
                inc=1,
                device_id={"ctx": lax.rem(self.z + k, self.ring)},
                device_id_type=pl.DeviceIdType.MESH,
            )
        pl.semaphore_wait(barrier, self.ring + 2)
        lefts = [self.left_copies(kind) for kind in (0, 1)]
        rights = [self.right_copies(which) for which in range(3)]
        for copies in (rights[0], lefts[0][1], lefts[0][0]):
            for copy in copies:
                copy.start()
        self.start_loads(0)
        for i in range(chunks + LAGS[-1]):
            if i < chunks:
                if i + 1 < chunks:
                    self.start_loads(i + 1)
                kind, chunk = self.order[i]
                if chunk == 0:
                    for copy in lefts[kind][0]:
                        copy.wait()
                    for copy in lefts[kind][1]:
                        copy.wait_recv()
                self.multiply(i)
                if i == 0:
                    for copies in (rights[1], *lefts[1], rights[2]):
                        for copy in copies:
                            copy.start()
                if kind == 0 and chunk == self.sizes[0][2] // self.sizes[0][3] - 1:
                    for copy in self.weight_loads(0):
                        copy.start()
                if kind == 1:
                    if i + 1 < chunks:
                        for copy in self.weight_loads(chunk + 1):
                            copy.start()
                    self.add_hidden(chunk)
            for lag, stage in zip(LAGS, (self.add_first, self.add_second, self.add_last)):
                if 0 <= i - lag < chunks:
                    stage(i - lag)
        for copies in (lefts[0][1], lefts[1][1], *rights):
            for copy in copies:
                copy.wait_send()
        for i in range(chunks):
            for k in range(2):
                self.step_first(i, k).wait_send()
            self.step_second(i).wait_send()
            for k in range(1, self.ring):
                self.step_last(i, k, k).wait_send()


def grad_sums_kernel(ring, micro, head_dim, sizes, *refs):
    GradSums(ring, micro, head_dim, sizes, refs).run()


def grad_sums(ring, head_dim, attended, hidden, branch, query, pair, weight, number):
    micro, rows = len(attended), attended[0].shape[0]
    tokens = 2 * micro * rows
    sizes = [
        (tokens, attended[0].shape[1] // 8, branch[0].shape[1], 256),
        (tokens, hidden.shape[3], query[0].shape[1] + pair[0].shape[1], 512),
    ]
    anywhere = pl.BlockSpec(memory_space=pl.ANY)
    assert weight.shape[0] == 2 * tokens and sizes[1][3] == sizes[0][1]
    share = sizes[1][1] // ring
    outs = [
        jax.ShapeDtypeStruct(shape, jnp.float32)
        for shape in (
            (sizes[0][1] // ring, sizes[0][2]),
            (share, query[0].shape[1]),
            (share, pair[0].shape[1] // 2),
            (share, pair[0].shape[1] // 2),
            (micro * rows, weight.shape[0]),
        )
    ]
    outs += [
        jax.ShapeDtypeStruct((micro,) + arrays[0].shape, jnp.bfloat16)
        for arrays in (branch, query, pair)
    ]
    return pl.pallas_call(
        functools.partial(grad_sums_kernel, ring, micro, head_dim, sizes),
        in_specs=[anywhere] * (4 * micro + 2),
        out_specs=[pl.BlockSpec(memory_space=pltpu.VMEM)] * 5 + [anywhere] * 3,
        out_shape=outs,
        scratch_shapes=GradSums.scratch(ring, micro, sizes),
        compiler_params=pltpu.CompilerParams(
            vmem_limit_bytes=60 * 2**20, collective_id=number, has_side_effects=True
        ),
        cost_estimate=SMALL,
    )(*attended, hidden, *branch, *query, *pair, weight)[:5]


def per_device(
    tokens,
    routes,
    route_weights,
    bounds,
    norm_attn,
    norm_ffn,
    q_gain,
    k_gain,
    w_q,
    w_k,
    w_v,
    w_o,
    w_gate,
    w_up,
    w_down,
    cotangent,
):
    micro = tokens.shape[0]
    local = tokens.shape[2]
    width = tokens.shape[3]
    head_dim = q_gain.shape[0]
    kv_heads = w_k.shape[1] // head_dim
    top = routes.shape[3]
    ring = lax.axis_size("ctx")
    plane = lax.axis_size("exp")
    assert w_gate.shape[0] == 1
    experts = ring * plane
    capacity = max(2, local * top * 5 // (4 * experts))
    seq_len = local * ring
    query_width = w_q.shape[1]
    pair_width = kv_heads * head_dim
    here = lax.axis_index("ctx")
    base = here * local
    cosine, sine = rope_tables(base + jnp.arange(local, dtype=jnp.int32), head_dim)
    gate_weight, up_weight, down_weight = w_gate[0], w_up[0], w_down[0]

    def dot(a, b):
        return jnp.dot(a, b, preferred_element_type=jnp.float32)

    def dot_t(a, b):
        return jnp.einsum("te,de->td", a, b, preferred_element_type=jnp.float32)

    def t_dot(a, b):
        return jnp.einsum("td,te->de", a, b, preferred_element_type=jnp.float32)

    def paired(keys, values):
        rows = keys.shape[0]
        return jnp.stack(
            [keys.reshape(rows, kv_heads, head_dim), values.reshape(rows, kv_heads, head_dim)], 2
        ).reshape(rows, 2 * pair_width)

    in_weight = lax.all_gather(
        jnp.concatenate([w_q, paired(w_k, w_v)], 1), "exp", axis=0, tiled=True
    )
    out_weight = lax.all_gather(w_o, "exp", axis=0, tiled=True)

    meta = jnp.concatenate([routes[:, 0].astype(jnp.float32), route_weights[:, 0]], -1)
    grads_low = [cotangent[step, 0] for step in range(micro)]
    grad_blocks, meta = line_gather(
        *grads_low, meta.reshape(-1, 128), number=0, stacked=micro
    )
    meta = meta.reshape(ring, micro, local, 2 * top)
    tables = [
        plane_tables(
            meta[:, step, :, :top].astype(jnp.int32), meta[:, step, :, top:], here * plane, plane
        )
        for step in range(micro)
    ]
    slots = jnp.arange(capacity, dtype=jnp.int32)
    chosen = [
        place.transpose(1, 0, 2)[:, :, None, :] == slots[None, None, :, None] for place, _ in tables
    ]

    def exchange(rows):
        return lax.all_to_all(rows, "exp", split_axis=0, concat_axis=0, tiled=True)

    def pick(blocks, step, weighted):
        return pick_rows(*tables[step], blocks, capacity, weighted)

    def combine(back, step, weighted):
        back = back.reshape(plane, ring, capacity, width)
        if capacity % 16 == 0:
            return combine_rows(*tables[step], back, weighted)
        factor = chosen[step]
        if weighted:
            weight = tables[step][1].transpose(1, 0, 2)
            factor = jnp.where(factor, weight[:, :, None, :], 0.0)
        part = jnp.einsum(
            "jcst,jcsd->ctd",
            factor.astype(jnp.bfloat16),
            back,
            preferred_element_type=jnp.float32,
        )
        return part.astype(jnp.bfloat16).reshape(seq_len, width)

    def scatter(part):
        return lax.psum_scatter(part, "ctx", scatter_dimension=0, tiled=True)

    picked = pick_rows(
        jnp.concatenate([place for place, _ in tables]),
        jnp.concatenate([weight for _, weight in tables]),
        grad_blocks.reshape(micro * seq_len, width),
        capacity,
        True,
    )
    incoming = exchange(picked.reshape(plane, micro * ring * capacity, width)).reshape(
        plane, micro, ring * capacity, width
    )

    rows = tokens[:, 0].astype(jnp.float32).reshape(micro * local, width)
    hidden, first_scale = norm_rows(rows, norm_attn)
    hidden = after(hidden.astype(jnp.bfloat16), picked)
    raw = dot(hidden, in_weight)
    hidden_parts = hidden.reshape(-1, ring, plane // 2, 2, width // experts)
    hidden_parts = hidden_parts.transpose(3, 2, 0, 1, 4).reshape(
        2, plane // 2, micro * local, ring * width // experts
    )
    pair_raw = raw[:, query_width:].reshape(micro * local, kv_heads, 2, head_dim)
    key_raw = pair_raw[:, :, 0]
    key_normed, key_scale = norm_rows(key_raw, k_gain)
    key_cos = jnp.tile(cosine, (micro, 1))[:, None, :]
    key_sin = jnp.tile(sine, (micro, 1))[:, None, :]
    keys = (key_normed * key_cos + swap_halves(key_normed) * key_sin).astype(jnp.bfloat16)
    pairs = jnp.stack([keys, pair_raw[:, :, 1].astype(jnp.bfloat16)], 2).reshape(
        micro * local, 2 * pair_width
    )
    gain_row = q_gain[None, :]
    both = list(line_gather(pairs[:local], number=3))
    both += [
        lax.all_gather(
            after(pairs[step * local : (step + 1) * local], both[0]), "ctx", axis=0, tiled=True
        )
        for step in range(1, micro)
    ]
    both = [gathered.reshape(ring, local, 2 * pair_width) for gathered in both]
    places, attended, middles, feeds, scales = [], [], [], [], []
    for step in range(micro):
        part = slice(step * local, (step + 1) * local)
        places.append(jnp.stack([base, bounds[step, 0]]).astype(jnp.int32))
        attended.append(
            attend(raw, both[step], gain_row, cosine, sine, places[step], step, feeds[-1:])
        )
        middles.append(rows[part] + dot(attended[step], out_weight))
        feed_in, second_scale = norm_rows(middles[step], norm_ffn)
        feeds.append(feed_in.astype(jnp.bfloat16))
        scales.append(second_scale)
    feed_blocks = [lax.all_gather(feed, "ctx", axis=0, tiled=True) for feed in feeds]

    def slotted(rows):
        return rows.reshape(plane, ring * capacity, width)

    received = []
    waits = (incoming,)
    feed_blocks[0] = after(feed_blocks[0], feeds[-1])
    for step in range(micro):
        picked = slotted(pick(feed_blocks[step], step, False))
        received.append(exchange(after(picked, *waits)))
        waits = (received[-1], hidden_parts)

    active, gate_grad, up_grad, produced, backs, pair_values = [], [], [], [], [], []
    for step in range(micro):
        parts = run_expert(received[step], incoming, gate_weight, up_weight, down_weight, step)
        for held, item in zip((active, gate_grad, up_grad, produced, backs, pair_values), parts):
            held.append(item)

    returned = []
    last = received[-1]
    for step in range(micro):
        returned.append(exchange(after(slotted(backs[step]), last)))
        last = returned[-1]
    gate_term, up_term, down_term = expert_weight_grads(
        received, incoming, active, gate_grad, up_grad
    )

    sums = jnp.stack([value.reshape(plane, ring * capacity) for value in pair_values], 1)
    sums = sums.reshape(plane, -1)
    spare = -sums.shape[1] % 1024
    extra = jnp.pad(sums, ((0, 0), (0, spare))).reshape(plane, -1, 128)

    branches, raw_grads, pair_grads = [], [], []
    middle_grads, gain_list, results = [], [], []
    waits = ()
    for step in range(micro):
        if step > 0:
            own_feed_grad = after(feed_grad, *waits)
        else:
            own_feed_grad = scatter(combine(after(returned[0], active[-1]), 0, False))
        if step == 0:
            returned[1] = after(returned[1], down_term)
            part_sums = combine(returned[1], 1, False)
            feed_grad = scatter(part_sums)
            waits = (part_sums,)
        raw_grad, pair_grad, gain_part, branch, middle_grad, norm_part, result, extra = attend_back(
            raw,
            own_feed_grad,
            middles[step],
            grads_low[step],
            norm_ffn[None, :],
            out_weight,
            both[step],
            gain_row,
            k_gain[None, :],
            cosine,
            sine,
            places[step],
            step,
            after(slotted(produced[step]), *waits),
            extra,
            ("exp", "ctx")[min(step, 1)],
        )
        if step == 0:
            sums = extra.reshape(plane, -1)[:, : micro * ring * capacity]
            sums = sums.reshape(plane, micro, ring, capacity)
            values = [
                jnp.sum(jnp.where(chosen[m], sums[:, m, :, :, None], 0.0), 2) for m in range(micro)
            ]
            values = jnp.stack(values, 1).transpose(2, 1, 0, 3)
            extra = values.reshape(ring, -1, 128)
        waits = (result,)
        results.append(result)
        raw_grads.append(raw_grad)
        pair_grads.append(pair_grad)
        branches.append(branch)
        middle_grads.append(middle_grad)
        gain_list.append((norm_part[0], gain_part[0], gain_part[1]))
    if plane == 8:
        out_total, query_total, key_total, value_total, hidden_grad = grad_sums(
            ring, head_dim, attended, hidden_parts, branches, raw_grads, pair_grads, in_weight, 5
        )
    else:

        def sum_over_devices(left, right):
            share = left.shape[1] // experts
            left = left.reshape(-1, ring, plane, share).transpose(0, 2, 1, 3)
            term = t_dot(left.reshape(-1, experts * share), right).astype(jnp.bfloat16)
            term = lax.psum_scatter(term, "exp", scatter_dimension=0, tiled=True)
            return lax.psum_scatter(term, "ctx", scatter_dimension=0, tiled=True).astype(
                jnp.float32
            )

        out_total = sum_over_devices(jnp.concatenate(attended, 0), jnp.concatenate(branches, 0))
        raw_grad = jnp.concatenate(
            [jnp.concatenate(raw_grads, 0), jnp.concatenate(pair_grads, 0)], 1
        )
        in_total = sum_over_devices(hidden, raw_grad)
        hidden_grad = dot_t(raw_grad, in_weight)
        query_total = in_total[:, :query_width]
        pair_total = in_total[:, query_width:].reshape(-1, kv_heads, 2, head_dim)
        key_total = pair_total[:, :, 0].reshape(-1, pair_width)
        value_total = pair_total[:, :, 1].reshape(-1, pair_width)
    first_grad, first_gain = norm_back(rows, first_scale, norm_attn, hidden_grad)
    tokens_grad = jnp.concatenate(middle_grads, 0) + first_grad
    gains = jnp.concatenate([jnp.sum(first_gain, 0)] + [sum(parts) for parts in zip(*gain_list)])
    gain_total = jnp.sum(
        lax.all_to_all(
            gains.reshape(experts, -1), ("ctx", "exp"), split_axis=0, concat_axis=0, tiled=True
        ),
        0,
    )

    outputs = [
        (middles[step] + scatter(combine(results[step], step, True)).astype(jnp.float32)).astype(
            jnp.bfloat16
        )
        for step in range(micro)
    ]

    values = extra.reshape(ring, micro, plane, local).transpose(1, 3, 0, 2)
    values = values.reshape(micro, local, experts)
    match = routes[:, 0, :, :, None] == jnp.arange(experts, dtype=jnp.int32)
    route_grads = jnp.sum(jnp.where(match, values[:, :, None, :], 0.0), -1) / route_weights[:, 0]

    return (
        jnp.stack(outputs)[:, None],
        tokens_grad.reshape(micro, 1, local, width),
        route_grads[:, None],
        query_total,
        key_total,
        value_total,
        out_total,
        gain_total,
        gate_term,
        up_term,
        down_term,
    )


def solution(mesh):
    in_specs = (
        P(None, "exp", "ctx", None),
        P(None, "exp", "ctx", None),
        P(None, "exp", "ctx", None),
        P(None, "exp"),
        P(),
        P(),
        P(),
        P(),
        P("exp", None),
        P("exp", None),
        P("exp", None),
        P("exp", None),
        P(("ctx", "exp"), None, None),
        P(("ctx", "exp"), None, None),
        P(("ctx", "exp"), None, None),
        P(None, "exp", "ctx", None),
    )
    out_specs = (
        P(None, "exp", "ctx", None),
        P(None, "exp", "ctx", None),
        P(None, "exp", "ctx", None),
        P(("ctx", "exp"), None),
        P(("ctx", "exp"), None),
        P(("ctx", "exp"), None),
        P(("ctx", "exp"), None),
        P(("ctx", "exp")),
        P(("ctx", "exp"), None, None),
        P(("ctx", "exp"), None, None),
        P(("ctx", "exp"), None, None),
    )
    return jax.shard_map(
        per_device, mesh=mesh, in_specs=in_specs, out_specs=out_specs, check_vma=False
    )
```
